256 devices in a mesh: lon: 64 (over y_lo, x, z), lat: 4 (over y_hi, core).
Axes of the slice: x: 4, y: 4 (y_hi: 2, y_lo: 2; y = y_hi * 2 + y_lo), z: 8, core: 2. Of those that a mesh axis runs over, the one named last changes fastest.
Arguments:
- tokens: bfloat16 [4, 24, 768, 1024], P(None, 'lat', 'lon'), may hold values from -50 to 50
- w_qkv: bfloat16 [2, 1024, 1536], replicated, may hold values from -4 to 4
- w_out: bfloat16 [2, 512, 1024], replicated, may hold values from -0.25 to 0.25
Outputs:
- updated: bfloat16 [4, 24, 768, 1024], P(None, 'lat', 'lon')
The draws below stay inside these ranges and needn't reach their ends.
All inputs are finite; a program needn't handle non-finite values.
Results may differ from the reference program's by a relative error of at most 0.006.
Values may be sent and summed in bfloat16 or wider, within the bound.
No kernel may reach another device: no remote copies, remote signals or barrier semaphores. Data moves between devices by JAX's collectives and lax.ppermute only.
A program may use at most 64 MiB of HBM per device.

```python
import math
import jax
import jax.numpy as jnp
from jax import lax

D = 1024
HEADS = 8
HEAD = 64
LEV = 4
HD = 512
NLAT = 24
NLON = 768


def draw_tokens(key, part):
    key = jax.random.fold_in(key, 5)
    first_key = jax.random.fold_in(key, 0)
    shape = (LEV, NLAT, NLON, D)
    values = jnp.clip(jax.random.normal(first_key, shape, jnp.float32), -4.0, 4.0)
    return values.astype(jnp.bfloat16)


def draw_w_qkv(key, part):
    key = jax.random.fold_in(key, 9)
    base_key = jax.random.fold_in(key, 0)
    shape = (2, D, 3, HEADS, HEAD)
    values = jnp.clip(jax.random.normal(base_key, shape, jnp.float32), -4.0, 4.0) * (1.0 / math.sqrt(D))
    return values.reshape(2, D, 3 * HEADS * HEAD).astype(jnp.bfloat16)


def centred(rng, shape, scale, limit, dtype=jnp.bfloat16):
    drawn = jax.random.normal(rng, shape, jnp.float32) * scale
    return jnp.minimum(jnp.maximum(drawn, -limit), limit).astype(dtype)


def setup_inputs(seed: int = 0) -> dict:
    seeds = jax.random.split(jax.random.key(seed), 4)
    return {
        "tokens": draw_tokens(jax.random.fold_in(seeds[3], 71), 0),
        "w_qkv": draw_w_qkv(jax.random.fold_in(seeds[3], 71), 0),
        "w_out": centred(seeds[2], (2, HD, D), HD ** -0.5, 0.25),
    }


def layer_normed(values):
    centre = values - lax.optimization_barrier(jnp.mean(values, axis=-1, keepdims=True))
    spread = lax.optimization_barrier(jnp.mean(centre * centre, axis=-1, keepdims=True))
    return centre * lax.rsqrt(spread + 1e-05)

def level_label(count):
    index = jnp.arange(count)
    return jnp.where(index < count - 2, 0, jnp.where(index < count - 1, 1, 2)).astype(jnp.int32)

def row_label(index, total):
    return jnp.where(index < total - 6, 0, jnp.where(index < total - 3, 1, 2)).astype(jnp.int32)

def window_attend(windows, labels, weight_qkv, weight_out):
    batch, span, feature = windows.shape
    normed = layer_normed(windows.astype(jnp.float32)).astype(jnp.bfloat16)
    projected = jnp.dot(normed.reshape(batch * span, feature), weight_qkv, preferred_element_type=jnp.float32).astype(jnp.bfloat16)
    projected = projected.reshape(batch, span, 3, HEADS, HEAD).astype(jnp.float32)
    queries = projected[:, :, 0]
    keys_all = projected[:, :, 1]
    values_all = projected[:, :, 2]
    scores = jnp.einsum('bqhe,bkhe->bhqk', queries, keys_all) * (1.0 / math.sqrt(HEAD))
    allowed = labels[:, None, :, None] == labels[:, None, None, :]
    scores = jnp.where(allowed, scores, -1e+30)
    highest = lax.optimization_barrier(jnp.max(scores, axis=-1, keepdims=True))
    raised = jnp.exp(scores - highest)
    attn_weights = (raised / lax.optimization_barrier(jnp.sum(raised, axis=-1, keepdims=True))).astype(jnp.bfloat16)
    attended = jnp.einsum('bhqk,bkhe->bqhe', attn_weights.astype(jnp.float32), values_all).astype(jnp.bfloat16)
    attended = attended.reshape(batch * span, HEADS * HEAD)
    update = jnp.dot(attended, weight_out, preferred_element_type=jnp.float32).reshape(batch, span, feature)
    return (windows.astype(jnp.float32) + update).astype(jnp.bfloat16)

def swin_block(grid, labels, weight_qkv, weight_out):
    levels, lat_rows, lon_cols, feature = grid.shape
    pairs, bands, strips = (levels // 2, lat_rows // 6, lon_cols // 12)
    windows = grid.reshape(pairs, 2, bands, 6, strips, 12, feature).transpose(4, 0, 2, 1, 3, 5, 6)
    windows = windows.reshape(strips, pairs * bands, 144, feature)
    label_win = labels.reshape(pairs, 2, bands, 6).transpose(0, 2, 1, 3)
    label_win = jnp.broadcast_to(label_win[..., None], (pairs, bands, 2, 6, 12)).reshape(pairs * bands, 144)

    def one_strip(strip_windows):
        return window_attend(strip_windows, label_win, weight_qkv, weight_out)
    result = lax.map(one_strip, windows)
    result = result.reshape(strips, pairs, bands, 2, 6, 12, feature).transpose(1, 3, 2, 4, 0, 5, 6)
    return result.reshape(levels, lat_rows, lon_cols, feature)

def reference(tokens, w_qkv, w_out):
    plain = jnp.zeros((LEV, NLAT), jnp.int32)
    first = swin_block(tokens, plain, w_qkv[0], w_out[0])
    rolled = jnp.roll(first, (-1, -3, -6), axis=(0, 1, 2))
    labels = (3 * level_label(LEV)[:, None] + row_label(jnp.arange(NLAT), NLAT)[None, :]).astype(jnp.int32)
    second = swin_block(rolled, labels, w_qkv[1], w_out[1])
    return jnp.roll(second, (1, 3, 6), axis=(0, 1, 2))
```

```python
import functools

import jax
import jax.numpy as jnp
import numpy as np
from jax import lax
from jax.experimental import pallas as pl
from jax.experimental.pallas import tpu as pltpu
from jax.sharding import PartitionSpec as P

LEVELS, ROWS, COLS, D = 4, 6, 12, 1024
HD, HEAD = 512, 64
SLABS = LEVELS * ROWS
PAD = 16
PADDED = SLABS * PAD
OWN = SLABS * COLS
HALF = OWN // 2
QUART = HALF // 2
UNIT = 36
QWIN = 48
KWIN = 64
NEG = -1e30
GROUP_LEVELS = ((1, 2), (3, 0))


def wire_to_padded():
    index = np.zeros(OWN, np.int64)
    for w in range(OWN):
        c, rest = divmod(w, HALF)
        k, u = divmod(rest, UNIT)
        t, g = divmod(k, 2)
        lev, rest = divmod(u, 18)
        row, col = divmod(rest, 6)
        index[w] = (GROUP_LEVELS[g][lev] * ROWS + 3 * t + row) * PAD + 6 * c + col
    return index


def query_start(k):
    return k * UNIT // 16 * 16


def key_start(first, size):
    return min(first // 16 * 16, size - KWIN)


def gather_matrix():
    out = np.zeros((OWN, PADDED), np.float32)
    out[np.arange(OWN), wire_to_padded()] = 1
    return out


def scatter_matrix():
    out = np.zeros((PADDED, 8 * QWIN), np.float32)
    index = wire_to_padded()
    for w in range(OWN):
        c, rest = divmod(w, HALF)
        k, u = divmod(rest, UNIT)
        out[index[w], (4 * c + k) * QWIN + UNIT * k - query_start(k) + u] = 1
    return out


def layer_normed(values):
    centre = values - jnp.mean(values, axis=-1, keepdims=True)
    spread = jnp.mean(centre * centre, axis=-1, keepdims=True)
    return (centre * lax.rsqrt(spread + 1e-05)).astype(jnp.bfloat16)


def dot(a, b):
    return jnp.dot(a, b, preferred_element_type=jnp.float32)


def four_heads(queries, keys, values, bias):
    rows = queries.shape[0]
    head_of = lax.broadcasted_iota(jnp.int32, (1, 4 * HEAD), 1) // HEAD
    queries = queries * jnp.bfloat16(0.125)
    spread = jnp.concatenate(
        [jnp.where(head_of == h, queries, jnp.bfloat16(0)) for h in range(4)], axis=0
    )
    scores = lax.dot_general(
        spread, keys, (((1,), (1,)), ((), ())), preferred_element_type=jnp.float32
    )
    scores = scores + bias
    highest = jnp.max(scores, axis=-1, keepdims=True)
    raised = jnp.exp(scores - highest)
    total = jnp.sum(raised, axis=-1, keepdims=True)
    mixed = dot(raised.astype(jnp.bfloat16), values) * (1.0 / total)
    out = mixed[:rows]
    for h in range(1, 4):
        out = jnp.where(head_of == h, mixed[h * rows : (h + 1) * rows], out)
    return out.astype(jnp.bfloat16)


def first_kernel(
    x_hbm, w_qkv_hbm, w_out_hbm, gather_hbm, q_out, left_out, right_out, first_out,
    x_in, x_pad, normed, qkv, att, w0, wo, w1, gather, sems,
):
    copies = [pltpu.make_async_copy(x_hbm, x_in, sems.at[0])]
    for i in range(3):
        cols = pl.ds(i * HD, HD)
        copies.append(pltpu.make_async_copy(w_qkv_hbm.at[0, :, cols], w0.at[i], sems.at[1 + i]))
    copies.append(pltpu.make_async_copy(w_out_hbm.at[0], wo, sems.at[4]))
    copies.append(pltpu.make_async_copy(gather_hbm, gather, sems.at[5]))
    for i in range(3):
        cols = pl.ds(i * HD, HD)
        copies.append(pltpu.make_async_copy(w_qkv_hbm.at[1, :, cols], w1.at[i], sems.at[6 + i]))
    for copy in copies:
        copy.start()

    x_pad[...] = jnp.zeros_like(x_pad)
    copies[0].wait()
    for slab in range(SLABS):
        x_pad[slab * PAD : slab * PAD + COLS, :] = x_in[slab // ROWS, slab % ROWS]
    chunk = 48
    for i in range(PADDED // chunk):
        rows = slice(i * chunk, (i + 1) * chunk)
        normed[rows, :] = layer_normed(x_pad[rows, :].astype(jnp.float32))
    for i in range(3):
        copies[1 + i].wait()
        qkv[:, i * HD : (i + 1) * HD] = dot(normed[...], w0[i]).astype(jnp.bfloat16)

    span = PADDED // 2
    lane = lax.broadcasted_iota(jnp.int32, (1, span), 1)
    bias = jnp.where(lane % PAD < COLS, 0.0, NEG).astype(jnp.float32)
    for window in range(2):
        rows = slice(window * span, (window + 1) * span)
        for half in range(2):
            cols = [slice(i * HD + half * 256, i * HD + half * 256 + 256) for i in range(3)]
            att[rows, cols[0]] = four_heads(
                qkv[rows, cols[0]], qkv[rows, cols[1]], qkv[rows, cols[2]], bias
            )

    copies[4].wait()
    for i in range(PADDED // chunk):
        rows = slice(i * chunk, (i + 1) * chunk)
        update = dot(att[rows, :], wo[...])
        first = (x_pad[rows, :].astype(jnp.float32) + update).astype(jnp.bfloat16)
        first_out[rows, :] = first
        normed[rows, :] = layer_normed(first.astype(jnp.float32))

    copies[5].wait()
    wire = dot(gather[...], normed[...]).astype(jnp.bfloat16)
    for i in range(3):
        copies[6 + i].wait()
        part = dot(wire, w1[i]).astype(jnp.bfloat16)
        if i == 0:
            q_out[...] = part
        else:
            cols = slice((i - 1) * HD, i * HD)
            left_out[:, cols] = part[:HALF]
            right_out[:, cols] = part[HALF:]


def second_kernel(
    lat, q, left, right, from_left, from_right, even, odd, first, w_out_hbm, scatter_hbm, out,
    att, wo, scatter, sems,
):
    copies = [
        pltpu.make_async_copy(scatter_hbm, scatter, sems.at[0]),
        pltpu.make_async_copy(w_out_hbm.at[1], wo, sems.at[1]),
    ]
    for copy in copies:
        copy.start()
    position = lat[0]
    is_odd = position % 2 == 1
    row = lax.broadcasted_iota(jnp.int32, (QWIN, 4 * KWIN), 0)
    lane = lax.broadcasted_iota(jnp.int32, (QWIN, 4 * KWIN), 1)
    own = ((left, from_left), (right, from_right))
    for c in range(2):
        for t in range(2):
            edge = position == (0 if t == 0 else 3)
            for g in range(2):
                k = 2 * t + g
                start = query_start(k)
                firsts = [UNIT * k, UNIT * k, QUART * c + UNIT * g, QUART * (2 + c) + UNIT * g]
                starts = [key_start(firsts[i], HALF if i < 2 else OWN) for i in range(4)]
                wanted = row - (UNIT * k - start)
                valid = jnp.zeros((QWIN, 4 * KWIN), jnp.bool_)
                for i in range(4):
                    at = lane - (i * KWIN + firsts[i] - starts[i])
                    inside = (at >= 0) & (at < UNIT)
                    if g == 1:
                        inside = inside & ((at >= 18) == (wanted >= 18))
                    if i >= 2:
                        inside = inside & jnp.logical_not(edge)
                    valid = valid | inside
                bias = jnp.where(valid, 0.0, NEG).astype(jnp.float32)
                bias = jnp.concatenate([bias] * 4, axis=0)
                for half in range(2):
                    cols = slice(half * 256, half * 256 + 256)

                    def window(base):
                        lanes = slice(base + half * 256, base + half * 256 + 256)
                        parts = [own[c][i][starts[i] : starts[i] + KWIN, lanes] for i in range(2)]
                        for i in (2, 3):
                            span = slice(starts[i], starts[i] + KWIN)
                            a, b = even[span, lanes], odd[span, lanes]
                            first_is_even = is_odd if t == 0 else jnp.logical_not(is_odd)
                            parts.append(jnp.where(first_is_even, a, b))
                        return jnp.concatenate(parts, axis=0)

                    n = 4 * c + k
                    att[n * QWIN : (n + 1) * QWIN, cols] = four_heads(
                        q[c * HALF + start : c * HALF + start + QWIN, cols], window(0), window(HD), bias
                    )
    copies[0].wait()
    copies[1].wait()
    placed = dot(scatter[...], att[...]).astype(jnp.bfloat16)
    for level in range(LEVELS):
        rows = slice(level * ROWS * PAD, (level + 1) * ROWS * PAD)
        done = (first[rows, :].astype(jnp.float32) + dot(placed[rows], wo[...])).astype(jnp.bfloat16)
        for r in range(ROWS):
            out[level, r] = done[r * PAD : r * PAD + COLS]


def shape(*dims):
    return jax.ShapeDtypeStruct(dims, jnp.bfloat16)


def vmem(*dims):
    return pltpu.VMEM(dims, jnp.bfloat16)


ANY = pl.BlockSpec(memory_space=pl.ANY)
WHOLE = pl.BlockSpec(memory_space=pltpu.VMEM)


def first_block(tokens, w_qkv, w_out):
    return pl.pallas_call(
        first_kernel,
        out_shape=(shape(OWN, HD), shape(HALF, D), shape(HALF, D), shape(PADDED, D)),
        in_specs=[ANY] * 4,
        out_specs=(WHOLE,) * 4,
        scratch_shapes=[
            vmem(LEVELS, ROWS, COLS, D),
            vmem(PADDED, D),
            vmem(PADDED, D),
            vmem(PADDED, 3 * HD),
            vmem(PADDED, HD),
            vmem(3, D, HD),
            vmem(HD, D),
            vmem(3, D, HD),
            vmem(OWN, PADDED),
            pltpu.SemaphoreType.DMA((9,)),
        ],
        compiler_params=pltpu.CompilerParams(vmem_limit_bytes=40 * 1024 * 1024),
        name="first_block",
    )(tokens, w_qkv, w_out, jnp.asarray(gather_matrix(), jnp.bfloat16))


def second_block(lat, q, left, right, from_left, from_right, even, odd, first, w_out):
    return pl.pallas_call(
        second_kernel,
        out_shape=shape(LEVELS, ROWS, COLS, D),
        in_specs=[pl.BlockSpec(memory_space=pltpu.SMEM)] + [WHOLE] * 8 + [ANY] * 2,
        out_specs=WHOLE,
        scratch_shapes=[
            vmem(8 * QWIN, HD),
            vmem(HD, D),
            vmem(PADDED, 8 * QWIN),
            pltpu.SemaphoreType.DMA((2,)),
        ],
        compiler_params=pltpu.CompilerParams(vmem_limit_bytes=32 * 1024 * 1024),
        name="second_block",
    )(lat, q, left, right, from_left, from_right, even, odd, first, w_out,
      jnp.asarray(scatter_matrix(), jnp.bfloat16))


def per_device(tokens, w_qkv, w_out):
    lons, lats = lax.axis_size("lon"), lax.axis_size("lat")
    q, left, right, first = first_block(tokens, w_qkv, w_out)
    from_left = lax.ppermute(right, "lon", [(i, (i + 1) % lons) for i in range(lons)])
    from_right = lax.ppermute(left, "lon", [(i, (i - 1) % lons) for i in range(lons)])
    parts = [left, right, from_left, from_right]
    top = jnp.concatenate([p[:QUART] for p in parts], axis=0)
    bottom = jnp.concatenate([p[QUART:] for p in parts], axis=0)
    lat = lax.axis_index("lat")
    is_even = lat % 2 == 0
    even = lax.ppermute(jnp.where(is_even, bottom, top), "lat", [(i, i ^ 1) for i in range(lats)])
    odd = lax.ppermute(
        jnp.where(is_even, top, bottom),
        "lat",
        [(i, i - 1 if i % 2 == 0 else i + 1) for i in range(1, lats - 1)],
    )
    return second_block(
        lat.astype(jnp.int32)[None], q, left, right, from_left, from_right, even, odd, first, w_out
    )


def solution(mesh):
    return jax.shard_map(
        per_device,
        mesh=mesh,
        in_specs=(P(None, "lat", "lon", None), P(), P()),
        out_specs=P(None, "lat", "lon", None),
        check_vma=False,
    )
```

```python
import jax
import jax.numpy as jnp
from jax import lax
from jax.experimental import pallas as pl
from jax.experimental.pallas import tpu as pltpu
from jax.sharding import PartitionSpec as P

LEVELS, ROWS, COLS, D = 4, 6, 12, 1024
HD, HEAD = 512, 64
CELLS = ROWS * COLS
OWN = LEVELS * CELLS
HALF = OWN // 2
QUART = HALF // 2
UNIT = 36
QWIN = 48
KWIN = 64
NEG = -1e30
GROUP_LEVELS = ((1, 2), (3, 0))


def at_least(index, *bounds):
    return sum(jnp.where(index >= bound, 1, 0) for bound in bounds)


def cell_of_window(index):
    pair = at_least(index, HALF)
    index = index - HALF * pair
    return (index >> 1) * LEVELS + 2 * pair + (index & 1)


def cell_of_wire(index):
    c = at_least(index, HALF)
    index = index - HALF * c
    k = at_least(index, UNIT, 2 * UNIT, 3 * UNIT)
    return cell_of_unit(c, k, index - UNIT * k)


def cell_of_unit(c, k, index):
    lev = at_least(index, UNIT // 2)
    index = index - UNIT // 2 * lev
    row = at_least(index, 6, 12)
    level = jnp.where((k & 1) == 0, 1 + lev, 3 - 3 * lev)
    return ((3 * (k >> 1) + row) * COLS + 6 * c + index - 6 * row) * LEVELS + level


def query_start(k):
    return k * UNIT // 16 * 16


def key_start(first, size):
    return min(first // 16 * 16, size - KWIN)


def iota(shape, axis):
    return lax.broadcasted_iota(jnp.int32, shape, axis)


def one_hot(rows, lanes):
    return jnp.where(rows == lanes, 1.0, 0.0).astype(jnp.bfloat16)


def scatter_matrix():
    lane = iota((1, 8 * QWIN), 1)
    n = at_least(lane, *(QWIN * i for i in range(1, 8)))
    k = n & 3
    index = lane - QWIN * n - 4 * k
    cell = jnp.where((index >= 0) & (index < UNIT), cell_of_unit(n >> 2, k, index), -1)
    return one_hot(iota((OWN, 8 * QWIN), 0), cell)


def layer_normed(values):
    centre = values - jnp.mean(values, axis=-1, keepdims=True)
    spread = jnp.mean(centre * centre, axis=-1, keepdims=True)
    return (centre * lax.rsqrt(spread + 1e-05)).astype(jnp.bfloat16)


def dot(a, b):
    return jnp.dot(a, b, preferred_element_type=jnp.float32)


def four_heads(queries, keys, values, bias):
    rows = queries.shape[0]
    head_of = iota((1, 4 * HEAD), 1) // HEAD
    queries = queries * jnp.bfloat16(0.125)
    spread = jnp.concatenate(
        [jnp.where(head_of == h, queries, jnp.bfloat16(0)) for h in range(4)], axis=0
    )
    scores = lax.dot_general(
        spread, keys, (((1,), (1,)), ((), ())), preferred_element_type=jnp.float32
    )
    if bias is not None:
        scores = scores + bias
    highest = jnp.max(scores, axis=-1, keepdims=True)
    raised = jnp.exp(scores - highest)
    total = jnp.sum(raised, axis=-1, keepdims=True)
    mixed = dot(raised.astype(jnp.bfloat16), values) * (1.0 / total)
    out = mixed[:rows]
    for h in range(1, 4):
        out = jnp.where(head_of == h, mixed[h * rows : (h + 1) * rows], out)
    return out.astype(jnp.bfloat16)


def first_kernel(
    x_hbm, w_qkv_hbm, w_out_hbm, q_out, left_out, right_out, first_out,
    x_in, x, normed, qkv, att, w0, wo, w1, sems,
):
    copies = [pltpu.make_async_copy(x_hbm, x_in, sems.at[0])]
    for i in range(3):
        cols = pl.ds(i * HD, HD)
        copies.append(pltpu.make_async_copy(w_qkv_hbm.at[0, :, cols], w0.at[i], sems.at[1 + i]))
    copies.append(pltpu.make_async_copy(w_out_hbm.at[0], wo, sems.at[4]))
    for i in range(3):
        cols = pl.ds(i * HD, HD)
        copies.append(pltpu.make_async_copy(w_qkv_hbm.at[1, :, cols], w1.at[i], sems.at[5 + i]))
    for copy in copies:
        copy.start()
    square = (OWN, OWN)
    to_window = one_hot(cell_of_window(iota((OWN, 1), 0)), iota(square, 1))
    from_window = one_hot(iota(square, 0), cell_of_window(iota((1, OWN), 1)))
    to_wire = one_hot(cell_of_wire(iota((OWN, 1), 0)), iota(square, 1))

    copies[0].wait()
    for i in range(CELLS):
        x[i * LEVELS : (i + 1) * LEVELS, :] = x_in[i].astype(jnp.float32)
    chunk = 48
    for i in range(OWN // chunk):
        rows = slice(i * chunk, (i + 1) * chunk)
        normed[rows, :] = layer_normed(x[rows, :])
    ordered = dot(to_window, normed[...]).astype(jnp.bfloat16)
    for i in range(3):
        copies[1 + i].wait()
        qkv[:, i * HD : (i + 1) * HD] = dot(ordered, w0[i]).astype(jnp.bfloat16)

    for window in range(2):
        rows = slice(window * HALF, (window + 1) * HALF)
        for half in range(2):
            cols = [slice(i * HD + half * 256, i * HD + half * 256 + 256) for i in range(3)]
            att[rows, cols[0]] = four_heads(
                qkv[rows, cols[0]], qkv[rows, cols[1]], qkv[rows, cols[2]], None
            )

    back = dot(from_window, att[...]).astype(jnp.bfloat16)
    copies[4].wait()
    for i in range(OWN // chunk):
        rows = slice(i * chunk, (i + 1) * chunk)
        first = (x[rows, :] + dot(back[rows], wo[...])).astype(jnp.bfloat16)
        first_out[rows, :] = first
        normed[rows, :] = layer_normed(first.astype(jnp.float32))

    wire = dot(to_wire, normed[...]).astype(jnp.bfloat16)
    for i in range(3):
        copies[5 + i].wait()
        part = dot(wire, w1[i]).astype(jnp.bfloat16)
        if i == 0:
            q_out[...] = part
        else:
            cols = slice((i - 1) * HD, i * HD)
            left_out[:, cols] = part[:HALF]
            right_out[:, cols] = part[HALF:]


def second_kernel(
    where, q, left, right, lon_even, lon_odd, lat_even, lat_odd, first, w_out_hbm, out,
    att, done, wo, sem,
):
    copy = pltpu.make_async_copy(w_out_hbm.at[1], wo, sem)
    copy.start()
    scatter = scatter_matrix()
    position = where[1]
    lon_is_even = where[0] % 2 == 0
    lat_is_even = position % 2 == 0
    row = iota((QWIN, 4 * KWIN), 0)
    lane = iota((QWIN, 4 * KWIN), 1)
    for c in range(2):
        for t in range(2):
            edge = position == (0 if t == 0 else 3)
            for g in range(2):
                k = 2 * t + g
                start = query_start(k)
                firsts = [UNIT * k, UNIT * k, QUART * c + UNIT * g, QUART * (2 + c) + UNIT * g]
                starts = [key_start(firsts[i], HALF if i < 2 else OWN) for i in range(4)]
                wanted = row - (UNIT * k - start)
                valid = jnp.zeros((QWIN, 4 * KWIN), jnp.bool_)
                for i in range(4):
                    at = lane - (i * KWIN + firsts[i] - starts[i])
                    inside = (at >= 0) & (at < UNIT)
                    if g == 1:
                        inside = inside & ((at >= 18) == (wanted >= 18))
                    if i >= 2:
                        inside = inside & jnp.logical_not(edge)
                    valid = valid | inside
                bias = jnp.where(valid, 0.0, NEG).astype(jnp.float32)
                bias = jnp.concatenate([bias] * 4, axis=0)
                for half in range(2):
                    cols = slice(half * 256, half * 256 + 256)

                    def window(base):
                        lanes = slice(base + half * 256, base + half * 256 + 256)
                        spans = [slice(start, start + KWIN) for start in starts]
                        parts = [(left, right)[c][spans[0], lanes]]
                        across = lon_is_even == (c == 1)
                        parts.append(jnp.where(across, lon_even[spans[1], lanes], lon_odd[spans[1], lanes]))
                        across = lat_is_even == (t == 1)
                        for i in (2, 3):
                            parts.append(jnp.where(across, lat_even[spans[i], lanes], lat_odd[spans[i], lanes]))
                        return jnp.concatenate(parts, axis=0)

                    n = 4 * c + k
                    att[n * QWIN : (n + 1) * QWIN, cols] = four_heads(
                        q[c * HALF + start : c * HALF + start + QWIN, cols], window(0), window(HD), bias
                    )
    copy.wait()
    placed = dot(scatter, att[...]).astype(jnp.bfloat16)
    done[...] = first[...].astype(jnp.float32) + dot(placed, wo[...])
    for i in range(CELLS):
        out[i] = done[i * LEVELS : (i + 1) * LEVELS, :].astype(jnp.bfloat16)


def shape(*dims):
    return jax.ShapeDtypeStruct(dims, jnp.bfloat16)


def vmem(*dims):
    return pltpu.VMEM(dims, jnp.bfloat16)


def in_hbm(array):
    return pltpu.with_memory_space_constraint(array, pltpu.HBM)


ANY = pl.BlockSpec(memory_space=pl.ANY)
WHOLE = pl.BlockSpec(memory_space=pltpu.VMEM)


def first_block(cells, w_qkv, w_out):
    return pl.pallas_call(
        first_kernel,
        out_shape=(shape(OWN, HD), shape(HALF, D), shape(HALF, D), shape(OWN, D)),
        in_specs=[ANY] * 3,
        out_specs=(WHOLE,) * 4,
        scratch_shapes=[
            vmem(CELLS, LEVELS, D),
            pltpu.VMEM((OWN, D), jnp.float32),
            vmem(OWN, D),
            vmem(OWN, 3 * HD),
            vmem(OWN, HD),
            vmem(3, D, HD),
            vmem(HD, D),
            vmem(3, D, HD),
            pltpu.SemaphoreType.DMA((8,)),
        ],
        compiler_params=pltpu.CompilerParams(vmem_limit_bytes=40 * 1024 * 1024),
        name="first_block",
    )(in_hbm(cells), in_hbm(w_qkv), in_hbm(w_out))


def second_block(lat, q, left, right, lon_even, lon_odd, lat_even, lat_odd, first, w_out):
    return pl.pallas_call(
        second_kernel,
        out_shape=shape(CELLS, LEVELS, D),
        in_specs=[pl.BlockSpec(memory_space=pltpu.SMEM)] + [WHOLE] * 8 + [ANY],
        out_specs=WHOLE,
        scratch_shapes=[
            vmem(8 * QWIN, HD),
            pltpu.VMEM((OWN, D), jnp.float32),
            vmem(HD, D),
            pltpu.SemaphoreType.DMA,
        ],
        compiler_params=pltpu.CompilerParams(vmem_limit_bytes=32 * 1024 * 1024),
        name="second_block",
    )(lat, q, left, right, lon_even, lon_odd, lat_even, lat_odd, first, in_hbm(w_out))


def odd_pairs(size):
    return [(i, (i - 1 if i % 2 == 0 else i + 1) % size) for i in range(size)]


def per_device(tokens, w_qkv, w_out):
    lons, lats = lax.axis_size("lon"), lax.axis_size("lat")
    lon, lat = lax.axis_index("lon"), lax.axis_index("lat")
    cells = tokens.transpose(1, 2, 0, 3).reshape(CELLS, LEVELS, D)
    q, left, right, first = first_block(cells, w_qkv, w_out)
    lon_is_even, lat_is_even = lon % 2 == 0, lat % 2 == 0
    lon_odd = lax.ppermute(jnp.where(lon_is_even, left, right), "lon", odd_pairs(lons))
    lon_even = lax.ppermute(
        jnp.where(lon_is_even, right, left), "lon", [(i, i ^ 1) for i in range(lons)]
    )
    parts = [left, right, jnp.where(lon_is_even, lon_odd, lon_even), jnp.where(lon_is_even, lon_even, lon_odd)]
    top = jnp.concatenate([p[:QUART] for p in parts], axis=0)
    bottom = jnp.concatenate([p[QUART:] for p in parts], axis=0)
    lat_odd = lax.ppermute(
        jnp.where(lat_is_even, top, bottom), "lat", odd_pairs(lats)[1 : lats - 1]
    )
    lat_even = lax.ppermute(
        jnp.where(lat_is_even, bottom, top), "lat", [(i, i ^ 1) for i in range(lats)]
    )
    where = jnp.stack([lon, lat]).astype(jnp.int32)
    out = second_block(where, q, left, right, lon_even, lon_odd, lat_even, lat_odd, first, w_out)
    return out.reshape(ROWS, COLS, LEVELS, D).transpose(2, 0, 1, 3)


def solution(mesh):
    return jax.shard_map(
        per_device,
        mesh=mesh,
        in_specs=(P(None, "lat", "lon", None), P(), P()),
        out_specs=P(None, "lat", "lon", None),
        check_vma=False,
    )
```

```python
import jax
import jax.numpy as jnp
from jax import lax
from jax.experimental import pallas as pl
from jax.experimental.pallas import tpu as pltpu
from jax.sharding import PartitionSpec as P

LEVELS, ROWS, COLS, D = 4, 6, 12, 1024
HD, HEAD = 512, 64
CELLS = ROWS * COLS
OWN = LEVELS * CELLS
HALF = OWN // 2
QUART = HALF // 2
UNIT = 36
WIN = 80
SIDE = 2 * WIN
QWIN = 48
KWIN = 64
NEG = -1e30


def at_least(index, *bounds):
    return sum(jnp.where(index >= bound, 1, 0) for bound in bounds)


def cell_of_window(index, lon_odd):
    side = at_least(index, SIDE)
    index = index - SIDE * side
    pair = at_least(index, WIN)
    index = index - WIN * pair
    valid = index < 2 * UNIT
    level = at_least(index, UNIT)
    index = index - UNIT * level
    row = at_least(index, *range(6, UNIT, 6))
    cell = (row * COLS + 6 * (side ^ lon_odd) + index - 6 * row) * LEVELS + 2 * pair + level
    return jnp.where(valid, cell, -1)


def split_unit(index, group):
    lev = at_least(index, UNIT // 2)
    index = index - UNIT // 2 * lev
    row = at_least(index, 6, 12)
    return jnp.where(group == 0, 1 + lev, 3 - 3 * lev), row, index - 6 * row


def window_of_wire(index, lat_odd):
    k = at_least(index, UNIT, 2 * UNIT, 3 * UNIT)
    level, row, col = split_unit(index - UNIT * k, k & 1)
    row = row + 3 * ((k >> 1) ^ lat_odd)
    return WIN * (level >> 1) + UNIT * (level & 1) + 6 * row + col


def cell_of_queries(index, lat_side, lon_odd):
    n = at_least(index, QWIN, 2 * QWIN, 3 * QWIN)
    group, side = n & 1, n >> 1
    index = index - QWIN * n - 4 * (2 * lat_side + group)
    level, row, col = split_unit(index, group)
    cell = (row * COLS + 6 * (side ^ lon_odd) + col) * LEVELS + level
    return jnp.where((index >= 0) & (index < UNIT), cell, -1)


def query_start(k):
    return k * UNIT // 16 * 16


def key_start(first, size):
    return min(first // 16 * 16, size - KWIN)


def iota(shape, axis):
    return lax.broadcasted_iota(jnp.int32, shape, axis)


def one_hot(rows, lanes):
    return jnp.where(rows == lanes, 1.0, 0.0).astype(jnp.bfloat16)


def layer_normed(values):
    centre = values - jnp.mean(values, axis=-1, keepdims=True)
    spread = jnp.mean(centre * centre, axis=-1, keepdims=True)
    return (centre * lax.rsqrt(spread + 1e-05)).astype(jnp.bfloat16)


def dot(a, b):
    return jnp.dot(a, b, preferred_element_type=jnp.float32)


def four_heads(queries, keys, values, bias):
    rows = queries.shape[0]
    head_of = iota((1, 4 * HEAD), 1) // HEAD
    queries = queries * jnp.bfloat16(0.125)
    spread = jnp.concatenate(
        [jnp.where(head_of == h, queries, jnp.bfloat16(0)) for h in range(4)], axis=0
    )
    scores = lax.dot_general(
        spread, keys, (((1,), (1,)), ((), ())), preferred_element_type=jnp.float32
    )
    scores = scores + bias
    highest = jnp.max(scores, axis=-1, keepdims=True)
    raised = jnp.exp(scores - highest)
    total = jnp.sum(raised, axis=-1, keepdims=True)
    mixed = dot(raised.astype(jnp.bfloat16), values) * (1.0 / total)
    out = mixed[:rows]
    for h in range(1, 4):
        out = jnp.where(head_of == h, mixed[h * rows : (h + 1) * rows], out)
    return out.astype(jnp.bfloat16)


def side_block(lat_odd, x, normed, kv, w_q, w_out, w_kv, first_out, wire_out, kv_out, att, scratch, ready):
    ready(0)
    queries = dot(normed, w_q[...]).astype(jnp.bfloat16)
    bias = jnp.where(iota((1, 2 * WIN), 1) % WIN < 2 * UNIT, 0.0, NEG).astype(jnp.float32)
    for pair in range(2):
        rows = slice(pair * WIN, (pair + 1) * WIN)
        far = slice(SIDE + pair * WIN, SIDE + (pair + 1) * WIN)
        for half in range(2):
            cols = slice(half * 256, half * 256 + 256)
            cols_v = slice(HD + half * 256, HD + half * 256 + 256)
            att[rows, cols] = four_heads(
                queries[rows, cols],
                jnp.concatenate([kv[rows, cols], kv[far, cols]], axis=0),
                jnp.concatenate([kv[rows, cols_v], kv[far, cols_v]], axis=0),
                bias,
            )
    to_wire = one_hot(window_of_wire(iota((HALF, 1), 0), lat_odd), iota((HALF, SIDE), 1))
    ready(1)
    for pair in range(2):
        rows = slice(pair * WIN, (pair + 1) * WIN)
        first = (x[rows, :].astype(jnp.float32) + dot(att[rows, :], w_out[...])).astype(jnp.bfloat16)
        first_out[rows, :] = first
        scratch[rows, :] = layer_normed(first.astype(jnp.float32))
    wire = dot(to_wire, scratch[...]).astype(jnp.bfloat16)
    wire_out[...] = wire
    for i in range(2):
        ready(2 + i)
        kv_out[:, i * HD : (i + 1) * HD] = dot(wire, w_kv[i]).astype(jnp.bfloat16)


def odd_kernel(
    where, x_hbm, w_qkv_hbm, w_out_hbm,
    kv_out, wire_out, first_out, kv0, x_even, normed_even, w_q, w_out, w_kv,
    x_in, x, x_odd, normed, att, scratch, w_kv0, sems,
):
    def part(block, i):
        return w_qkv_hbm.at[block, :, pl.ds(i * HD, HD)]

    pairs = [
        (x_hbm, x_in), (part(0, 1), w_kv0.at[0]), (part(0, 2), w_kv0.at[1]), (part(0, 0), w_q),
        (w_out_hbm.at[0], w_out), (part(1, 1), w_kv.at[0]), (part(1, 2), w_kv.at[1]),
    ]
    copies = [pltpu.make_async_copy(src, dst, sems.at[i]) for i, (src, dst) in enumerate(pairs)]
    for copy in copies:
        copy.start()
    lon_odd, lat_odd = where[0] & 1, where[1] & 1
    rows = 2 * SIDE
    to_window = one_hot(cell_of_window(iota((rows, 1), 0), lon_odd), iota((rows, OWN), 1))
    copies[0].wait()
    for i in range(CELLS):
        x[i * LEVELS : (i + 1) * LEVELS, :] = x_in[i].astype(jnp.float32)
    cells = x[...].astype(jnp.bfloat16)
    for i in range(4):
        span = slice(i * WIN, (i + 1) * WIN)
        ordered = dot(to_window[span], cells)
        target = x_odd if i < 2 else x_even
        target[(i % 2) * WIN : (i % 2 + 1) * WIN, :] = ordered.astype(jnp.bfloat16)
        normed[span, :] = layer_normed(ordered)
    normed_even[...] = normed[SIDE:, :]
    for i in range(2):
        copies[1 + i].wait()
        kv0[:, i * HD : (i + 1) * HD] = dot(normed[...], w_kv0[i]).astype(jnp.bfloat16)
    side_block(
        lat_odd, x_odd, normed[:SIDE, :], kv0, w_q, w_out, w_kv, first_out, wire_out, kv_out, att, scratch,
        lambda i: copies[3 + i].wait(),
    )


def even_kernel(
    where, x, normed, kv0, w_q, w_out, w_kv, kv_out, wire_out, first_out, att, scratch
):
    side_block(
        where[1] & 1, x, normed[...], kv0, w_q, w_out, w_kv, first_out, wire_out, kv_out, att, scratch,
        lambda i: None,
    )


def query_kernel(
    where, wire_odd, wire_even, first_odd, first_even, w_qkv_hbm, q_out, first_out, w_q, sem
):
    copy = pltpu.make_async_copy(w_qkv_hbm.at[1, :, pl.ds(0, HD)], w_q, sem)
    copy.start()
    lane = cell_of_window(iota((1, 2 * SIDE), 1), where[0] & 1)
    to_cell = one_hot(iota((OWN, 2 * SIDE), 0), lane)
    first = jnp.concatenate([first_odd[...], first_even[...]], axis=0)
    first_out[...] = dot(to_cell, first).astype(jnp.bfloat16)
    copy.wait()
    q_out[:HALF, :] = dot(wire_odd[...], w_q[...]).astype(jnp.bfloat16)
    q_out[HALF:, :] = dot(wire_even[...], w_q[...]).astype(jnp.bfloat16)


def lat_side_block(lat_side, where, q, kv_odd, kv_even, lon_odd, lon_even, lat, first, w_out, att, done):
    position = where[1]
    edge = (position == 0) | (position == 3)
    row = iota((QWIN, 4 * KWIN), 0)
    lane = iota((QWIN, 4 * KWIN), 1)
    for side in range(2):
        own, across = ((kv_odd, lon_odd), (kv_even, lon_even))[side]
        for g in range(2):
            k = 2 * lat_side + g
            start = query_start(k)
            firsts = [UNIT * k, UNIT * k, QUART * side + UNIT * g, QUART * (2 + side) + UNIT * g]
            sources = [own, across, lat, lat]
            starts = [key_start(f, s.shape[0]) for f, s in zip(firsts, sources)]
            late = row >= UNIT * k - start + UNIT // 2
            valid = jnp.zeros((QWIN, 4 * KWIN), jnp.bool_)
            for i in range(4):
                at = lane - (i * KWIN + firsts[i] - starts[i])
                inside = (at >= 0) & (at < UNIT)
                if g == 1:
                    inside = inside & ((at >= UNIT // 2) == late)
                if i >= 2 and lat_side == 0:
                    inside = inside & jnp.logical_not(edge)
                valid = valid | inside
            bias = jnp.where(valid, 0.0, NEG).astype(jnp.float32)
            bias = jnp.concatenate([bias] * 4, axis=0)
            n = 2 * side + g
            for half in range(2):
                cols = slice(half * 256, half * 256 + 256)

                def window(base):
                    lanes = slice(base + half * 256, base + half * 256 + 256)
                    parts = [s[f : f + KWIN, lanes] for s, f in zip(sources, starts)]
                    return jnp.concatenate(parts, axis=0)

                att[n * QWIN : (n + 1) * QWIN, cols] = four_heads(
                    q[side * HALF + start : side * HALF + start + QWIN, cols], window(0), window(HD), bias
                )
    lane = cell_of_queries(iota((1, 4 * QWIN), 1), lat_side, where[0] & 1)
    placed = dot(one_hot(iota((HALF, 4 * QWIN), 0), lane), att[...]).astype(jnp.bfloat16)
    rows = pl.ds(pl.multiple_of(HALF * ((position & 1) ^ lat_side), 16), HALF)
    done[...] = first[rows, :].astype(jnp.float32) + dot(placed, w_out[1])


def near_kernel(
    where, q, kv_odd, kv_even, lon_odd, lon_even, lat, first, w_out, out, att, done
):
    lat_side_block(1, where, q, kv_odd, kv_even, lon_odd, lon_even, lat, first, w_out, att, done)
    for i in range(CELLS // 2):
        out[i] = done[i * LEVELS : (i + 1) * LEVELS, :].astype(jnp.bfloat16)


def far_kernel(
    where, q, kv_odd, kv_even, lon_odd, lon_even, lat, first, w_out, near, out, att, done, staged, sems
):
    top = (where[1] & 1) * (CELLS // 2)
    copy = pltpu.make_async_copy(near, out.at[pl.ds(CELLS // 2 - top, CELLS // 2)], sems.at[0])
    copy.start()
    lat_side_block(0, where, q, kv_odd, kv_even, lon_odd, lon_even, lat, first, w_out, att, done)
    copies = [copy]
    step = CELLS // 6
    for j in range(3):
        for i in range(j * step, (j + 1) * step):
            staged[i] = done[i * LEVELS : (i + 1) * LEVELS, :].astype(jnp.bfloat16)
        span = pl.ds(top + j * step, step)
        copies.append(
            pltpu.make_async_copy(staged.at[pl.ds(j * step, step)], out.at[span], sems.at[1 + j])
        )
        copies[-1].start()
    for copy in copies:
        copy.wait()


def shape(*dims):
    return jax.ShapeDtypeStruct(dims, jnp.bfloat16)


def vmem(*dims):
    return pltpu.VMEM(dims, jnp.bfloat16)


def in_hbm(array):
    return pltpu.with_memory_space_constraint(array, pltpu.HBM)


ANY = pl.BlockSpec(memory_space=pl.ANY)
WHOLE = pl.BlockSpec(memory_space=pltpu.VMEM)
SCALARS = pl.BlockSpec(memory_space=pltpu.SMEM)


def call(kernel, ins, outs, scratch, flops, name, out_spec=WHOLE, limit=40):
    return pl.pallas_call(
        kernel,
        out_shape=outs,
        in_specs=[SCALARS, *ins],
        out_specs=jax.tree.map(lambda _: out_spec, outs),
        scratch_shapes=scratch,
        compiler_params=pltpu.CompilerParams(vmem_limit_bytes=limit * 1024 * 1024),
        cost_estimate=pl.CostEstimate(flops=flops, bytes_accessed=4_000_000, transcendentals=0),
        name=name,
    )


def odd_pairs(size):
    return [(i, (i - 1 if i % 2 == 0 else i + 1) % size) for i in range(size)]


def even_pairs(size):
    return [(i, i ^ 1) for i in range(size)]


def per_device(tokens, w_qkv, w_out):
    lons, lats = lax.axis_size("lon"), lax.axis_size("lat")
    where = jnp.stack([lax.axis_index("lon"), lax.axis_index("lat")]).astype(jnp.int32)
    cells = tokens.transpose(1, 2, 0, 3).reshape(CELLS, LEVELS, D)
    w_qkv, w_out_hbm = in_hbm(w_qkv), in_hbm(w_out)

    kv_odd, wire_odd, first_odd, kv0, x_even, normed_even, w_q, w_o, w_kv = call(
        odd_kernel,
        [ANY] * 3,
        (
            shape(HALF, D), shape(HALF, D), shape(SIDE, D), shape(2 * SIDE, D), shape(SIDE, D),
            shape(SIDE, D), shape(D, HD), shape(HD, D), shape(2, D, HD),
        ),
        [
            vmem(CELLS, LEVELS, D), pltpu.VMEM((OWN, D), jnp.float32), vmem(SIDE, D), vmem(2 * SIDE, D),
            vmem(SIDE, HD), vmem(SIDE, D), vmem(2, D, HD), pltpu.SemaphoreType.DMA((7,)),
        ],
        2_000_000_000,
        "odd_side",
    )(where, in_hbm(cells), w_qkv, w_out_hbm)
    lon_odd = lax.ppermute(kv_odd, "lon", odd_pairs(lons))

    kv_even, wire_even, first_even = call(
        even_kernel,
        [WHOLE] * 6,
        (shape(HALF, D), shape(HALF, D), shape(SIDE, D)),
        [vmem(SIDE, HD), vmem(SIDE, D)],
        2_000_000_000,
        "even_side",
    )(where, x_even, normed_even, kv0, w_q, w_o, w_kv)
    lon_even = lax.ppermute(kv_even, "lon", even_pairs(lons))

    q, first = call(
        query_kernel,
        [WHOLE] * 4 + [ANY],
        (shape(OWN, HD), shape(OWN, D)),
        [vmem(D, HD), pltpu.SemaphoreType.DMA],
        1_000_000_000,
        "queries",
    )(where, wire_odd, wire_even, first_odd, first_even, w_qkv)

    parts = [kv_odd, kv_even, lon_odd, lon_even]
    lat_odd = lax.ppermute(
        jnp.concatenate([p[:QUART] for p in parts], axis=0), "lat", odd_pairs(lats)[1 : lats - 1]
    )
    lat_even = lax.ppermute(
        jnp.concatenate([p[QUART:] for p in parts], axis=0), "lat", even_pairs(lats)
    )
    shared = [where, q, kv_odd, kv_even, lon_odd, lon_even]
    scratch = [vmem(4 * QWIN, HD), pltpu.VMEM((HALF, D), jnp.float32)]
    near = call(
        near_kernel, [WHOLE] * 8, shape(CELLS // 2, LEVELS, D), scratch, 2_000_000_000, "near_rows"
    )(*shared, lat_even, first, w_out)
    out = call(
        far_kernel,
        [WHOLE] * 9,
        shape(CELLS, LEVELS, D),
        [*scratch, vmem(CELLS // 2, LEVELS, D), pltpu.SemaphoreType.DMA((4,))],
        2_000_000_000,
        "far_rows",
        out_spec=ANY,
    )(*shared, lat_odd, first, w_out, near)
    return out.reshape(ROWS, COLS, LEVELS, D).transpose(2, 0, 1, 3)


def solution(mesh):
    return jax.shard_map(
        per_device,
        mesh=mesh,
        in_specs=(P(None, "lat", "lon", None), P(), P()),
        out_specs=P(None, "lat", "lon", None),
        check_vma=False,
    )
```

```python
import jax
import jax.numpy as jnp
from jax import lax
from jax.experimental import pallas as pl
from jax.experimental.pallas import tpu as pltpu
from jax.sharding import PartitionSpec as P

LEVELS, ROWS, COLS, D = 4, 6, 12, 1024
HD, HEAD = 512, 64
CELLS = ROWS * COLS
OWN = LEVELS * CELLS
HALF = OWN // 2
QUART = HALF // 2
UNIT = 36
WIN = 80
SIDE = 2 * WIN
QWIN = 48
KWIN = 64
NEG = -1e30


def at_least(index, *bounds):
    return sum(jnp.where(index >= bound, 1, 0) for bound in bounds)


def cell_of_window(index, lon_odd):
    side = at_least(index, SIDE)
    index = index - SIDE * side
    pair = at_least(index, WIN)
    index = index - WIN * pair
    valid = index < 2 * UNIT
    level = at_least(index, UNIT)
    index = index - UNIT * level
    row = at_least(index, *range(6, UNIT, 6))
    cell = (row * COLS + 6 * (side ^ lon_odd) + index - 6 * row) * LEVELS + 2 * pair + level
    return jnp.where(valid, cell, -1)


def split_unit(index, group):
    lev = at_least(index, UNIT // 2)
    index = index - UNIT // 2 * lev
    row = at_least(index, 6, 12)
    return jnp.where(group == 0, 1 + lev, 3 - 3 * lev), row, index - 6 * row


def window_of_wire(index, lat_odd):
    k = at_least(index, UNIT, 2 * UNIT, 3 * UNIT)
    level, row, col = split_unit(index - UNIT * k, k & 1)
    row = row + 3 * ((k >> 1) ^ lat_odd)
    return WIN * (level >> 1) + UNIT * (level & 1) + 6 * row + col


def cell_of_queries(index, lat_side, lon_odd):
    n = at_least(index, QWIN, 2 * QWIN, 3 * QWIN)
    group, side = n & 1, n >> 1
    index = index - QWIN * n - 4 * (2 * lat_side + group)
    level, row, col = split_unit(index, group)
    cell = (row * COLS + 6 * (side ^ lon_odd) + col) * LEVELS + level
    return jnp.where((index >= 0) & (index < UNIT), cell, -1)


def query_start(k):
    return k * UNIT // 16 * 16


def key_start(first, size):
    return min(first // 16 * 16, size - KWIN)


def iota(shape, axis):
    return lax.broadcasted_iota(jnp.int32, shape, axis)


def one_hot(rows, lanes):
    return jnp.where(rows == lanes, 1.0, 0.0).astype(jnp.bfloat16)


def layer_normed(values):
    centre = values - jnp.mean(values, axis=-1, keepdims=True)
    spread = jnp.mean(centre * centre, axis=-1, keepdims=True)
    return (centre * lax.rsqrt(spread + 1e-05)).astype(jnp.bfloat16)


def dot(a, b):
    return jnp.dot(a, b, preferred_element_type=jnp.float32)


def four_heads(queries, keys, values, bias):
    rows = queries.shape[0]
    head_of = iota((1, 4 * HEAD), 1) // HEAD
    queries = queries * jnp.bfloat16(0.125)
    spread = jnp.concatenate(
        [jnp.where(head_of == h, queries, jnp.bfloat16(0)) for h in range(4)], axis=0
    )
    scores = lax.dot_general(
        spread, keys, (((1,), (1,)), ((), ())), preferred_element_type=jnp.float32
    )
    scores = scores + bias
    highest = jnp.max(scores, axis=-1, keepdims=True)
    raised = jnp.exp(scores - highest)
    total = jnp.sum(raised, axis=-1, keepdims=True)
    mixed = dot(raised.astype(jnp.bfloat16), values) * (1.0 / total)
    out = mixed[:rows]
    for h in range(1, 4):
        out = jnp.where(head_of == h, mixed[h * rows : (h + 1) * rows], out)
    return out.astype(jnp.bfloat16)


def side_block(lat_odd, x, normed, kv, w_q, w_out, w_kv, first_out, wire_out, kv_out, att, scratch, ready):
    ready(0)
    queries = dot(normed, w_q[...]).astype(jnp.bfloat16)
    bias = jnp.where(iota((1, 2 * WIN), 1) % WIN < 2 * UNIT, 0.0, NEG).astype(jnp.float32)
    for pair in range(2):
        rows = slice(pair * WIN, (pair + 1) * WIN)
        far = slice(SIDE + pair * WIN, SIDE + (pair + 1) * WIN)
        for half in range(2):
            cols = slice(half * 256, half * 256 + 256)
            cols_v = slice(HD + half * 256, HD + half * 256 + 256)
            att[rows, cols] = four_heads(
                queries[rows, cols],
                jnp.concatenate([kv[rows, cols], kv[far, cols]], axis=0),
                jnp.concatenate([kv[rows, cols_v], kv[far, cols_v]], axis=0),
                bias,
            )
    to_wire = one_hot(window_of_wire(iota((HALF, 1), 0), lat_odd), iota((HALF, SIDE), 1))
    ready(1)
    for pair in range(2):
        rows = slice(pair * WIN, (pair + 1) * WIN)
        first = (x[rows, :].astype(jnp.float32) + dot(att[rows, :], w_out[...])).astype(jnp.bfloat16)
        first_out[rows, :] = first
        scratch[rows, :] = layer_normed(first.astype(jnp.float32))
    wire = dot(to_wire, scratch[...]).astype(jnp.bfloat16)
    wire_out[...] = wire
    for i in range(2):
        ready(2 + i)
        kv_out[:, i * HD : (i + 1) * HD] = dot(wire, w_kv[i]).astype(jnp.bfloat16)


def odd_kernel(
    where, x_hbm, w_qkv_hbm, w_out_hbm,
    kv_out, wire_out, first_out, x_even, normed_even, kv0, w_q, w_out, w_kv,
    x_in, x, x_odd, normed, att, scratch, w_kv0, sems,
):
    def part(block, i):
        return w_qkv_hbm.at[block, :, pl.ds(i * HD, HD)]

    pairs = [
        (x_hbm, x_in), (part(0, 1), w_kv0.at[0]), (part(0, 2), w_kv0.at[1]), (part(0, 0), w_q),
        (w_out_hbm.at[0], w_out), (part(1, 1), w_kv.at[0]), (part(1, 2), w_kv.at[1]),
    ]
    copies = [pltpu.make_async_copy(src, dst, sems.at[i]) for i, (src, dst) in enumerate(pairs)]
    for copy in copies:
        copy.start()
    lon_odd, lat_odd = where[0] & 1, where[1] & 1
    rows = 2 * SIDE
    to_window = one_hot(cell_of_window(iota((rows, 1), 0), lon_odd), iota((rows, OWN), 1))
    copies[0].wait()
    for i in range(CELLS):
        x[i * LEVELS : (i + 1) * LEVELS, :] = x_in[i].astype(jnp.float32)
    cells = x[...].astype(jnp.bfloat16)
    for i in range(4):
        span = slice(i * WIN, (i + 1) * WIN)
        ordered = dot(to_window[span], cells)
        target = x_odd if i < 2 else x_even
        target[(i % 2) * WIN : (i % 2 + 1) * WIN, :] = ordered.astype(jnp.bfloat16)
        normed[span, :] = layer_normed(ordered)
    normed_even[...] = normed[SIDE:, :]
    for i in range(2):
        copies[1 + i].wait()
        kv0[:, i * HD : (i + 1) * HD] = dot(normed[...], w_kv0[i]).astype(jnp.bfloat16)
    side_block(
        lat_odd, x_odd, normed[:SIDE, :], kv0, w_q, w_out, w_kv, first_out, wire_out, kv_out, att, scratch,
        lambda i: copies[3 + i].wait(),
    )


def even_kernel(
    where, x, normed, kv0, w_q, w_out, w_kv, kv_out, wire_out, first_out, att, scratch
):
    side_block(
        where[1] & 1, x, normed[...], kv0, w_q, w_out, w_kv, first_out, wire_out, kv_out, att, scratch,
        lambda i: None,
    )


def query_kernel(
    where, wire_odd, wire_even, first_odd, first_even, w_qkv_hbm, q_out, first_out, w_q, sem
):
    copy = pltpu.make_async_copy(w_qkv_hbm.at[1, :, pl.ds(0, HD)], w_q, sem)
    copy.start()
    lane = cell_of_window(iota((1, 2 * SIDE), 1), where[0] & 1)
    to_cell = one_hot(iota((OWN, 2 * SIDE), 0), lane)
    first = jnp.concatenate([first_odd[...], first_even[...]], axis=0)
    first_out[...] = dot(to_cell, first).astype(jnp.bfloat16)
    copy.wait()
    q_out[:HALF, :] = dot(wire_odd[...], w_q[...]).astype(jnp.bfloat16)
    q_out[HALF:, :] = dot(wire_even[...], w_q[...]).astype(jnp.bfloat16)


def lat_side_block(lat_side, where, q, kv_odd, kv_even, lon_odd, lon_even, lat, first, w_out, att, done):
    position = where[1]
    edge = (position == 0) | (position == 3)
    row = iota((QWIN, 4 * KWIN), 0)
    lane = iota((QWIN, 4 * KWIN), 1)
    for side in range(2):
        own, across = ((kv_odd, lon_odd), (kv_even, lon_even))[side]
        for g in range(2):
            k = 2 * lat_side + g
            start = query_start(k)
            firsts = [UNIT * k, UNIT * k, QUART * side + UNIT * g, QUART * (2 + side) + UNIT * g]
            sources = [own, across, lat, lat]
            starts = [key_start(f, s.shape[0]) for f, s in zip(firsts, sources)]
            late = row >= UNIT * k - start + UNIT // 2
            valid = jnp.zeros((QWIN, 4 * KWIN), jnp.bool_)
            for i in range(4):
                at = lane - (i * KWIN + firsts[i] - starts[i])
                inside = (at >= 0) & (at < UNIT)
                if g == 1:
                    inside = inside & ((at >= UNIT // 2) == late)
                if i >= 2 and lat_side == 0:
                    inside = inside & jnp.logical_not(edge)
                valid = valid | inside
            bias = jnp.where(valid, 0.0, NEG).astype(jnp.float32)
            bias = jnp.concatenate([bias] * 4, axis=0)
            n = 2 * side + g
            for half in range(2):
                cols = slice(half * 256, half * 256 + 256)

                def window(base):
                    lanes = slice(base + half * 256, base + half * 256 + 256)
                    parts = [s[f : f + KWIN, lanes] for s, f in zip(sources, starts)]
                    return jnp.concatenate(parts, axis=0)

                att[n * QWIN : (n + 1) * QWIN, cols] = four_heads(
                    q[side * HALF + start : side * HALF + start + QWIN, cols], window(0), window(HD), bias
                )
    lane = cell_of_queries(iota((1, 4 * QWIN), 1), lat_side, where[0] & 1)
    placed = dot(one_hot(iota((HALF, 4 * QWIN), 0), lane), att[...]).astype(jnp.bfloat16)
    rows = pl.ds(pl.multiple_of(HALF * ((position & 1) ^ lat_side), 16), HALF)
    done[...] = first[rows, :].astype(jnp.float32) + dot(placed, w_out[1])


def near_kernel(
    where, q, kv_odd, kv_even, lon_odd, lon_even, lat, first, w_out, out, att, done
):
    lat_side_block(1, where, q, kv_odd, kv_even, lon_odd, lon_even, lat, first, w_out, att, done)
    for i in range(CELLS // 2):
        out[i] = done[i * LEVELS : (i + 1) * LEVELS, :].astype(jnp.bfloat16)


def far_kernel(
    where, q, kv_odd, kv_even, lon_odd, lon_even, lat, first, w_out, near, out, att, done, staged, sems
):
    top = (where[1] & 1) * (CELLS // 2)
    copy = pltpu.make_async_copy(near, out.at[pl.ds(CELLS // 2 - top, CELLS // 2)], sems.at[0])
    copy.start()
    lat_side_block(0, where, q, kv_odd, kv_even, lon_odd, lon_even, lat, first, w_out, att, done)
    copies = [copy]
    step = CELLS // 6
    for j in range(3):
        for i in range(j * step, (j + 1) * step):
            staged[i] = done[i * LEVELS : (i + 1) * LEVELS, :].astype(jnp.bfloat16)
        span = pl.ds(top + j * step, step)
        copies.append(
            pltpu.make_async_copy(staged.at[pl.ds(j * step, step)], out.at[span], sems.at[1 + j])
        )
        copies[-1].start()
    for copy in copies:
        copy.wait()


def shape(*dims):
    return jax.ShapeDtypeStruct(dims, jnp.bfloat16)


def vmem(*dims):
    return pltpu.VMEM(dims, jnp.bfloat16)


def in_hbm(array):
    return pltpu.with_memory_space_constraint(array, pltpu.HBM)


ANY = pl.BlockSpec(memory_space=pl.ANY)
WHOLE = pl.BlockSpec(memory_space=pltpu.VMEM)
SCALARS = pl.BlockSpec(memory_space=pltpu.SMEM)


def call(kernel, ins, outs, scratch, flops, name, out_spec=WHOLE, limit=40):
    return pl.pallas_call(
        kernel,
        out_shape=outs,
        in_specs=[SCALARS, *ins],
        out_specs=jax.tree.map(lambda _: out_spec, outs),
        scratch_shapes=scratch,
        compiler_params=pltpu.CompilerParams(vmem_limit_bytes=limit * 1024 * 1024),
        cost_estimate=pl.CostEstimate(flops=flops, bytes_accessed=4_000_000, transcendentals=0),
        name=name,
    )


def odd_pairs(size):
    return [(i, (i - 1 if i % 2 == 0 else i + 1) % size) for i in range(size)]


def even_pairs(size):
    return [(i, i ^ 1) for i in range(size)]


def odd_side(where, cells, w_qkv, w_out):
    return call(
        odd_kernel,
        [ANY] * 3,
        (
            shape(HALF, D), shape(HALF, D), shape(SIDE, D), shape(SIDE, D), shape(SIDE, D),
            shape(2 * SIDE, D), shape(D, HD), shape(HD, D), shape(2, D, HD),
        ),
        [
            vmem(CELLS, LEVELS, D), pltpu.VMEM((OWN, D), jnp.float32), vmem(SIDE, D), vmem(2 * SIDE, D),
            vmem(SIDE, HD), vmem(SIDE, D), vmem(2, D, HD), pltpu.SemaphoreType.DMA((7,)),
        ],
        2_000_000_000,
        "odd_side",
    )(where, in_hbm(cells), in_hbm(w_qkv), in_hbm(w_out))


def even_side(*args):
    return call(
        even_kernel,
        [WHOLE] * 6,
        (shape(HALF, D), shape(HALF, D), shape(SIDE, D)),
        [vmem(SIDE, HD), vmem(SIDE, D)],
        2_000_000_000,
        "even_side",
    )(*args)


def queries(where, wire_odd, wire_even, first_odd, first_even, w_qkv):
    return call(
        query_kernel,
        [WHOLE] * 4 + [ANY],
        (shape(OWN, HD), shape(OWN, D)),
        [vmem(D, HD), pltpu.SemaphoreType.DMA],
        1_000_000_000,
        "queries",
    )(where, wire_odd, wire_even, first_odd, first_even, in_hbm(w_qkv))


SIDE_SCRATCH = [vmem(4 * QWIN, HD), pltpu.VMEM((HALF, D), jnp.float32)]


def near_rows(*args):
    return call(
        near_kernel,
        [WHOLE] * 8,
        shape(CELLS // 2, LEVELS, D),
        SIDE_SCRATCH,
        2_000_000_000,
        "near_rows",
    )(*args)


def far_rows(*args):
    return call(
        far_kernel,
        [WHOLE] * 9,
        shape(CELLS, LEVELS, D),
        [*SIDE_SCRATCH, vmem(CELLS // 2, LEVELS, D), pltpu.SemaphoreType.DMA((4,))],
        2_000_000_000,
        "far_rows",
        out_spec=ANY,
    )(*args)


def per_device(tokens, w_qkv, w_out):
    lons, lats = lax.axis_size("lon"), lax.axis_size("lat")
    where = jnp.stack([lax.axis_index("lon"), lax.axis_index("lat")]).astype(jnp.int32)
    cells = tokens.transpose(1, 2, 0, 3).reshape(CELLS, LEVELS, D)

    kv_odd, wire_odd, first_odd, *rest = odd_side(where, cells, w_qkv, w_out)
    lon_odd = lax.ppermute(kv_odd, "lon", odd_pairs(lons))
    kv_even, wire_even, first_even = even_side(where, *rest)
    lon_even = lax.ppermute(kv_even, "lon", even_pairs(lons))
    q, first = queries(where, wire_odd, wire_even, first_odd, first_even, w_qkv)
    lon_odd, q = lax.optimization_barrier((lon_odd, q))
    q, first, lon_odd, lon_even = lax.optimization_barrier((q, first, lon_odd, lon_even))

    parts = [kv_odd, kv_even, lon_odd, lon_even]
    to_far = jnp.concatenate([p[:QUART] for p in parts], axis=0)
    to_near = jnp.concatenate([p[QUART:] for p in parts], axis=0)
    lat_odd = lax.ppermute(to_far, "lat", odd_pairs(lats)[1 : lats - 1])
    lat_even = lax.ppermute(to_near, "lat", even_pairs(lats))
    shared = [where, q, kv_odd, kv_even, lon_odd, lon_even]
    near = near_rows(*shared, lat_even, first, w_out)
    out = far_rows(*shared, lat_odd, first, w_out, near)
    return out.reshape(ROWS, COLS, LEVELS, D).transpose(2, 0, 1, 3)


def solution(mesh):
    return jax.shard_map(
        per_device,
        mesh=mesh,
        in_specs=(P(None, "lat", "lon", None), P(), P()),
        out_specs=P(None, "lat", "lon", None),
        check_vma=False,
    )
```

```python
import jax
import jax.numpy as jnp
from jax import lax
from jax.experimental import pallas as pl
from jax.experimental.pallas import tpu as pltpu
from jax.sharding import PartitionSpec as P

LEVELS, ROWS, COLS, D = 4, 6, 12, 1024
HD, HEAD = 512, 64
CELLS = ROWS * COLS
OWN = LEVELS * CELLS
HALF = OWN // 2
QUART = HALF // 2
UNIT = 36
WIN = 80
SIDE = 2 * WIN
QWIN = 48
KWIN = 64
NEG = -1e30


def at_least(index, *bounds):
    return sum(jnp.where(index >= bound, 1, 0) for bound in bounds)


def cell_of_window(index, lon_odd):
    side = at_least(index, SIDE)
    index = index - SIDE * side
    pair = at_least(index, WIN)
    index = index - WIN * pair
    valid = index < 2 * UNIT
    level = at_least(index, UNIT)
    index = index - UNIT * level
    row = at_least(index, *range(6, UNIT, 6))
    cell = (row * COLS + 6 * (side ^ lon_odd) + index - 6 * row) * LEVELS + 2 * pair + level
    return jnp.where(valid, cell, -1)


def split_unit(index, group):
    lev = at_least(index, UNIT // 2)
    index = index - UNIT // 2 * lev
    row = at_least(index, 6, 12)
    return jnp.where(group == 0, 1 + lev, 3 - 3 * lev), row, index - 6 * row


def window_of_wire(index, lat_odd):
    k = at_least(index, UNIT, 2 * UNIT, 3 * UNIT)
    level, row, col = split_unit(index - UNIT * k, k & 1)
    row = row + 3 * ((k >> 1) ^ lat_odd)
    return WIN * (level >> 1) + UNIT * (level & 1) + 6 * row + col


def cell_of_queries(index, lat_side, lon_odd):
    n = at_least(index, QWIN, 2 * QWIN, 3 * QWIN)
    group, side = n & 1, n >> 1
    index = index - QWIN * n - 4 * (2 * lat_side + group)
    level, row, col = split_unit(index, group)
    cell = (row * COLS + 6 * (side ^ lon_odd) + col) * LEVELS + level
    return jnp.where((index >= 0) & (index < UNIT), cell, -1)


def query_start(k):
    return k * UNIT // 16 * 16


def key_start(first, size):
    return min(first // 16 * 16, size - KWIN)


def iota(shape, axis):
    return lax.broadcasted_iota(jnp.int32, shape, axis)


def one_hot(rows, lanes):
    return jnp.where(rows == lanes, 1.0, 0.0).astype(jnp.bfloat16)


def layer_normed(values):
    centre = values - jnp.mean(values, axis=-1, keepdims=True)
    spread = jnp.mean(centre * centre, axis=-1, keepdims=True)
    return (centre * lax.rsqrt(spread + 1e-05)).astype(jnp.bfloat16)


def dot(a, b):
    return jnp.dot(a, b, preferred_element_type=jnp.float32)


def four_heads(queries, keys, values, bias):
    rows = queries.shape[0]
    head_of = iota((1, 4 * HEAD), 1) // HEAD
    queries = queries * jnp.bfloat16(0.125)
    spread = jnp.concatenate(
        [jnp.where(head_of == h, queries, jnp.bfloat16(0)) for h in range(4)], axis=0
    )
    scores = lax.dot_general(
        spread, keys, (((1,), (1,)), ((), ())), preferred_element_type=jnp.float32
    )
    scores = scores + bias
    highest = jnp.max(scores, axis=-1, keepdims=True)
    raised = jnp.exp(scores - highest)
    total = jnp.sum(raised, axis=-1, keepdims=True)
    mixed = dot(raised.astype(jnp.bfloat16), values) * (1.0 / total)
    out = mixed[:rows]
    for h in range(1, 4):
        out = jnp.where(head_of == h, mixed[h * rows : (h + 1) * rows], out)
    return out.astype(jnp.bfloat16)


def side_block(lat_odd, x, normed, kv, w_q, w_out, w_kv, first_out, wire_out, kv_out, att, scratch, ready):
    ready(0)
    queries = dot(normed, w_q[...]).astype(jnp.bfloat16)
    bias = jnp.where(iota((1, 2 * WIN), 1) % WIN < 2 * UNIT, 0.0, NEG).astype(jnp.float32)
    for pair in range(2):
        rows = slice(pair * WIN, (pair + 1) * WIN)
        far = slice(SIDE + pair * WIN, SIDE + (pair + 1) * WIN)
        for half in range(2):
            cols = slice(half * 256, half * 256 + 256)
            cols_v = slice(HD + half * 256, HD + half * 256 + 256)
            att[rows, cols] = four_heads(
                queries[rows, cols],
                jnp.concatenate([kv[rows, cols], kv[far, cols]], axis=0),
                jnp.concatenate([kv[rows, cols_v], kv[far, cols_v]], axis=0),
                bias,
            )
    to_wire = one_hot(window_of_wire(iota((HALF, 1), 0), lat_odd), iota((HALF, SIDE), 1))
    ready(1)
    for pair in range(2):
        rows = slice(pair * WIN, (pair + 1) * WIN)
        first = (x[rows, :].astype(jnp.float32) + dot(att[rows, :], w_out[...])).astype(jnp.bfloat16)
        first_out[rows, :] = first
        scratch[rows, :] = layer_normed(first.astype(jnp.float32))
    wire = dot(to_wire, scratch[...]).astype(jnp.bfloat16)
    wire_out[...] = wire
    for i in range(2):
        ready(2 + i)
        kv_out[:, i * HD : (i + 1) * HD] = dot(wire, w_kv[i]).astype(jnp.bfloat16)


def odd_kernel(
    where, x_hbm, w_qkv_hbm, w_out_hbm,
    kv_out, wire_out, first_out, x_even, normed_even, kv0, w_q, w_out, w_kv,
    x_in, x, x_odd, normed, att, scratch, w_kv0, sems,
):
    def part(block, i):
        return w_qkv_hbm.at[block, :, pl.ds(i * HD, HD)]

    pairs = [
        (x_hbm, x_in), (part(0, 1), w_kv0.at[0]), (part(0, 2), w_kv0.at[1]), (part(0, 0), w_q),
        (w_out_hbm.at[0], w_out), (part(1, 1), w_kv.at[0]), (part(1, 2), w_kv.at[1]),
    ]
    copies = [pltpu.make_async_copy(src, dst, sems.at[i]) for i, (src, dst) in enumerate(pairs)]
    for copy in copies:
        copy.start()
    lon_odd, lat_odd = where[0] & 1, where[1] & 1
    rows = 2 * SIDE
    to_window = one_hot(cell_of_window(iota((rows, 1), 0), lon_odd), iota((rows, OWN), 1))
    copies[0].wait()
    for i in range(CELLS):
        x[i * LEVELS : (i + 1) * LEVELS, :] = x_in[i].astype(jnp.float32)
    cells = x[...].astype(jnp.bfloat16)
    for i in range(4):
        span = slice(i * WIN, (i + 1) * WIN)
        ordered = dot(to_window[span], cells)
        target = x_odd if i < 2 else x_even
        target[(i % 2) * WIN : (i % 2 + 1) * WIN, :] = ordered.astype(jnp.bfloat16)
        normed[span, :] = layer_normed(ordered)
    normed_even[...] = normed[SIDE:, :]
    for i in range(2):
        copies[1 + i].wait()
        kv0[:, i * HD : (i + 1) * HD] = dot(normed[...], w_kv0[i]).astype(jnp.bfloat16)
    side_block(
        lat_odd, x_odd, normed[:SIDE, :], kv0, w_q, w_out, w_kv, first_out, wire_out, kv_out, att, scratch,
        lambda i: copies[3 + i].wait(),
    )


def even_kernel(
    where, x, normed, kv0, w_q, w_out, w_kv, kv_out, wire_out, first_out, att, scratch
):
    side_block(
        where[1] & 1, x, normed[...], kv0, w_q, w_out, w_kv, first_out, wire_out, kv_out, att, scratch,
        lambda i: None,
    )


def query_kernel(
    where, wire_odd, wire_even, first_odd, first_even, w_qkv_hbm, q_out, first_out, w_q, sem
):
    copy = pltpu.make_async_copy(w_qkv_hbm.at[1, :, pl.ds(0, HD)], w_q, sem)
    copy.start()
    lane = cell_of_window(iota((1, 2 * SIDE), 1), where[0] & 1)
    to_cell = one_hot(iota((OWN, 2 * SIDE), 0), lane)
    first = jnp.concatenate([first_odd[...], first_even[...]], axis=0)
    first_out[...] = dot(to_cell, first).astype(jnp.bfloat16)
    copy.wait()
    q_out[:HALF, :] = dot(wire_odd[...], w_q[...]).astype(jnp.bfloat16)
    q_out[HALF:, :] = dot(wire_even[...], w_q[...]).astype(jnp.bfloat16)


def lat_side_block(
    lat_side, where, q, kv_odd, kv_even, lon_odd, lon_even, direct, corner, corner_at, first, w_out, att, done
):
    position = where[1]
    edge = (position == 0) | (position == 3)
    row = iota((QWIN, 4 * KWIN), 0)
    lane = iota((QWIN, 4 * KWIN), 1)
    for side in range(2):
        own, across = ((kv_odd, lon_odd), (kv_even, lon_even))[side]
        for g in range(2):
            k = 2 * lat_side + g
            start = query_start(k)
            firsts = [UNIT * k, UNIT * k, QUART * side + UNIT * g, corner_at + QUART * side + UNIT * g]
            sources = [own, across, direct, corner]
            starts = [key_start(f, s.shape[0]) for f, s in zip(firsts, sources)]
            late = row >= UNIT * k - start + UNIT // 2
            valid = jnp.zeros((QWIN, 4 * KWIN), jnp.bool_)
            for i in range(4):
                at = lane - (i * KWIN + firsts[i] - starts[i])
                inside = (at >= 0) & (at < UNIT)
                if g == 1:
                    inside = inside & ((at >= UNIT // 2) == late)
                if i >= 2 and lat_side == 0:
                    inside = inside & jnp.logical_not(edge)
                valid = valid | inside
            bias = jnp.where(valid, 0.0, NEG).astype(jnp.float32)
            bias = jnp.concatenate([bias] * 4, axis=0)
            n = 2 * side + g
            for half in range(2):
                cols = slice(half * 256, half * 256 + 256)

                def window(base):
                    lanes = slice(base + half * 256, base + half * 256 + 256)
                    parts = [s[f : f + KWIN, lanes] for s, f in zip(sources, starts)]
                    return jnp.concatenate(parts, axis=0)

                att[n * QWIN : (n + 1) * QWIN, cols] = four_heads(
                    q[side * HALF + start : side * HALF + start + QWIN, cols], window(0), window(HD), bias
                )
    lane = cell_of_queries(iota((1, 4 * QWIN), 1), lat_side, where[0] & 1)
    placed = dot(one_hot(iota((HALF, 4 * QWIN), 0), lane), att[...]).astype(jnp.bfloat16)
    rows = pl.ds(pl.multiple_of(HALF * ((position & 1) ^ lat_side), 16), HALF)
    done[...] = first[rows, :].astype(jnp.float32) + dot(placed, w_out[1])


def near_kernel(
    where, q, kv_odd, kv_even, lon_odd, lon_even, lat, first, w_out, out, att, done
):
    lat_side_block(
        1, where, q, kv_odd, kv_even, lon_odd, lon_even, lat, lat, HALF, first, w_out, att, done
    )
    for i in range(CELLS // 2):
        out[i] = done[i * LEVELS : (i + 1) * LEVELS, :].astype(jnp.bfloat16)


def far_kernel(
    where, q, kv_odd, kv_even, lon_odd, lon_even, direct, corner, first, w_out, near, out,
    att, done, staged, sems,
):
    top = (where[1] & 1) * (CELLS // 2)
    copy = pltpu.make_async_copy(near, out.at[pl.ds(CELLS // 2 - top, CELLS // 2)], sems.at[0])
    copy.start()
    lat_side_block(
        0, where, q, kv_odd, kv_even, lon_odd, lon_even, direct, corner, 0, first, w_out, att, done
    )
    copies = [copy]
    step = CELLS // 6
    for j in range(3):
        for i in range(j * step, (j + 1) * step):
            staged[i] = done[i * LEVELS : (i + 1) * LEVELS, :].astype(jnp.bfloat16)
        span = pl.ds(top + j * step, step)
        copies.append(
            pltpu.make_async_copy(staged.at[pl.ds(j * step, step)], out.at[span], sems.at[1 + j])
        )
        copies[-1].start()
    for copy in copies:
        copy.wait()


def shape(*dims):
    return jax.ShapeDtypeStruct(dims, jnp.bfloat16)


def vmem(*dims):
    return pltpu.VMEM(dims, jnp.bfloat16)


def in_hbm(array):
    return pltpu.with_memory_space_constraint(array, pltpu.HBM)


ANY = pl.BlockSpec(memory_space=pl.ANY)
WHOLE = pl.BlockSpec(memory_space=pltpu.VMEM)
SCALARS = pl.BlockSpec(memory_space=pltpu.SMEM)


def call(kernel, ins, outs, scratch, flops, name, out_spec=WHOLE, limit=40):
    return pl.pallas_call(
        kernel,
        out_shape=outs,
        in_specs=[SCALARS, *ins],
        out_specs=jax.tree.map(lambda _: out_spec, outs),
        scratch_shapes=scratch,
        compiler_params=pltpu.CompilerParams(vmem_limit_bytes=limit * 1024 * 1024),
        cost_estimate=pl.CostEstimate(flops=flops, bytes_accessed=4_000_000, transcendentals=0),
        name=name,
    )


def odd_side(where, cells, w_qkv, w_out):
    return call(
        odd_kernel,
        [ANY] * 3,
        (
            shape(HALF, D), shape(HALF, D), shape(SIDE, D), shape(SIDE, D), shape(SIDE, D),
            shape(2 * SIDE, D), shape(D, HD), shape(HD, D), shape(2, D, HD),
        ),
        [
            vmem(CELLS, LEVELS, D), pltpu.VMEM((OWN, D), jnp.float32), vmem(SIDE, D), vmem(2 * SIDE, D),
            vmem(SIDE, HD), vmem(SIDE, D), vmem(2, D, HD), pltpu.SemaphoreType.DMA((7,)),
        ],
        2_000_000_000,
        "odd_side",
    )(where, in_hbm(cells), in_hbm(w_qkv), in_hbm(w_out))


def even_side(*args):
    return call(
        even_kernel,
        [WHOLE] * 6,
        (shape(HALF, D), shape(HALF, D), shape(SIDE, D)),
        [vmem(SIDE, HD), vmem(SIDE, D)],
        2_000_000_000,
        "even_side",
    )(*args)


def queries(where, wire_odd, wire_even, first_odd, first_even, w_qkv):
    return call(
        query_kernel,
        [WHOLE] * 4 + [ANY],
        (shape(OWN, HD), shape(OWN, D)),
        [vmem(D, HD), pltpu.SemaphoreType.DMA],
        1_000_000_000,
        "queries",
    )(where, wire_odd, wire_even, first_odd, first_even, in_hbm(w_qkv))


SIDE_SCRATCH = [vmem(4 * QWIN, HD), pltpu.VMEM((HALF, D), jnp.float32)]


def near_rows(*args):
    return call(
        near_kernel,
        [WHOLE] * 8,
        shape(CELLS // 2, LEVELS, D),
        SIDE_SCRATCH,
        2_000_000_000,
        "near_rows",
    )(*args)


def far_rows(*args):
    return call(
        far_kernel,
        [WHOLE] * 10,
        shape(CELLS, LEVELS, D),
        [*SIDE_SCRATCH, vmem(CELLS // 2, LEVELS, D), pltpu.SemaphoreType.DMA((4,))],
        2_000_000_000,
        "far_rows",
        out_spec=ANY,
    )(*args)


def per_device(tokens, w_qkv, w_out):
    lons, lats = lax.axis_size("lon"), lax.axis_size("lat")
    where = jnp.stack([lax.axis_index("lon"), lax.axis_index("lat")]).astype(jnp.int32)
    cells = tokens.transpose(1, 2, 0, 3).reshape(CELLS, LEVELS, D)

    kv_odd, wire_odd, first_odd, *rest = odd_side(where, cells, w_qkv, w_out)
    up = [(i, (i + 1) % lons) for i in range(1, lons, 2)]
    from_below = lax.ppermute(kv_odd, "lon", up)
    kv_even, wire_even, first_even = even_side(where, *rest)
    lon_even = lax.ppermute(kv_even, "lon", [(i, i ^ 1) for i in range(lons)])
    far_pairs = [pair for i in range(1, lats - 1, 2) for pair in ((i, i + 1), (i + 1, i))]
    own_far = jnp.concatenate([kv_odd[:QUART], kv_even[:QUART]], axis=0)
    direct = lax.ppermute(own_far, "lat", far_pairs)
    from_above = lax.ppermute(kv_odd, "lon", [(j, i) for i, j in up])
    q, first = queries(where, wire_odd, wire_even, first_odd, first_even, w_qkv)

    received = [q, first]
    for array in (from_below, lon_even, direct, from_above):
        received = list(lax.optimization_barrier((*received, array)))
    q, first, from_below, lon_even, direct, from_above = received
    lon_odd = jnp.where(where[0] % 2 == 0, from_below, from_above)

    corner_far = jnp.concatenate([lon_odd[:QUART], lon_even[:QUART]], axis=0)
    to_near = jnp.concatenate([p[QUART:] for p in (kv_odd, kv_even, lon_odd, lon_even)], axis=0)
    corner = lax.ppermute(corner_far, "lat", far_pairs)
    from_near = lax.ppermute(to_near, "lat", [(i, i ^ 1) for i in range(lats)])
    shared = [where, q, kv_odd, kv_even, lon_odd, lon_even]
    near = near_rows(*shared, from_near, first, w_out)
    out = far_rows(*shared, direct, corner, first, w_out, near)
    return out.reshape(ROWS, COLS, LEVELS, D).transpose(2, 0, 1, 3)


def solution(mesh):
    return jax.shard_map(
        per_device,
        mesh=mesh,
        in_specs=(P(None, "lat", "lon", None), P(), P()),
        out_specs=P(None, "lat", "lon", None),
        check_vma=False,
    )
```

```python
import jax
import jax.numpy as jnp
from jax import lax
from jax.experimental import pallas as pl
from jax.experimental.pallas import tpu as pltpu
from jax.sharding import PartitionSpec as P

LEVELS, ROWS, COLS, D = 4, 6, 12, 1024
HD, HEAD = 512, 64
CELLS = ROWS * COLS
OWN = LEVELS * CELLS
HALF = OWN // 2
QUART = HALF // 2
UNIT = 36
WIN = 80
SIDE = 2 * WIN
QWIN = 48
KWIN = 64
NEG = -1e30


def at_least(index, *bounds):
    return sum(jnp.where(index >= bound, 1, 0) for bound in bounds)


def cell_of_window(index, lon_odd):
    side = at_least(index, SIDE)
    index = index - SIDE * side
    pair = at_least(index, WIN)
    index = index - WIN * pair
    valid = index < 2 * UNIT
    level = at_least(index, UNIT)
    index = index - UNIT * level
    row = at_least(index, *range(6, UNIT, 6))
    cell = (row * COLS + 6 * (side ^ lon_odd) + index - 6 * row) * LEVELS + 2 * pair + level
    return jnp.where(valid, cell, -1)


def split_unit(index, group):
    lev = at_least(index, UNIT // 2)
    index = index - UNIT // 2 * lev
    row = at_least(index, 6, 12)
    return jnp.where(group == 0, 1 + lev, 3 - 3 * lev), row, index - 6 * row


def window_of_wire(index, lat_odd):
    k = at_least(index, UNIT, 2 * UNIT, 3 * UNIT)
    level, row, col = split_unit(index - UNIT * k, k & 1)
    row = row + 3 * ((k >> 1) ^ lat_odd)
    return WIN * (level >> 1) + UNIT * (level & 1) + 6 * row + col


def cell_of_queries(index, lat_side, lon_odd):
    n = at_least(index, QWIN, 2 * QWIN, 3 * QWIN)
    group, side = n & 1, n >> 1
    index = index - QWIN * n - 4 * (2 * lat_side + group)
    level, row, col = split_unit(index, group)
    cell = (row * COLS + 6 * (side ^ lon_odd) + col) * LEVELS + level
    return jnp.where((index >= 0) & (index < UNIT), cell, -1)


def query_start(k):
    return k * UNIT // 16 * 16


def key_start(first, size):
    return min(first // 16 * 16, size - KWIN)


def iota(shape, axis):
    return lax.broadcasted_iota(jnp.int32, shape, axis)


def one_hot(rows, lanes):
    return jnp.where(rows == lanes, 1.0, 0.0).astype(jnp.bfloat16)


def layer_normed(values):
    centre = values - jnp.mean(values, axis=-1, keepdims=True)
    spread = jnp.mean(centre * centre, axis=-1, keepdims=True)
    return (centre * lax.rsqrt(spread + 1e-05)).astype(jnp.bfloat16)


def dot(a, b):
    return jnp.dot(a, b, preferred_element_type=jnp.float32)


def four_heads(queries, keys, values, bias):
    rows = queries.shape[0]
    head_of = iota((1, 4 * HEAD), 1) // HEAD
    queries = queries * jnp.bfloat16(0.125)
    spread = jnp.concatenate(
        [jnp.where(head_of == h, queries, jnp.bfloat16(0)) for h in range(4)], axis=0
    )
    scores = lax.dot_general(
        spread, keys, (((1,), (1,)), ((), ())), preferred_element_type=jnp.float32
    )
    scores = scores + bias
    highest = jnp.max(scores, axis=-1, keepdims=True)
    raised = jnp.exp(scores - highest)
    total = jnp.sum(raised, axis=-1, keepdims=True)
    mixed = dot(raised.astype(jnp.bfloat16), values) * (1.0 / total)
    out = mixed[:rows]
    for h in range(1, 4):
        out = jnp.where(head_of == h, mixed[h * rows : (h + 1) * rows], out)
    return out.astype(jnp.bfloat16)


def side_block(lat_odd, x, normed, kv, w_q, w_out, w_kv, first_out, wire_out, kv_out, att, scratch, ready):
    ready(0)
    queries = dot(normed, w_q[...]).astype(jnp.bfloat16)
    bias = jnp.where(iota((1, 2 * WIN), 1) % WIN < 2 * UNIT, 0.0, NEG).astype(jnp.float32)
    for pair in range(2):
        rows = slice(pair * WIN, (pair + 1) * WIN)
        far = slice(SIDE + pair * WIN, SIDE + (pair + 1) * WIN)
        for half in range(2):
            cols = slice(half * 256, half * 256 + 256)
            cols_v = slice(HD + half * 256, HD + half * 256 + 256)
            att[rows, cols] = four_heads(
                queries[rows, cols],
                jnp.concatenate([kv[rows, cols], kv[far, cols]], axis=0),
                jnp.concatenate([kv[rows, cols_v], kv[far, cols_v]], axis=0),
                bias,
            )
    to_wire = one_hot(window_of_wire(iota((HALF, 1), 0), lat_odd), iota((HALF, SIDE), 1))
    ready(1)
    for pair in range(2):
        rows = slice(pair * WIN, (pair + 1) * WIN)
        first = (x[rows, :].astype(jnp.float32) + dot(att[rows, :], w_out[...])).astype(jnp.bfloat16)
        first_out[rows, :] = first
        scratch[rows, :] = layer_normed(first.astype(jnp.float32))
    wire = dot(to_wire, scratch[...]).astype(jnp.bfloat16)
    wire_out[...] = wire
    for i in range(2):
        ready(2 + i)
        kv_out[:, i * HD : (i + 1) * HD] = dot(wire, w_kv[i]).astype(jnp.bfloat16)


def odd_kernel(
    where, x_hbm, w_qkv_hbm, w_out_hbm,
    kv_out, wire_out, first_out, kv_even, wire_even, first_even, x_even, normed_even, kv0, w_q, w_out, w_kv,
    x_in, x, x_odd, normed, att, scratch, w_kv0, sems,
):
    def part(block, i):
        return w_qkv_hbm.at[block, :, pl.ds(i * HD, HD)]

    pairs = [
        (x_hbm, x_in), (part(0, 1), w_kv0.at[0]), (part(0, 2), w_kv0.at[1]), (part(0, 0), w_q),
        (w_out_hbm.at[0], w_out), (part(1, 1), w_kv.at[0]), (part(1, 2), w_kv.at[1]),
    ]
    copies = [pltpu.make_async_copy(src, dst, sems.at[i]) for i, (src, dst) in enumerate(pairs)]
    for copy in copies:
        copy.start()
    lon_odd, lat_odd = where[0] & 1, where[1] & 1
    rows = 2 * SIDE
    to_window = one_hot(cell_of_window(iota((rows, 1), 0), lon_odd), iota((rows, OWN), 1))
    copies[0].wait()
    for i in range(CELLS):
        x[i * LEVELS : (i + 1) * LEVELS, :] = x_in[i].astype(jnp.float32)
    cells = x[...].astype(jnp.bfloat16)
    for i in range(4):
        span = slice(i * WIN, (i + 1) * WIN)
        ordered = dot(to_window[span], cells)
        target = x_odd if i < 2 else x_even
        target[(i % 2) * WIN : (i % 2 + 1) * WIN, :] = ordered.astype(jnp.bfloat16)
        normed[span, :] = layer_normed(ordered)
    normed_even[...] = normed[SIDE:, :]
    for i in range(2):
        copies[1 + i].wait()
        kv0[:, i * HD : (i + 1) * HD] = dot(normed[...], w_kv0[i]).astype(jnp.bfloat16)
    side_block(
        lat_odd, x_odd, normed[:SIDE, :], kv0, w_q, w_out, w_kv, first_out, wire_out, kv_out, att, scratch,
        lambda i: copies[3 + i].wait(),
    )

    @pl.when(lon_odd == 0)
    def _():
        side_block(
            lat_odd, x_even, normed_even[...], kv0, w_q, w_out, w_kv, first_even, wire_even, kv_even, att, scratch,
            lambda i: None,
        )


def even_kernel(
    where, kv_odd, kv_made, wire_made, first_made, x, normed, kv0, w_q, w_out, w_kv,
    kv_out, wire_out, first_out, own_far, att, scratch,
):
    @pl.when(where[0] & 1 == 1)
    def _():
        side_block(
            where[1] & 1, x, normed[...], kv0, w_q, w_out, w_kv, first_out, wire_out, kv_out, att, scratch,
            lambda i: None,
        )

    @pl.when(where[0] & 1 == 0)
    def _():
        kv_out[...] = kv_made[...]
        wire_out[...] = wire_made[...]
        first_out[...] = first_made[...]

    own_far[0] = kv_odd[:QUART, :]
    own_far[1] = kv_out[:QUART, :]


def query_kernel(
    where, wire_odd, wire_even, first_odd, first_even, w_qkv_hbm, q_out, first_out, w_q, sem
):
    copy = pltpu.make_async_copy(w_qkv_hbm.at[1, :, pl.ds(0, HD)], w_q, sem)
    copy.start()
    lane = cell_of_window(iota((1, 2 * SIDE), 1), where[0] & 1)
    to_cell = one_hot(iota((OWN, 2 * SIDE), 0), lane)
    first = jnp.concatenate([first_odd[...], first_even[...]], axis=0)
    first_out[...] = dot(to_cell, first).astype(jnp.bfloat16)
    copy.wait()
    q_out[:HALF, :] = dot(wire_odd[...], w_q[...]).astype(jnp.bfloat16)
    q_out[HALF:, :] = dot(wire_even[...], w_q[...]).astype(jnp.bfloat16)


def lat_side_block(
    lat_side, where, q, kv_odd, kv_even, lon_odd, lon_even, direct, corner, corner_at, first, w_out, att, done
):
    position = where[1]
    edge = (position == 0) | (position == 3)
    row = iota((QWIN, 4 * KWIN), 0)
    lane = iota((QWIN, 4 * KWIN), 1)
    for side in range(2):
        own, across = ((kv_odd, lon_odd), (kv_even, lon_even))[side]
        for g in range(2):
            k = 2 * lat_side + g
            start = query_start(k)
            firsts = [UNIT * k, UNIT * k, QUART * side + UNIT * g, corner_at + QUART * side + UNIT * g]
            sources = [own, across, direct, corner]
            starts = [key_start(f, s.shape[0]) for f, s in zip(firsts, sources)]
            late = row >= UNIT * k - start + UNIT // 2
            valid = jnp.zeros((QWIN, 4 * KWIN), jnp.bool_)
            for i in range(4):
                at = lane - (i * KWIN + firsts[i] - starts[i])
                inside = (at >= 0) & (at < UNIT)
                if g == 1:
                    inside = inside & ((at >= UNIT // 2) == late)
                if i >= 2 and lat_side == 0:
                    inside = inside & jnp.logical_not(edge)
                valid = valid | inside
            bias = jnp.where(valid, 0.0, NEG).astype(jnp.float32)
            bias = jnp.concatenate([bias] * 4, axis=0)
            n = 2 * side + g
            for half in range(2):
                cols = slice(half * 256, half * 256 + 256)

                def window(base):
                    lanes = slice(base + half * 256, base + half * 256 + 256)
                    parts = [s[f : f + KWIN, lanes] for s, f in zip(sources, starts)]
                    return jnp.concatenate(parts, axis=0)

                att[n * QWIN : (n + 1) * QWIN, cols] = four_heads(
                    q[side * HALF + start : side * HALF + start + QWIN, cols], window(0), window(HD), bias
                )
    lane = cell_of_queries(iota((1, 4 * QWIN), 1), lat_side, where[0] & 1)
    placed = dot(one_hot(iota((HALF, 4 * QWIN), 0), lane), att[...]).astype(jnp.bfloat16)
    rows = pl.ds(pl.multiple_of(HALF * ((position & 1) ^ lat_side), 16), HALF)
    done[...] = first[rows, :].astype(jnp.float32) + dot(placed, w_out[1])


def near_kernel(
    where, q, kv_odd, kv_even, lon_odd, lon_even, lat, first, w_out, out, att, done
):
    lat_side_block(
        1, where, q, kv_odd, kv_even, lon_odd, lon_even, lat, lat, HALF, first, w_out, att, done
    )
    for i in range(CELLS // 2):
        out[i] = done[i * LEVELS : (i + 1) * LEVELS, :].astype(jnp.bfloat16)


def far_kernel(
    where, q, kv_odd, kv_even, lon_odd, lon_even, direct, corner, first, w_out, near, out,
    att, done, staged, sems,
):
    top = (where[1] & 1) * (CELLS // 2)
    copy = pltpu.make_async_copy(near, out.at[pl.ds(CELLS // 2 - top, CELLS // 2)], sems.at[0])
    copy.start()
    lat_side_block(
        0, where, q, kv_odd, kv_even, lon_odd, lon_even, direct, corner, 0, first, w_out, att, done
    )
    copies = [copy]
    step = CELLS // 6
    for j in range(3):
        for i in range(j * step, (j + 1) * step):
            staged[i] = done[i * LEVELS : (i + 1) * LEVELS, :].astype(jnp.bfloat16)
        span = pl.ds(top + j * step, step)
        copies.append(
            pltpu.make_async_copy(staged.at[pl.ds(j * step, step)], out.at[span], sems.at[1 + j])
        )
        copies[-1].start()
    for copy in copies:
        copy.wait()


def shape(*dims):
    return jax.ShapeDtypeStruct(dims, jnp.bfloat16)


def vmem(*dims):
    return pltpu.VMEM(dims, jnp.bfloat16)


def in_hbm(array):
    return pltpu.with_memory_space_constraint(array, pltpu.HBM)


ANY = pl.BlockSpec(memory_space=pl.ANY)
WHOLE = pl.BlockSpec(memory_space=pltpu.VMEM)
SCALARS = pl.BlockSpec(memory_space=pltpu.SMEM)


def call(kernel, ins, outs, scratch, flops, name, out_spec=WHOLE, limit=40):
    return pl.pallas_call(
        kernel,
        out_shape=outs,
        in_specs=[SCALARS, *ins],
        out_specs=jax.tree.map(lambda _: out_spec, outs),
        scratch_shapes=scratch,
        compiler_params=pltpu.CompilerParams(vmem_limit_bytes=limit * 1024 * 1024),
        cost_estimate=pl.CostEstimate(flops=flops, bytes_accessed=4_000_000, transcendentals=0),
        name=name,
    )


def odd_side(where, cells, w_qkv, w_out):
    return call(
        odd_kernel,
        [ANY] * 3,
        (
            shape(HALF, D), shape(HALF, D), shape(SIDE, D), shape(HALF, D), shape(HALF, D), shape(SIDE, D),
            shape(SIDE, D), shape(SIDE, D), shape(2 * SIDE, D), shape(D, HD), shape(HD, D), shape(2, D, HD),
        ),
        [
            vmem(CELLS, LEVELS, D), pltpu.VMEM((OWN, D), jnp.float32), vmem(SIDE, D), vmem(2 * SIDE, D),
            vmem(SIDE, HD), vmem(SIDE, D), vmem(2, D, HD), pltpu.SemaphoreType.DMA((7,)),
        ],
        2_000_000_000,
        "odd_side",
    )(where, in_hbm(cells), in_hbm(w_qkv), in_hbm(w_out))


def even_side(*args):
    return call(
        even_kernel,
        [WHOLE] * 10,
        (shape(HALF, D), shape(HALF, D), shape(SIDE, D), shape(2, QUART, D)),
        [vmem(SIDE, HD), vmem(SIDE, D)],
        2_000_000_000,
        "even_side",
    )(*args)


def queries(where, wire_odd, wire_even, first_odd, first_even, w_qkv):
    return call(
        query_kernel,
        [WHOLE] * 4 + [ANY],
        (shape(OWN, HD), shape(OWN, D)),
        [vmem(D, HD), pltpu.SemaphoreType.DMA],
        1_000_000_000,
        "queries",
    )(where, wire_odd, wire_even, first_odd, first_even, in_hbm(w_qkv))


SIDE_SCRATCH = [vmem(4 * QWIN, HD), pltpu.VMEM((HALF, D), jnp.float32)]


def near_rows(*args):
    return call(
        near_kernel,
        [WHOLE] * 8,
        shape(CELLS // 2, LEVELS, D),
        SIDE_SCRATCH,
        2_000_000_000,
        "near_rows",
    )(*args)


def far_rows(*args):
    return call(
        far_kernel,
        [WHOLE] * 10,
        shape(CELLS, LEVELS, D),
        [*SIDE_SCRATCH, vmem(CELLS // 2, LEVELS, D), pltpu.SemaphoreType.DMA((4,))],
        2_000_000_000,
        "far_rows",
        out_spec=ANY,
    )(*args)


def per_device(tokens, w_qkv, w_out):
    lons, lats = lax.axis_size("lon"), lax.axis_size("lat")
    where = jnp.stack([lax.axis_index("lon"), lax.axis_index("lat")]).astype(jnp.int32)
    cells = tokens.transpose(1, 2, 0, 3).reshape(CELLS, LEVELS, D)

    kv_odd, wire_odd, first_odd, *rest = odd_side(where, cells, w_qkv, w_out)
    odd_pairs = [(i, ((i + 1) ^ 1) - 1) for i in range(lons)]
    lon_odd = lax.ppermute(kv_odd, "lon", [(i, j % lons) for i, j in odd_pairs])
    kv_even, wire_even, first_even, own_far = even_side(where, kv_odd, *rest)
    lon_even = lax.ppermute(kv_even, "lon", [(i, i ^ 1) for i in range(lons)])
    far_pairs = [pair for i in range(1, lats - 1, 2) for pair in ((i, i + 1), (i + 1, i))]
    direct = lax.ppermute(own_far, "lat", far_pairs).reshape(HALF, D)
    q, first = queries(where, wire_odd, wire_even, first_odd, first_even, w_qkv)

    received = [q, first]
    for array in (lon_odd, lon_even, direct):
        received = list(lax.optimization_barrier((*received, array)))
    q, first, lon_odd, lon_even, direct = received

    corner_far = jnp.concatenate([lon_odd[:QUART], lon_even[:QUART]], axis=0)
    to_near = jnp.concatenate([p[QUART:] for p in (kv_odd, kv_even, lon_odd, lon_even)], axis=0)
    corner = lax.ppermute(corner_far, "lat", far_pairs)
    from_near = lax.ppermute(to_near, "lat", [(i, i ^ 1) for i in range(lats)])
    shared = [where, q, kv_odd, kv_even, lon_odd, lon_even]
    near = near_rows(*shared, from_near, first, w_out)
    out = far_rows(*shared, direct, corner, first, w_out, near)
    return out.reshape(ROWS, COLS, LEVELS, D).transpose(2, 0, 1, 3)


def solution(mesh):
    return jax.shard_map(
        per_device,
        mesh=mesh,
        in_specs=(P(None, "lat", "lon", None), P(), P()),
        out_specs=P(None, "lat", "lon", None),
        check_vma=False,
    )
```

```python
import jax
import jax.numpy as jnp
from jax import lax
from jax.experimental import pallas as pl
from jax.experimental.pallas import tpu as pltpu
from jax.sharding import PartitionSpec as P

LEVELS, ROWS, COLS, D = 4, 6, 12, 1024
HD, HEAD = 512, 64
CELLS = ROWS * COLS
OWN = LEVELS * CELLS
HALF = OWN // 2
QUART = HALF // 2
UNIT = 36
WIN = 80
SIDE = 2 * WIN
QWIN = 48
KWIN = 64
NEG = -1e30


def at_least(index, *bounds):
    return sum(jnp.where(index >= bound, 1, 0) for bound in bounds)


def cell_of_window(index):
    side = at_least(index, SIDE)
    index = index - SIDE * side
    pair = at_least(index, WIN)
    index = index - WIN * pair
    valid = index < 2 * UNIT
    level = at_least(index, UNIT)
    index = index - UNIT * level
    row = at_least(index, *range(6, UNIT, 6))
    cell = (row * COLS + 6 * (1 - side) + index - 6 * row) * LEVELS + 2 * pair + level
    return jnp.where(valid, cell, -1)


def split_unit(index, group):
    lev = at_least(index, UNIT // 2)
    index = index - UNIT // 2 * lev
    row = at_least(index, 6, 12)
    return jnp.where(group == 0, 1 + lev, 3 - 3 * lev), row, index - 6 * row


def window_of_wire(index, lat_odd):
    k = at_least(index, UNIT, 2 * UNIT, 3 * UNIT)
    level, row, col = split_unit(index - UNIT * k, k & 1)
    row = row + 3 * ((k >> 1) ^ lat_odd)
    return WIN * (level >> 1) + UNIT * (level & 1) + 6 * row + col


def cell_of_queries(index, lat_side):
    n = at_least(index, QWIN, 2 * QWIN, 3 * QWIN)
    group, side = n & 1, n >> 1
    index = index - QWIN * n - 4 * (2 * lat_side + group)
    level, row, col = split_unit(index, group)
    cell = (row * COLS + 6 * (1 - side) + col) * LEVELS + level
    return jnp.where((index >= 0) & (index < UNIT), cell, -1)


def query_start(k):
    return k * UNIT // 16 * 16


def key_start(first, size):
    return min(first // 16 * 16, size - KWIN)


def iota(shape, axis):
    return lax.broadcasted_iota(jnp.int32, shape, axis)


def one_hot(rows, lanes):
    return jnp.where(rows == lanes, 1.0, 0.0).astype(jnp.bfloat16)


def layer_normed(values):
    centre = values - jnp.mean(values, axis=-1, keepdims=True)
    spread = jnp.mean(centre * centre, axis=-1, keepdims=True)
    return (centre * lax.rsqrt(spread + 1e-05)).astype(jnp.bfloat16)


def dot(a, b):
    return jnp.dot(a, b, preferred_element_type=jnp.float32)


def four_heads(queries, keys, values, bias):
    rows = queries.shape[0]
    head_of = iota((1, 4 * HEAD), 1) // HEAD
    queries = queries * jnp.bfloat16(0.125)
    spread = jnp.concatenate(
        [jnp.where(head_of == h, queries, jnp.bfloat16(0)) for h in range(4)], axis=0
    )
    scores = lax.dot_general(
        spread, keys, (((1,), (1,)), ((), ())), preferred_element_type=jnp.float32
    )
    scores = scores + bias
    highest = jnp.max(scores, axis=-1, keepdims=True)
    raised = jnp.exp(scores - highest)
    total = jnp.sum(raised, axis=-1, keepdims=True)
    mixed = dot(raised.astype(jnp.bfloat16), values) * (1.0 / total)
    out = mixed[:rows]
    for h in range(1, 4):
        out = jnp.where(head_of == h, mixed[h * rows : (h + 1) * rows], out)
    return out.astype(jnp.bfloat16)


def side_block(lat_odd, x, normed, kv, w_q, w_out, w_kv, first_out, wire_out, kv_out, att, scratch, ready):
    ready(0)
    queries = dot(normed, w_q[...]).astype(jnp.bfloat16)
    bias = jnp.where(iota((1, 2 * WIN), 1) % WIN < 2 * UNIT, 0.0, NEG).astype(jnp.float32)
    for pair in range(2):
        rows = slice(pair * WIN, (pair + 1) * WIN)
        far = slice(SIDE + pair * WIN, SIDE + (pair + 1) * WIN)
        for half in range(2):
            cols = slice(half * 256, half * 256 + 256)
            cols_v = slice(HD + half * 256, HD + half * 256 + 256)
            att[rows, cols] = four_heads(
                queries[rows, cols],
                jnp.concatenate([kv[rows, cols], kv[far, cols]], axis=0),
                jnp.concatenate([kv[rows, cols_v], kv[far, cols_v]], axis=0),
                bias,
            )
    to_wire = one_hot(window_of_wire(iota((HALF, 1), 0), lat_odd), iota((HALF, SIDE), 1))
    ready(1)
    for pair in range(2):
        rows = slice(pair * WIN, (pair + 1) * WIN)
        first = (x[rows, :].astype(jnp.float32) + dot(att[rows, :], w_out[...])).astype(jnp.bfloat16)
        first_out[rows, :] = first
        scratch[rows, :] = layer_normed(first.astype(jnp.float32))
    wire = dot(to_wire, scratch[...]).astype(jnp.bfloat16)
    wire_out[...] = wire
    for i in range(2):
        ready(2 + i)
        kv_out[:, i * HD : (i + 1) * HD] = dot(wire, w_kv[i]).astype(jnp.bfloat16)


def right_kernel(
    where, x_hbm, w_qkv_hbm, w_out_hbm,
    kv_out, wire_out, first_out, x_left, normed_left, kv0, w_q, w_out, w_kv,
    x_in, x, x_right, normed, att, scratch, w_kv0, sems,
):
    def part(block, i):
        return w_qkv_hbm.at[block, :, pl.ds(i * HD, HD)]

    pairs = [
        (x_hbm, x_in), (part(0, 1), w_kv0.at[0]), (part(0, 2), w_kv0.at[1]), (part(0, 0), w_q),
        (w_out_hbm.at[0], w_out), (part(1, 1), w_kv.at[0]), (part(1, 2), w_kv.at[1]),
    ]
    copies = [pltpu.make_async_copy(src, dst, sems.at[i]) for i, (src, dst) in enumerate(pairs)]
    for copy in copies:
        copy.start()
    lat_odd = where[0] & 1
    rows = 2 * SIDE
    to_window = one_hot(cell_of_window(iota((rows, 1), 0)), iota((rows, OWN), 1))
    copies[0].wait()
    for i in range(CELLS):
        x[i * LEVELS : (i + 1) * LEVELS, :] = x_in[i].astype(jnp.float32)
    cells = x[...].astype(jnp.bfloat16)
    for i in range(4):
        span = slice(i * WIN, (i + 1) * WIN)
        ordered = dot(to_window[span], cells)
        target = x_right if i < 2 else x_left
        target[(i % 2) * WIN : (i % 2 + 1) * WIN, :] = ordered.astype(jnp.bfloat16)
        normed[span, :] = layer_normed(ordered)
    normed_left[...] = normed[SIDE:, :]
    for i in range(2):
        copies[1 + i].wait()
        kv0[:, i * HD : (i + 1) * HD] = dot(normed[...], w_kv0[i]).astype(jnp.bfloat16)
    side_block(
        lat_odd, x_right, normed[:SIDE, :], kv0, w_q, w_out, w_kv, first_out, wire_out, kv_out, att, scratch,
        lambda i: copies[3 + i].wait(),
    )


def left_kernel(
    where, kv_right, x, normed, kv0, w_q, w_out, w_kv, kv_out, wire_out, first_out, own_far, att, scratch
):
    side_block(
        where[0] & 1, x, normed[...], kv0, w_q, w_out, w_kv, first_out, wire_out, kv_out, att, scratch,
        lambda i: None,
    )
    own_far[0] = kv_right[:QUART, :]
    own_far[1] = kv_out[:QUART, :]


def query_kernel(
    where, wire_right, wire_left, first_right, first_left, w_qkv_hbm, q_out, first_out, w_q, sem
):
    copy = pltpu.make_async_copy(w_qkv_hbm.at[1, :, pl.ds(0, HD)], w_q, sem)
    copy.start()
    lane = cell_of_window(iota((1, 2 * SIDE), 1))
    to_cell = one_hot(iota((OWN, 2 * SIDE), 0), lane)
    first = jnp.concatenate([first_right[...], first_left[...]], axis=0)
    first_out[...] = dot(to_cell, first).astype(jnp.bfloat16)
    copy.wait()
    q_out[:HALF, :] = dot(wire_right[...], w_q[...]).astype(jnp.bfloat16)
    q_out[HALF:, :] = dot(wire_left[...], w_q[...]).astype(jnp.bfloat16)


def lat_side_block(
    lat_side, where, q, kv_right, kv_left, from_right, from_left, direct, corner, corner_at, first, w_out, att, done
):
    position = where[0]
    edge = (position == 0) | (position == 3)
    row = iota((QWIN, 4 * KWIN), 0)
    lane = iota((QWIN, 4 * KWIN), 1)
    for side in range(2):
        own, across = ((kv_right, from_right), (kv_left, from_left))[side]
        for g in range(2):
            k = 2 * lat_side + g
            start = query_start(k)
            firsts = [UNIT * k, UNIT * k, QUART * side + UNIT * g, corner_at + QUART * side + UNIT * g]
            sources = [own, across, direct, corner]
            starts = [key_start(f, s.shape[0]) for f, s in zip(firsts, sources)]
            late = row >= UNIT * k - start + UNIT // 2
            valid = jnp.zeros((QWIN, 4 * KWIN), jnp.bool_)
            for i in range(4):
                at = lane - (i * KWIN + firsts[i] - starts[i])
                inside = (at >= 0) & (at < UNIT)
                if g == 1:
                    inside = inside & ((at >= UNIT // 2) == late)
                if i >= 2 and lat_side == 0:
                    inside = inside & jnp.logical_not(edge)
                valid = valid | inside
            bias = jnp.where(valid, 0.0, NEG).astype(jnp.float32)
            bias = jnp.concatenate([bias] * 4, axis=0)
            n = 2 * side + g
            for half in range(2):
                cols = slice(half * 256, half * 256 + 256)

                def window(base):
                    lanes = slice(base + half * 256, base + half * 256 + 256)
                    parts = [s[f : f + KWIN, lanes] for s, f in zip(sources, starts)]
                    return jnp.concatenate(parts, axis=0)

                att[n * QWIN : (n + 1) * QWIN, cols] = four_heads(
                    q[side * HALF + start : side * HALF + start + QWIN, cols], window(0), window(HD), bias
                )
    lane = cell_of_queries(iota((1, 4 * QWIN), 1), lat_side)
    placed = dot(one_hot(iota((HALF, 4 * QWIN), 0), lane), att[...]).astype(jnp.bfloat16)
    rows = pl.ds(pl.multiple_of(HALF * ((position & 1) ^ lat_side), 16), HALF)
    done[...] = first[rows, :].astype(jnp.float32) + dot(placed, w_out[1])


def near_kernel(
    where, q, kv_right, kv_left, from_right, from_left, lat, first, w_out, out, att, done
):
    lat_side_block(
        1, where, q, kv_right, kv_left, from_right, from_left, lat, lat, HALF, first, w_out, att, done
    )
    for i in range(CELLS // 2):
        out[i] = done[i * LEVELS : (i + 1) * LEVELS, :].astype(jnp.bfloat16)


def far_kernel(
    where, q, kv_right, kv_left, from_right, from_left, direct, corner, first, w_out, near, out,
    att, done, staged, sems,
):
    top = (where[0] & 1) * (CELLS // 2)
    copy = pltpu.make_async_copy(near, out.at[pl.ds(CELLS // 2 - top, CELLS // 2)], sems.at[0])
    copy.start()
    lat_side_block(
        0, where, q, kv_right, kv_left, from_right, from_left, direct, corner, 0, first, w_out, att, done
    )
    copies = [copy]
    step = CELLS // 6
    for j in range(3):
        for i in range(j * step, (j + 1) * step):
            staged[i] = done[i * LEVELS : (i + 1) * LEVELS, :].astype(jnp.bfloat16)
        span = pl.ds(top + j * step, step)
        copies.append(
            pltpu.make_async_copy(staged.at[pl.ds(j * step, step)], out.at[span], sems.at[1 + j])
        )
        copies[-1].start()
    for copy in copies:
        copy.wait()


def shape(*dims):
    return jax.ShapeDtypeStruct(dims, jnp.bfloat16)


def vmem(*dims):
    return pltpu.VMEM(dims, jnp.bfloat16)


def in_hbm(array):
    return pltpu.with_memory_space_constraint(array, pltpu.HBM)


ANY = pl.BlockSpec(memory_space=pl.ANY)
WHOLE = pl.BlockSpec(memory_space=pltpu.VMEM)
SCALARS = pl.BlockSpec(memory_space=pltpu.SMEM)


def call(kernel, ins, outs, scratch, flops, name, out_spec=WHOLE, limit=40):
    return pl.pallas_call(
        kernel,
        out_shape=outs,
        in_specs=[SCALARS, *ins],
        out_specs=jax.tree.map(lambda _: out_spec, outs),
        scratch_shapes=scratch,
        compiler_params=pltpu.CompilerParams(vmem_limit_bytes=limit * 1024 * 1024),
        cost_estimate=pl.CostEstimate(flops=flops, bytes_accessed=4_000_000, transcendentals=0),
        name=name,
    )


def right_side(where, cells, w_qkv, w_out):
    return call(
        right_kernel,
        [ANY] * 3,
        (
            shape(HALF, D), shape(HALF, D), shape(SIDE, D), shape(SIDE, D), shape(SIDE, D),
            shape(2 * SIDE, D), shape(D, HD), shape(HD, D), shape(2, D, HD),
        ),
        [
            vmem(CELLS, LEVELS, D), pltpu.VMEM((OWN, D), jnp.float32), vmem(SIDE, D), vmem(2 * SIDE, D),
            vmem(SIDE, HD), vmem(SIDE, D), vmem(2, D, HD), pltpu.SemaphoreType.DMA((7,)),
        ],
        2_000_000_000,
        "right_side",
    )(where, in_hbm(cells), in_hbm(w_qkv), in_hbm(w_out))


def left_side(*args):
    return call(
        left_kernel,
        [WHOLE] * 7,
        (shape(HALF, D), shape(HALF, D), shape(SIDE, D), shape(2, QUART, D)),
        [vmem(SIDE, HD), vmem(SIDE, D)],
        2_000_000_000,
        "left_side",
    )(*args)


def queries(where, wire_right, wire_left, first_right, first_left, w_qkv):
    return call(
        query_kernel,
        [WHOLE] * 4 + [ANY],
        (shape(OWN, HD), shape(OWN, D)),
        [vmem(D, HD), pltpu.SemaphoreType.DMA],
        1_000_000_000,
        "queries",
    )(where, wire_right, wire_left, first_right, first_left, in_hbm(w_qkv))


SIDE_SCRATCH = [vmem(4 * QWIN, HD), pltpu.VMEM((HALF, D), jnp.float32)]


def near_rows(*args):
    return call(
        near_kernel,
        [WHOLE] * 8,
        shape(CELLS // 2, LEVELS, D),
        SIDE_SCRATCH,
        2_000_000_000,
        "near_rows",
    )(*args)


def far_rows(*args):
    return call(
        far_kernel,
        [WHOLE] * 10,
        shape(CELLS, LEVELS, D),
        [*SIDE_SCRATCH, vmem(CELLS // 2, LEVELS, D), pltpu.SemaphoreType.DMA((4,))],
        2_000_000_000,
        "far_rows",
        out_spec=ANY,
    )(*args)


def per_device(tokens, w_qkv, w_out):
    lons, lats = lax.axis_size("lon"), lax.axis_size("lat")
    where = lax.axis_index("lat").astype(jnp.int32)[None]
    cells = tokens.transpose(1, 2, 0, 3).reshape(CELLS, LEVELS, D)

    kv_right, wire_right, first_right, *rest = right_side(where, cells, w_qkv, w_out)
    from_left = lax.ppermute(kv_right, "lon", [(i, (i + 1) % lons) for i in range(lons)])
    kv_left, wire_left, first_left, own_far = left_side(where, kv_right, *rest)
    far_pairs = [pair for i in range(1, lats - 1, 2) for pair in ((i, i + 1), (i + 1, i))]
    direct = lax.ppermute(own_far, "lat", far_pairs).reshape(HALF, D)
    from_right = lax.ppermute(kv_left, "lon", [(i, (i - 1) % lons) for i in range(lons)])

    received = [wire_left]
    for array in (from_left, direct, from_right):
        received = list(lax.optimization_barrier((*received, array)))
    wire_left, from_left, direct, from_right = received

    corner_far = jnp.concatenate([from_right[:QUART], from_left[:QUART]], axis=0)
    to_near = jnp.concatenate([p[QUART:] for p in (kv_right, kv_left, from_right, from_left)], axis=0)
    corner = lax.ppermute(corner_far, "lat", far_pairs)
    from_near = lax.ppermute(to_near, "lat", [(i, i ^ 1) for i in range(lats)])
    q, first = queries(where, wire_right, wire_left, first_right, first_left, w_qkv)
    shared = [where, q, kv_right, kv_left, from_right, from_left]
    near = near_rows(*shared, from_near, first, w_out)
    out = far_rows(*shared, direct, corner, first, w_out, near)
    return out.reshape(ROWS, COLS, LEVELS, D).transpose(2, 0, 1, 3)


def solution(mesh):
    return jax.shard_map(
        per_device,
        mesh=mesh,
        in_specs=(P(None, "lat", "lon", None), P(), P()),
        out_specs=P(None, "lat", "lon", None),
        check_vma=False,
    )
```

```python
import jax
import jax.numpy as jnp
from jax import lax
from jax.experimental import pallas as pl
from jax.experimental.pallas import tpu as pltpu
from jax.sharding import PartitionSpec as P

LEVELS, ROWS, COLS, D = 4, 6, 12, 1024
HD, HEAD = 512, 64
CELLS = ROWS * COLS
OWN = LEVELS * CELLS
HALF = OWN // 2
QUART = HALF // 2
UNIT = 36
WIN = 80
SIDE = 2 * WIN
QWIN = 48
KWIN = 64
NEG = -1e30
GROUP = 8


def at_least(index, *bounds):
    return sum(jnp.where(index >= bound, 1, 0) for bound in bounds)


def cell_of_window(index):
    side = at_least(index, SIDE)
    index = index - SIDE * side
    pair = at_least(index, WIN)
    index = index - WIN * pair
    valid = index < 2 * UNIT
    level = at_least(index, UNIT)
    index = index - UNIT * level
    row = at_least(index, *range(6, UNIT, 6))
    cell = (row * COLS + 6 * (1 - side) + index - 6 * row) * LEVELS + 2 * pair + level
    return jnp.where(valid, cell, -1)


def split_unit(index, group):
    lev = at_least(index, UNIT // 2)
    index = index - UNIT // 2 * lev
    row = at_least(index, 6, 12)
    return jnp.where(group == 0, 1 + lev, 3 - 3 * lev), row, index - 6 * row


def window_of_wire(index, lat_odd):
    k = at_least(index, UNIT, 2 * UNIT, 3 * UNIT)
    level, row, col = split_unit(index - UNIT * k, k & 1)
    row = row + 3 * ((k >> 1) ^ lat_odd)
    return WIN * (level >> 1) + UNIT * (level & 1) + 6 * row + col


def cell_of_queries(index, lat_side):
    n = at_least(index, QWIN, 2 * QWIN, 3 * QWIN)
    group, side = n & 1, n >> 1
    index = index - QWIN * n - 4 * (2 * lat_side + group)
    level, row, col = split_unit(index, group)
    cell = (row * COLS + 6 * (1 - side) + col) * LEVELS + level
    return jnp.where((index >= 0) & (index < UNIT), cell, -1)


def query_start(k):
    return k * UNIT // 16 * 16


def key_start(first, size):
    return min(first // 16 * 16, size - KWIN)


def iota(shape, axis):
    return lax.broadcasted_iota(jnp.int32, shape, axis)


def one_hot(rows, lanes):
    return jnp.where(rows == lanes, 1.0, 0.0).astype(jnp.bfloat16)


def layer_normed(values):
    centre = values - jnp.mean(values, axis=-1, keepdims=True)
    spread = jnp.mean(centre * centre, axis=-1, keepdims=True)
    return (centre * lax.rsqrt(spread + 1e-05)).astype(jnp.bfloat16)


def dot(a, b):
    return jnp.dot(a, b, preferred_element_type=jnp.float32)


def attention(calls):
    head_of = iota((1, 4 * HEAD), 1) // HEAD
    scores = []
    for queries, keys, _, bias in calls:
        queries = queries * jnp.bfloat16(0.125)
        spread = jnp.concatenate(
            [jnp.where(head_of == h, queries, jnp.bfloat16(0)) for h in range(4)], axis=0
        )
        product = lax.dot_general(
            spread, keys, (((1,), (1,)), ((), ())), preferred_element_type=jnp.float32
        )
        scores.append(product + bias)
    raised = [jnp.exp(s - jnp.max(s, axis=-1, keepdims=True)) for s in scores]
    mixed = [dot(r.astype(jnp.bfloat16), call[2]) for r, call in zip(raised, calls)]
    outs = []
    for r, m in zip(raised, mixed):
        m = m * (1.0 / jnp.sum(r, axis=-1, keepdims=True))
        rows = m.shape[0] // 4
        out = m[:rows]
        for h in range(1, 4):
            out = jnp.where(head_of == h, m[h * rows : (h + 1) * rows], out)
        outs.append(out.astype(jnp.bfloat16))
    return outs


def side_block(lat_odd, x, normed, kv, w_q, w_out, w_kv, first_out, wire_out, kv_out, att, scratch, ready):
    ready(0)
    queries = dot(normed, w_q[...]).astype(jnp.bfloat16)
    bias = jnp.where(iota((1, 2 * WIN), 1) % WIN < 2 * UNIT, 0.0, NEG).astype(jnp.float32)
    calls, places = [], []
    for pair in range(2):
        rows = slice(pair * WIN, (pair + 1) * WIN)
        far = slice(SIDE + pair * WIN, SIDE + (pair + 1) * WIN)
        for half in range(2):
            cols = slice(half * 256, half * 256 + 256)
            cols_v = slice(HD + half * 256, HD + half * 256 + 256)
            places.append((rows, cols))
            calls.append(
                (
                    queries[rows, cols],
                    jnp.concatenate([kv[rows, cols], kv[far, cols]], axis=0),
                    jnp.concatenate([kv[rows, cols_v], kv[far, cols_v]], axis=0),
                    bias,
                )
            )
    for (rows, cols), out in zip(places, attention(calls)):
        att[rows, cols] = out
    to_wire = one_hot(window_of_wire(iota((HALF, 1), 0), lat_odd), iota((HALF, SIDE), 1))
    ready(1)
    for pair in range(2):
        rows = slice(pair * WIN, (pair + 1) * WIN)
        first = (x[rows, :].astype(jnp.float32) + dot(att[rows, :], w_out[...])).astype(jnp.bfloat16)
        first_out[rows, :] = first
        scratch[rows, :] = layer_normed(first.astype(jnp.float32))
    wire = dot(to_wire, scratch[...]).astype(jnp.bfloat16)
    wire_out[...] = wire
    for i in range(2):
        ready(2 + i)
        kv_out[:, i * HD : (i + 1) * HD] = dot(wire, w_kv[i]).astype(jnp.bfloat16)


def right_kernel(
    where, x_hbm, w_qkv_hbm, w_out_hbm,
    kv_out, wire_out, first_out, x_left, normed_left, kv0, w_q, w_out, w_kv,
    x_in, x, x_right, normed, att, scratch, w_kv0, sems,
):
    def part(block, i):
        return w_qkv_hbm.at[block, :, pl.ds(i * HD, HD)]

    pairs = [
        (x_hbm, x_in), (part(0, 1), w_kv0.at[0]), (part(0, 2), w_kv0.at[1]), (part(0, 0), w_q),
        (w_out_hbm.at[0], w_out), (part(1, 1), w_kv.at[0]), (part(1, 2), w_kv.at[1]),
    ]
    copies = [pltpu.make_async_copy(src, dst, sems.at[i]) for i, (src, dst) in enumerate(pairs)]
    for copy in copies:
        copy.start()
    lat_odd = where[0] & 1
    rows = 2 * SIDE
    to_window = one_hot(cell_of_window(iota((rows, 1), 0)), iota((rows, OWN), 1))
    copies[0].wait()
    for i in range(CELLS):
        x[i * LEVELS : (i + 1) * LEVELS, :] = x_in[i].astype(jnp.float32)
    cells = x[...].astype(jnp.bfloat16)
    for i in range(4):
        span = slice(i * WIN, (i + 1) * WIN)
        ordered = dot(to_window[span], cells)
        target = x_right if i < 2 else x_left
        target[(i % 2) * WIN : (i % 2 + 1) * WIN, :] = ordered.astype(jnp.bfloat16)
        normed[span, :] = layer_normed(ordered)
    normed_left[...] = normed[SIDE:, :]
    for i in range(2):
        copies[1 + i].wait()
        kv0[:, i * HD : (i + 1) * HD] = dot(normed[...], w_kv0[i]).astype(jnp.bfloat16)
    side_block(
        lat_odd, x_right, normed[:SIDE, :], kv0, w_q, w_out, w_kv, first_out, wire_out, kv_out, att, scratch,
        lambda i: copies[3 + i].wait(),
    )


def left_kernel(
    where, kv_right, x, normed, kv0, w_q, w_out, w_kv, kv_out, wire_out, first_out, own_far, att, scratch
):
    side_block(
        where[0] & 1, x, normed[...], kv0, w_q, w_out, w_kv, first_out, wire_out, kv_out, att, scratch,
        lambda i: None,
    )
    own_far[0] = kv_right[:QUART, :]
    own_far[1] = kv_out[:QUART, :]


def query_kernel(
    where, wire_right, wire_left, first_right, first_left, w_qkv_hbm, q_out, first_out, w_q, sem
):
    copy = pltpu.make_async_copy(w_qkv_hbm.at[1, :, pl.ds(0, HD)], w_q, sem)
    copy.start()
    lane = cell_of_window(iota((1, 2 * SIDE), 1))
    to_cell = one_hot(iota((OWN, 2 * SIDE), 0), lane)
    first = jnp.concatenate([first_right[...], first_left[...]], axis=0)
    first_out[...] = dot(to_cell, first).astype(jnp.bfloat16)
    copy.wait()
    q_out[:HALF, :] = dot(wire_right[...], w_q[...]).astype(jnp.bfloat16)
    q_out[HALF:, :] = dot(wire_left[...], w_q[...]).astype(jnp.bfloat16)


def lat_side_block(
    lat_side, where, q, kv_right, kv_left, from_right, from_left, direct, corner, corner_at, first, w_out, att, done
):
    position = where[0]
    edge = (position == 0) | (position == 3)
    row = iota((QWIN, 4 * KWIN), 0)
    lane = iota((QWIN, 4 * KWIN), 1)
    calls, places = [], []
    for side in range(2):
        own, across = ((kv_right, from_right), (kv_left, from_left))[side]
        for g in range(2):
            k = 2 * lat_side + g
            start = query_start(k)
            firsts = [UNIT * k, UNIT * k, QUART * side + UNIT * g, corner_at + QUART * side + UNIT * g]
            sources = [own, across, direct, corner]
            starts = [key_start(f, s.shape[0]) for f, s in zip(firsts, sources)]
            late = row >= UNIT * k - start + UNIT // 2
            valid = jnp.zeros((QWIN, 4 * KWIN), jnp.bool_)
            for i in range(4):
                at = lane - (i * KWIN + firsts[i] - starts[i])
                inside = (at >= 0) & (at < UNIT)
                if g == 1:
                    inside = inside & ((at >= UNIT // 2) == late)
                if i >= 2 and lat_side == 0:
                    inside = inside & jnp.logical_not(edge)
                valid = valid | inside
            bias = jnp.where(valid, 0.0, NEG).astype(jnp.float32)
            bias = jnp.concatenate([bias] * 4, axis=0)
            n = 2 * side + g
            for half in range(2):
                cols = slice(half * 256, half * 256 + 256)

                def window(base):
                    lanes = slice(base + half * 256, base + half * 256 + 256)
                    parts = [s[f : f + KWIN, lanes] for s, f in zip(sources, starts)]
                    return jnp.concatenate(parts, axis=0)

                places.append((slice(n * QWIN, (n + 1) * QWIN), cols))
                rows = slice(side * HALF + start, side * HALF + start + QWIN)
                calls.append((q[rows, cols], window(0), window(HD), bias))
    for i in range(0, len(calls), GROUP):
        for (rows, cols), out in zip(places[i : i + GROUP], attention(calls[i : i + GROUP])):
            att[rows, cols] = out
    lane = cell_of_queries(iota((1, 4 * QWIN), 1), lat_side)
    placed = dot(one_hot(iota((HALF, 4 * QWIN), 0), lane), att[...]).astype(jnp.bfloat16)
    rows = pl.ds(pl.multiple_of(HALF * ((position & 1) ^ lat_side), 16), HALF)
    done[...] = first[rows, :].astype(jnp.float32) + dot(placed, w_out[1])


def near_kernel(
    where, q, kv_right, kv_left, from_right, from_left, lat, first, w_out, out, att, done
):
    lat_side_block(
        1, where, q, kv_right, kv_left, from_right, from_left, lat, lat, HALF, first, w_out, att, done
    )
    for i in range(CELLS // 2):
        out[i] = done[i * LEVELS : (i + 1) * LEVELS, :].astype(jnp.bfloat16)


def far_kernel(
    where, q, kv_right, kv_left, from_right, from_left, direct, corner, first, w_out, near, out,
    att, done, staged, sems,
):
    top = (where[0] & 1) * (CELLS // 2)
    copy = pltpu.make_async_copy(near, out.at[pl.ds(CELLS // 2 - top, CELLS // 2)], sems.at[0])
    copy.start()
    lat_side_block(
        0, where, q, kv_right, kv_left, from_right, from_left, direct, corner, 0, first, w_out, att, done
    )
    copies = [copy]
    step = CELLS // 6
    for j in range(3):
        for i in range(j * step, (j + 1) * step):
            staged[i] = done[i * LEVELS : (i + 1) * LEVELS, :].astype(jnp.bfloat16)
        span = pl.ds(top + j * step, step)
        copies.append(
            pltpu.make_async_copy(staged.at[pl.ds(j * step, step)], out.at[span], sems.at[1 + j])
        )
        copies[-1].start()
    for copy in copies:
        copy.wait()


def shape(*dims):
    return jax.ShapeDtypeStruct(dims, jnp.bfloat16)


def vmem(*dims):
    return pltpu.VMEM(dims, jnp.bfloat16)


def in_hbm(array):
    return pltpu.with_memory_space_constraint(array, pltpu.HBM)


ANY = pl.BlockSpec(memory_space=pl.ANY)
WHOLE = pl.BlockSpec(memory_space=pltpu.VMEM)
SCALARS = pl.BlockSpec(memory_space=pltpu.SMEM)


def call(kernel, ins, outs, scratch, flops, name, out_spec=WHOLE, limit=40):
    return pl.pallas_call(
        kernel,
        out_shape=outs,
        in_specs=[SCALARS, *ins],
        out_specs=jax.tree.map(lambda _: out_spec, outs),
        scratch_shapes=scratch,
        compiler_params=pltpu.CompilerParams(vmem_limit_bytes=limit * 1024 * 1024),
        cost_estimate=pl.CostEstimate(flops=flops, bytes_accessed=4_000_000, transcendentals=0),
        name=name,
    )


def right_side(where, cells, w_qkv, w_out):
    return call(
        right_kernel,
        [ANY] * 3,
        (
            shape(HALF, D), shape(HALF, D), shape(SIDE, D), shape(SIDE, D), shape(SIDE, D),
            shape(2 * SIDE, D), shape(D, HD), shape(HD, D), shape(2, D, HD),
        ),
        [
            vmem(CELLS, LEVELS, D), pltpu.VMEM((OWN, D), jnp.float32), vmem(SIDE, D), vmem(2 * SIDE, D),
            vmem(SIDE, HD), vmem(SIDE, D), vmem(2, D, HD), pltpu.SemaphoreType.DMA((7,)),
        ],
        2_000_000_000,
        "right_side",
    )(where, in_hbm(cells), in_hbm(w_qkv), in_hbm(w_out))


def left_side(*args):
    return call(
        left_kernel,
        [WHOLE] * 7,
        (shape(HALF, D), shape(HALF, D), shape(SIDE, D), shape(2, QUART, D)),
        [vmem(SIDE, HD), vmem(SIDE, D)],
        2_000_000_000,
        "left_side",
    )(*args)


def queries(where, wire_right, wire_left, first_right, first_left, w_qkv):
    return call(
        query_kernel,
        [WHOLE] * 4 + [ANY],
        (shape(OWN, HD), shape(OWN, D)),
        [vmem(D, HD), pltpu.SemaphoreType.DMA],
        1_000_000_000,
        "queries",
    )(where, wire_right, wire_left, first_right, first_left, in_hbm(w_qkv))


SIDE_SCRATCH = [vmem(4 * QWIN, HD), pltpu.VMEM((HALF, D), jnp.float32)]


def near_rows(*args):
    return call(
        near_kernel,
        [WHOLE] * 8,
        shape(CELLS // 2, LEVELS, D),
        SIDE_SCRATCH,
        2_000_000_000,
        "near_rows",
    )(*args)


def far_rows(*args):
    return call(
        far_kernel,
        [WHOLE] * 10,
        shape(CELLS, LEVELS, D),
        [*SIDE_SCRATCH, vmem(CELLS // 2, LEVELS, D), pltpu.SemaphoreType.DMA((4,))],
        2_000_000_000,
        "far_rows",
        out_spec=ANY,
    )(*args)


def per_device(tokens, w_qkv, w_out):
    lons, lats = lax.axis_size("lon"), lax.axis_size("lat")
    where = lax.axis_index("lat").astype(jnp.int32)[None]
    cells = tokens.transpose(1, 2, 0, 3).reshape(CELLS, LEVELS, D)

    kv_right, wire_right, first_right, *rest = right_side(where, cells, w_qkv, w_out)
    from_left = lax.ppermute(kv_right, "lon", [(i, (i + 1) % lons) for i in range(lons)])
    kv_left, wire_left, first_left, own_far = left_side(where, kv_right, *rest)
    far_pairs = [pair for i in range(1, lats - 1, 2) for pair in ((i, i + 1), (i + 1, i))]
    direct = lax.ppermute(own_far, "lat", far_pairs).reshape(HALF, D)
    from_right = lax.ppermute(kv_left, "lon", [(i, (i - 1) % lons) for i in range(lons)])

    received = [wire_left]
    for array in (from_left, direct, from_right):
        received = list(lax.optimization_barrier((*received, array)))
    wire_left, from_left, direct, from_right = received

    corner_far = jnp.concatenate([from_right[:QUART], from_left[:QUART]], axis=0)
    to_near = jnp.concatenate([p[QUART:] for p in (kv_right, kv_left, from_right, from_left)], axis=0)
    corner = lax.ppermute(corner_far, "lat", far_pairs)
    from_near = lax.ppermute(to_near, "lat", [(i, i ^ 1) for i in range(lats)])
    q, first = queries(where, wire_right, wire_left, first_right, first_left, w_qkv)
    shared = [where, q, kv_right, kv_left, from_right, from_left]
    near = near_rows(*shared, from_near, first, w_out)
    out = far_rows(*shared, direct, corner, first, w_out, near)
    return out.reshape(ROWS, COLS, LEVELS, D).transpose(2, 0, 1, 3)


def solution(mesh):
    return jax.shard_map(
        per_device,
        mesh=mesh,
        in_specs=(P(None, "lat", "lon", None), P(), P()),
        out_specs=P(None, "lat", "lon", None),
        check_vma=False,
    )
```

```python
import functools

import jax
import jax.numpy as jnp
from jax import lax
from jax.experimental import pallas as pl
from jax.experimental.pallas import tpu as pltpu
from jax.sharding import PartitionSpec as P

LEVELS, ROWS, COLS, D = 4, 6, 12, 1024
HD, HEAD = 512, 64
CELLS = ROWS * COLS
OWN = LEVELS * CELLS
HALF = OWN // 2
QUART = HALF // 2
UNIT = 36
WIN = 80
SIDE = 2 * WIN
QWIN = 48
KWIN = 64
NEG = -1e30
LOGS = 128


def at_least(index, *bounds):
    return sum(jnp.where(index >= bound, 1, 0) for bound in bounds)


def cell_of_window(index):
    side = at_least(index, SIDE)
    index = index - SIDE * side
    pair = at_least(index, WIN)
    index = index - WIN * pair
    valid = index < 2 * UNIT
    level = at_least(index, UNIT)
    index = index - UNIT * level
    row = at_least(index, *range(6, UNIT, 6))
    cell = (row * COLS + 6 * (1 - side) + index - 6 * row) * LEVELS + 2 * pair + level
    return jnp.where(valid, cell, -1)


def split_unit(index, group):
    lev = at_least(index, UNIT // 2)
    index = index - UNIT // 2 * lev
    row = at_least(index, 6, 12)
    return jnp.where(group == 0, 1 + lev, 3 - 3 * lev), row, index - 6 * row


def window_of_wire(index, lat_odd):
    k = at_least(index, UNIT, 2 * UNIT, 3 * UNIT)
    level, row, col = split_unit(index - UNIT * k, k & 1)
    row = row + 3 * ((k >> 1) ^ lat_odd)
    return WIN * (level >> 1) + UNIT * (level & 1) + 6 * row + col


def split_queries(index):
    n = at_least(index, QWIN, 2 * QWIN, 3 * QWIN)
    return n, index - (QWIN + 4) * n


def cell_of_unit(n, index):
    level, row, col = split_unit(index, n & 1)
    return (row * COLS + 6 * (1 - (n >> 1)) + col) * LEVELS + level


def query_start(k):
    return k * UNIT // 16 * 16


def key_start(first, size):
    return min(first // 16 * 16, size - KWIN)


def iota(shape, axis):
    return lax.broadcasted_iota(jnp.int32, shape, axis)


def one_hot(rows, lanes):
    return jnp.where(rows == lanes, 1.0, 0.0).astype(jnp.bfloat16)


def layer_normed(values):
    centre = values - jnp.mean(values, axis=-1, keepdims=True)
    spread = jnp.mean(centre * centre, axis=-1, keepdims=True)
    return (centre * lax.rsqrt(spread + 1e-05)).astype(jnp.bfloat16)


def dot(a, b):
    return jnp.dot(a, b, preferred_element_type=jnp.float32)


def spread_heads(queries):
    head_of = iota((1, 4 * HEAD), 1) // HEAD
    queries = queries * jnp.bfloat16(0.125)
    return jnp.concatenate(
        [jnp.where(head_of == h, queries, jnp.bfloat16(0)) for h in range(4)], axis=0
    )


def attention(calls, with_logs=False):
    head_of = iota((1, 4 * HEAD), 1) // HEAD
    scores = []
    for queries, keys, _, bias in calls:
        product = lax.dot_general(
            queries, keys, (((1,), (1,)), ((), ())), preferred_element_type=jnp.float32
        )
        scores.append(product + bias)
    highest = [jnp.max(s, axis=-1, keepdims=True) for s in scores]
    raised = [jnp.exp(s - h) for s, h in zip(scores, highest)]
    mixed = [dot(r.astype(jnp.bfloat16), call[2]) for r, call in zip(raised, calls)]
    outs, logs = [], []
    for r, m, high in zip(raised, mixed, highest):
        total = jnp.sum(r, axis=-1, keepdims=True)
        m = m * (1.0 / total)
        rows = m.shape[0] // 4
        out = m[:rows]
        for h in range(1, 4):
            out = jnp.where(head_of == h, m[h * rows : (h + 1) * rows], out)
        outs.append(out.astype(jnp.bfloat16))
        logs.append(high + jnp.log(total) if with_logs else None)
    return outs, logs


def side_block(lat_odd, x, normed, kv, w_q, w_out, w_kv, first_out, wire_out, kv_out, att, scratch, ready):
    ready(0)
    queries = dot(normed, w_q[...]).astype(jnp.bfloat16)
    bias = jnp.where(iota((1, 2 * WIN), 1) % WIN < 2 * UNIT, 0.0, NEG).astype(jnp.float32)
    calls, places = [], []
    for pair in range(2):
        rows = slice(pair * WIN, (pair + 1) * WIN)
        far = slice(SIDE + pair * WIN, SIDE + (pair + 1) * WIN)
        for half in range(2):
            cols = slice(half * 256, half * 256 + 256)
            cols_v = slice(HD + half * 256, HD + half * 256 + 256)
            places.append((rows, cols))
            calls.append(
                (
                    spread_heads(queries[rows, cols]),
                    jnp.concatenate([kv[rows, cols], kv[far, cols]], axis=0),
                    jnp.concatenate([kv[rows, cols_v], kv[far, cols_v]], axis=0),
                    bias,
                )
            )
    for (rows, cols), out in zip(places, attention(calls)[0]):
        att[rows, cols] = out
    to_wire = one_hot(window_of_wire(iota((HALF, 1), 0), lat_odd), iota((HALF, SIDE), 1))
    ready(1)
    for pair in range(2):
        rows = slice(pair * WIN, (pair + 1) * WIN)
        first = (x[rows, :].astype(jnp.float32) + dot(att[rows, :], w_out[...])).astype(jnp.bfloat16)
        first_out[rows, :] = first
        scratch[rows, :] = layer_normed(first.astype(jnp.float32))
    wire = dot(to_wire, scratch[...]).astype(jnp.bfloat16)
    wire_out[...] = wire
    for i in range(2):
        ready(2 + i)
        kv_out[:, i * HD : (i + 1) * HD] = dot(wire, w_kv[i]).astype(jnp.bfloat16)


def right_kernel(
    where, x_hbm, w_qkv_hbm, w_out_hbm,
    kv_out, wire_out, first_out, x_left, normed_left, kv0, w_q, w_out, w_kv, w_q1,
    x_in, x, x_right, normed, att, scratch, w_kv0, sems,
):
    def part(block, i):
        return w_qkv_hbm.at[block, :, pl.ds(i * HD, HD)]

    pairs = [
        (x_hbm, x_in), (part(0, 1), w_kv0.at[0]), (part(0, 2), w_kv0.at[1]), (part(0, 0), w_q),
        (w_out_hbm.at[0], w_out), (part(1, 1), w_kv.at[0]), (part(1, 2), w_kv.at[1]), (part(1, 0), w_q1),
    ]
    copies = [pltpu.make_async_copy(src, dst, sems.at[i]) for i, (src, dst) in enumerate(pairs)]
    for copy in copies:
        copy.start()
    lat_odd = where[0] & 1
    rows = 2 * SIDE
    to_window = one_hot(cell_of_window(iota((rows, 1), 0)), iota((rows, OWN), 1))
    copies[0].wait()
    for i in range(CELLS):
        x[i * LEVELS : (i + 1) * LEVELS, :] = x_in[i].astype(jnp.float32)
    cells = x[...].astype(jnp.bfloat16)
    for i in range(4):
        span = slice(i * WIN, (i + 1) * WIN)
        ordered = dot(to_window[span], cells)
        target = x_right if i < 2 else x_left
        target[(i % 2) * WIN : (i % 2 + 1) * WIN, :] = ordered.astype(jnp.bfloat16)
        normed[span, :] = layer_normed(ordered)
    normed_left[...] = normed[SIDE:, :]
    for i in range(2):
        copies[1 + i].wait()
        kv0[:, i * HD : (i + 1) * HD] = dot(normed[...], w_kv0[i]).astype(jnp.bfloat16)
    side_block(
        lat_odd, x_right, normed[:SIDE, :], kv0, w_q, w_out, w_kv, first_out, wire_out, kv_out, att, scratch,
        lambda i: copies[3 + i].wait(),
    )
    copies[7].wait()


def left_kernel(
    where, wire_right, x, normed, kv0, w_q, w_out, w_kv, w_q1,
    kv_out, wire_out, first_out, q_far, q_near, att, scratch,
):
    side_block(
        where[0] & 1, x, normed[...], kv0, w_q, w_out, w_kv, first_out, wire_out, kv_out, att, scratch,
        lambda i: None,
    )
    for side, wire in enumerate((wire_right, wire_out)):
        queries = dot(wire[...], w_q1[...])
        q_far[side] = queries[:QUART].astype(jnp.bfloat16)
        q_near[side] = queries[QUART:].astype(jnp.bfloat16)


def residual_kernel(where, first_right, first_left, first_out):
    to_cell = one_hot(iota((OWN, 2 * SIDE), 0), cell_of_window(iota((1, 2 * SIDE), 1)))
    first = jnp.concatenate([first_right[...], first_left[...]], axis=0)
    first_out[...] = dot(to_cell, first).astype(jnp.bfloat16)


def lat_side_calls(q, side_sources, spread=False):
    calls, places = [], []
    for n in range(4):
        group = n & 1
        sources = side_sources[n >> 1]
        lanes = KWIN * len(sources)
        row = iota((QWIN, lanes), 0)
        lane = iota((QWIN, lanes), 1)
        firsts = [first + UNIT * group for _, first in sources]
        starts = [key_start(f, s.shape[0]) for f, (s, _) in zip(firsts, sources)]
        late = row >= 4 * n + UNIT // 2
        valid = jnp.zeros((QWIN, lanes), jnp.bool_)
        for i in range(len(sources)):
            at = lane - (i * KWIN + firsts[i] - starts[i])
            inside = (at >= 0) & (at < UNIT)
            if group == 1:
                inside = inside & ((at >= UNIT // 2) == late)
            valid = valid | inside
        bias = jnp.where(valid, 0.0, NEG).astype(jnp.float32)
        bias = jnp.concatenate([bias] * 4, axis=0)
        start = query_start(n)
        for half in range(2):

            def window(base):
                lanes = slice(base + half * 256, base + half * 256 + 256)
                parts = [s[f : f + KWIN, lanes] for (s, _), f in zip(sources, starts)]
                return jnp.concatenate(parts, axis=0)

            cols = slice(half * 256, half * 256 + 256)
            places.append((slice(n * QWIN, (n + 1) * QWIN), cols))
            if spread:
                queries = q[2 * n + half]
            else:
                queries = spread_heads(q[start : start + QWIN, cols])
            calls.append((queries, window(0), window(HD), bias))
    return calls, places


def spread_kernel(where, q, out):
    for n in range(4):
        for half in range(2):
            rows = slice(query_start(n), query_start(n) + QWIN)
            out[2 * n + half] = spread_heads(q[rows, half * 256 : half * 256 + 256])


def partial_kernel(where, q, kv_right, kv_left, from_right, from_left, out, att, logs, spread):
    calls, places = lat_side_calls(q, [[(kv_right, 0), (from_right, 0)], [(kv_left, 0), (from_left, 0)]], spread)
    outs, sums = attention(calls, with_logs=True)
    head = iota((1, LOGS), 1) & 7
    for n in range(4):
        column = jnp.zeros((QWIN, LOGS), jnp.float32)
        for half in range(2):
            rows, cols = places[2 * n + half]
            att[rows, cols] = outs[2 * n + half]
            for h in range(4):
                part = sums[2 * n + half][h * QWIN : (h + 1) * QWIN]
                column = jnp.where(head == 4 * half + h, part, column)
        high = column.astype(jnp.bfloat16).astype(jnp.float32)
        rest = column - high
        middle = rest.astype(jnp.bfloat16).astype(jnp.float32)
        third = iota((1, LOGS), 1) >> 3
        parts = jnp.where(third == 0, high, jnp.where(third == 1, middle, rest - middle))
        logs[rows, :] = parts.astype(jnp.bfloat16)
    n, index = split_queries(iota((1, 4 * QWIN), 1))
    compact = jnp.where((index >= 0) & (index < UNIT), UNIT * n + index, -1)
    to_compact = one_hot(iota((HALF, 4 * QWIN), 0), compact)
    out[:, :HD] = dot(to_compact, att[...]).astype(jnp.bfloat16)
    out[:, HD:] = dot(to_compact, logs[...]).astype(jnp.bfloat16)


def near_kernel(where, q, kv_right, kv_left, from_right, from_left, lat, first, w_out, out, att, done):
    own = ((kv_right, from_right), (kv_left, from_left))
    sources = [
        [(own[s][0], QUART), (own[s][1], QUART), (lat, QUART * s), (lat, HALF + QUART * s)] for s in range(2)
    ]
    calls, places = lat_side_calls(q, sources)
    for (rows, cols), result in zip(places, attention(calls)[0]):
        att[rows, cols] = result
    n, index = split_queries(iota((1, 4 * QWIN), 1))
    cell = jnp.where((index >= 0) & (index < UNIT), cell_of_unit(n, index), -1)
    placed = dot(one_hot(iota((HALF, 4 * QWIN), 0), cell), att[...]).astype(jnp.bfloat16)
    rows = pl.ds(pl.multiple_of(HALF * (1 - (where[0] & 1)), 16), HALF)
    done[...] = first[rows, :].astype(jnp.float32) + dot(placed, w_out[1])
    for i in range(CELLS // 2):
        out[i] = done[i * LEVELS : (i + 1) * LEVELS, :].astype(jnp.bfloat16)


def merge_kernel(where, mine, theirs, first, w_out, near, out, done, staged, sems):
    position = where[0]
    far = position & 1
    copy = pltpu.make_async_copy(
        near, out.at[pl.ds((1 - far) * (CELLS // 2), CELLS // 2)], sems.at[0]
    )
    copy.start()
    log_row = iota((LOGS, HD), 0)
    head_of = iota((LOGS, HD), 1) // HEAD
    to_lanes = one_hot(jnp.where(log_row < 24, log_row & 7, -1), head_of)
    gap = dot(mine[:, HD:], to_lanes) - dot(theirs[:, HD:], to_lanes)
    alone = (position == 0) | (position == 3)
    gate = jnp.where(alone, 0.0, 1.0 / (1.0 + jnp.exp(gap)))
    own = mine[:, :HD].astype(jnp.float32)
    att = (own + (theirs[:, :HD].astype(jnp.float32) - own) * gate).astype(jnp.bfloat16)
    index = iota((1, HALF), 1)
    n = at_least(index, UNIT, 2 * UNIT, 3 * UNIT)
    to_cell = one_hot(iota((HALF, HALF), 0), cell_of_unit(n, index - UNIT * n))
    placed = dot(to_cell, att).astype(jnp.bfloat16)
    rows = pl.ds(pl.multiple_of(HALF * far, 16), HALF)
    done[...] = first[rows, :].astype(jnp.float32) + dot(placed, w_out[1])
    copies = [copy]
    step = CELLS // 6
    for j in range(3):
        for i in range(j * step, (j + 1) * step):
            staged[i] = done[i * LEVELS : (i + 1) * LEVELS, :].astype(jnp.bfloat16)
        span = pl.ds(far * (CELLS // 2) + j * step, step)
        copies.append(
            pltpu.make_async_copy(staged.at[pl.ds(j * step, step)], out.at[span], sems.at[1 + j])
        )
        copies[-1].start()
    for copy in copies:
        copy.wait()


def shape(*dims):
    return jax.ShapeDtypeStruct(dims, jnp.bfloat16)


def vmem(*dims):
    return pltpu.VMEM(dims, jnp.bfloat16)


def in_hbm(array):
    return pltpu.with_memory_space_constraint(array, pltpu.HBM)


ANY = pl.BlockSpec(memory_space=pl.ANY)
WHOLE = pl.BlockSpec(memory_space=pltpu.VMEM)
SCALARS = pl.BlockSpec(memory_space=pltpu.SMEM)


def call(kernel, ins, outs, scratch, flops, name, out_spec=WHOLE, limit=40):
    return pl.pallas_call(
        kernel,
        out_shape=outs,
        in_specs=[SCALARS, *ins],
        out_specs=jax.tree.map(lambda _: out_spec, outs),
        scratch_shapes=scratch,
        compiler_params=pltpu.CompilerParams(vmem_limit_bytes=limit * 1024 * 1024),
        cost_estimate=pl.CostEstimate(flops=flops, bytes_accessed=4_000_000, transcendentals=0),
        name=name,
    )


def right_side(where, cells, w_qkv, w_out):
    return call(
        right_kernel,
        [ANY] * 3,
        (
            shape(HALF, D), shape(HALF, D), shape(SIDE, D), shape(SIDE, D), shape(SIDE, D),
            shape(2 * SIDE, D), shape(D, HD), shape(HD, D), shape(2, D, HD), shape(D, HD),
        ),
        [
            vmem(CELLS, LEVELS, D), pltpu.VMEM((OWN, D), jnp.float32), vmem(SIDE, D), vmem(2 * SIDE, D),
            vmem(SIDE, HD), vmem(SIDE, D), vmem(2, D, HD), pltpu.SemaphoreType.DMA((8,)),
        ],
        2_000_000_000,
        "right_side",
    )(where, in_hbm(cells), in_hbm(w_qkv), in_hbm(w_out))


def left_side(*args):
    return call(
        left_kernel,
        [WHOLE] * 8,
        (shape(HALF, D), shape(HALF, D), shape(SIDE, D), shape(2, QUART, HD), shape(2, QUART, HD)),
        [vmem(SIDE, HD), vmem(SIDE, D)],
        2_000_000_000,
        "left_side",
    )(*args)


def residual(*args):
    return call(residual_kernel, [WHOLE] * 2, shape(OWN, D), [], 1_000_000_000, "residual")(*args)


def spread(*args):
    return call(
        spread_kernel, [WHOLE], shape(8, 4 * QWIN, 4 * HEAD), [], 2_500_000_000, "spread"
    )(*args)


def partial(name, is_spread, *args):
    return call(
        functools.partial(partial_kernel, spread=is_spread),
        [WHOLE] * 5,
        shape(HALF, HD + LOGS),
        [vmem(4 * QWIN, HD), vmem(4 * QWIN, LOGS)],
        1_000_000_000,
        name,
    )(*args)


DONE = pltpu.VMEM((HALF, D), jnp.float32)


def near_rows(*args):
    return call(
        near_kernel,
        [WHOLE] * 8,
        shape(CELLS // 2, LEVELS, D),
        [vmem(4 * QWIN, HD), DONE],
        2_000_000_000,
        "near_rows",
    )(*args)


def merge(*args):
    return call(
        merge_kernel,
        [WHOLE] * 5,
        shape(CELLS, LEVELS, D),
        [DONE, vmem(CELLS // 2, LEVELS, D), pltpu.SemaphoreType.DMA((4,))],
        2_000_000_000,
        "merge",
        out_spec=ANY,
    )(*args)


def per_device(tokens, w_qkv, w_out):
    lons, lats = lax.axis_size("lon"), lax.axis_size("lat")
    where = lax.axis_index("lat").astype(jnp.int32)[None]
    cells = tokens.transpose(1, 2, 0, 3).reshape(CELLS, LEVELS, D)

    kv_right, wire_right, first_right, *rest = right_side(where, cells, w_qkv, w_out)
    from_left = lax.ppermute(kv_right, "lon", [(i, (i + 1) % lons) for i in range(lons)])
    kv_left, _, first_left, q_far, q_near = left_side(where, wire_right, *rest)
    q_far, q_near = q_far.reshape(HALF, HD), q_near.reshape(HALF, HD)
    far_pairs = [pair for i in range(1, lats - 1, 2) for pair in ((i, i + 1), (i + 1, i))]
    foreign = lax.ppermute(q_far, "lat", far_pairs)
    from_right = lax.ppermute(kv_left, "lon", [(i, (i - 1) % lons) for i in range(lons)])

    foreign, from_left = lax.optimization_barrier((foreign, from_left))
    queries = spread(where, foreign)
    received = (first_left, queries, from_left, from_right)
    first_left, queries, from_left, from_right = lax.optimization_barrier(received)

    keys = [kv_right, kv_left, from_right, from_left]
    theirs = lax.ppermute(partial("foreign_rows", True, where, queries, *keys), "lat", far_pairs)
    to_near = jnp.concatenate([p[QUART:] for p in keys], axis=0)
    from_near = lax.ppermute(to_near, "lat", [(i, i ^ 1) for i in range(lats)])
    first = residual(where, first_right, first_left)
    mine = partial("own_rows", False, where, q_far, *keys)
    near = near_rows(where, q_near, *keys, from_near, first, w_out)
    out = merge(where, mine, theirs, first, w_out, near)
    return out.reshape(ROWS, COLS, LEVELS, D).transpose(2, 0, 1, 3)


def solution(mesh):
    return jax.shard_map(
        per_device,
        mesh=mesh,
        in_specs=(P(None, "lat", "lon", None), P(), P()),
        out_specs=P(None, "lat", "lon", None),
        check_vma=False,
    )
```

```python
import jax
import jax.numpy as jnp
from jax import lax
from jax.experimental import pallas as pl
from jax.experimental.pallas import tpu as pltpu
from jax.sharding import PartitionSpec as P

LEVELS, ROWS, COLS, D = 4, 6, 12, 1024
HD, HEAD = 512, 64
CELLS = ROWS * COLS
OWN = LEVELS * CELLS
HALF = OWN // 2
QUART = HALF // 2
UNIT = 36
WIN = 80
SIDE = 2 * WIN
QWIN = 48
KWIN = 64
NEG = -1e30
LOGS = 128
RUN = 8


def at_least(index, *bounds):
    return sum(jnp.where(index >= bound, 1, 0) for bound in bounds)


def cell_of_window(index):
    side = at_least(index, SIDE)
    index = index - SIDE * side
    pair = at_least(index, WIN)
    index = index - WIN * pair
    valid = index < 2 * UNIT
    level = at_least(index, UNIT)
    index = index - UNIT * level
    row = at_least(index, *range(6, UNIT, 6))
    cell = (row * COLS + 6 * (1 - side) + index - 6 * row) * LEVELS + 2 * pair + level
    return jnp.where(valid, cell, -1)


def split_unit(index, group):
    lev = at_least(index, UNIT // 2)
    index = index - UNIT // 2 * lev
    row = at_least(index, 6, 12)
    return jnp.where(group == 0, 1 + lev, 3 - 3 * lev), row, index - 6 * row


def window_of_wire(index, lat_odd):
    k = at_least(index, UNIT, 2 * UNIT, 3 * UNIT)
    level, row, col = split_unit(index - UNIT * k, k & 1)
    row = row + 3 * ((k >> 1) ^ lat_odd)
    return WIN * (level >> 1) + UNIT * (level & 1) + 6 * row + col


def split_queries(index):
    n = at_least(index, QWIN, 2 * QWIN, 3 * QWIN)
    return n, index - (QWIN + 4) * n


def cell_of_unit(n, index):
    level, row, col = split_unit(index, n & 1)
    return (row * COLS + 6 * (1 - (n >> 1)) + col) * LEVELS + level


def query_start(k):
    return k * UNIT // 16 * 16


def key_start(first, size):
    return min(first // 16 * 16, size - KWIN)


def iota(shape, axis):
    return lax.broadcasted_iota(jnp.int32, shape, axis)


def one_hot(rows, lanes):
    return jnp.where(rows == lanes, 1.0, 0.0).astype(jnp.bfloat16)


def layer_normed(values):
    centre = values - jnp.mean(values, axis=-1, keepdims=True)
    spread = jnp.mean(centre * centre, axis=-1, keepdims=True)
    return (centre * lax.rsqrt(spread + 1e-05)).astype(jnp.bfloat16)


def dot(a, b):
    return jnp.dot(a, b, preferred_element_type=jnp.float32)


def spread_heads(queries):
    head_of = iota((1, 4 * HEAD), 1) // HEAD
    queries = queries * jnp.bfloat16(0.125)
    return jnp.concatenate(
        [jnp.where(head_of == h, queries, jnp.bfloat16(0)) for h in range(4)], axis=0
    )


def attention(calls, with_logs=False):
    head_of = iota((1, 4 * HEAD), 1) // HEAD
    scores = []
    for queries, keys, _, bias in calls:
        product = lax.dot_general(
            queries, keys, (((1,), (1,)), ((), ())), preferred_element_type=jnp.float32
        )
        scores.append(product + bias)
    highest = [jnp.max(s, axis=-1, keepdims=True) for s in scores]
    raised = [jnp.exp(s - h) for s, h in zip(scores, highest)]
    mixed = [dot(r.astype(jnp.bfloat16), call[2]) for r, call in zip(raised, calls)]
    outs, logs = [], []
    for r, m, high in zip(raised, mixed, highest):
        total = jnp.sum(r, axis=-1, keepdims=True)
        m = m * (1.0 / total)
        rows = m.shape[0] // 4
        out = m[:rows]
        for h in range(1, 4):
            out = jnp.where(head_of == h, m[h * rows : (h + 1) * rows], out)
        outs.append(out.astype(jnp.bfloat16))
        logs.append(high + jnp.log(total) if with_logs else None)
    return outs, logs


def side_block(lat_odd, x, normed, kv, w_q, w_out, w_kv, first_out, wire_out, kv_out, att, scratch, ready):
    ready(0)
    queries = dot(normed, w_q[...]).astype(jnp.bfloat16)
    bias = jnp.where(iota((1, 2 * WIN), 1) % WIN < 2 * UNIT, 0.0, NEG).astype(jnp.float32)
    calls, places = [], []
    for pair in range(2):
        rows = slice(pair * WIN, (pair + 1) * WIN)
        far = slice(SIDE + pair * WIN, SIDE + (pair + 1) * WIN)
        for half in range(2):
            cols = slice(half * 256, half * 256 + 256)
            cols_v = slice(HD + half * 256, HD + half * 256 + 256)
            places.append((rows, cols))
            calls.append(
                (
                    spread_heads(queries[rows, cols]),
                    jnp.concatenate([kv[rows, cols], kv[far, cols]], axis=0),
                    jnp.concatenate([kv[rows, cols_v], kv[far, cols_v]], axis=0),
                    bias,
                )
            )
    for (rows, cols), out in zip(places, attention(calls)[0]):
        att[rows, cols] = out
    to_wire = one_hot(window_of_wire(iota((HALF, 1), 0), lat_odd), iota((HALF, SIDE), 1))
    ready(1)
    for pair in range(2):
        rows = slice(pair * WIN, (pair + 1) * WIN)
        first = (x[rows, :].astype(jnp.float32) + dot(att[rows, :], w_out[...])).astype(jnp.bfloat16)
        first_out[rows, :] = first
        scratch[rows, :] = layer_normed(first.astype(jnp.float32))
    wire = dot(to_wire, scratch[...]).astype(jnp.bfloat16)
    wire_out[...] = wire
    for i in range(2):
        ready(2 + i)
        kv_out[:, i * HD : (i + 1) * HD] = dot(wire, w_kv[i]).astype(jnp.bfloat16)


def right_kernel(
    where, x_hbm, w_qkv_hbm, w_out_hbm,
    kv_out, wire_out, first_out, x_left, normed_left, kv0, w_q, w_out, w_kv, w_q1, w_out1,
    x_in, x, x_right, normed, att, scratch, w_kv0, sems,
):
    def part(block, i):
        return w_qkv_hbm.at[block, :, pl.ds(i * HD, HD)]

    pairs = [
        (x_hbm, x_in), (part(0, 1), w_kv0.at[0]), (part(0, 2), w_kv0.at[1]), (part(0, 0), w_q),
        (w_out_hbm.at[0], w_out), (part(1, 1), w_kv.at[0]), (part(1, 2), w_kv.at[1]), (part(1, 0), w_q1),
        (w_out_hbm.at[1], w_out1),
    ]
    copies = [pltpu.make_async_copy(src, dst, sems.at[i]) for i, (src, dst) in enumerate(pairs)]
    for copy in copies:
        copy.start()
    lat_odd = where[0] & 1
    rows = 2 * SIDE
    to_window = one_hot(cell_of_window(iota((rows, 1), 0)), iota((rows, OWN), 1))
    copies[0].wait()
    for i in range(CELLS):
        x[i * LEVELS : (i + 1) * LEVELS, :] = x_in[i].astype(jnp.float32)
    cells = x[...].astype(jnp.bfloat16)
    for i in range(4):
        span = slice(i * WIN, (i + 1) * WIN)
        ordered = dot(to_window[span], cells)
        target = x_right if i < 2 else x_left
        target[(i % 2) * WIN : (i % 2 + 1) * WIN, :] = ordered.astype(jnp.bfloat16)
        normed[span, :] = layer_normed(ordered)
    normed_left[...] = normed[SIDE:, :]
    copies[1].wait()
    copies[2].wait()
    for i in range(2):
        kv0[:, i * HD : (i + 1) * HD] = dot(normed[...], w_kv0[i]).astype(jnp.bfloat16)
    side_block(
        lat_odd, x_right, normed[:SIDE, :], kv0, w_q, w_out, w_kv, first_out, wire_out, kv_out, att, scratch,
        lambda i: copies[3 + i].wait(),
    )
    copies[7].wait()
    copies[8].wait()


def left_kernel(
    where, wire_right, x, normed, kv0, w_q, w_out, w_kv, w_q1,
    kv_out, wire_out, first_out, q_far, att, scratch,
):
    side_block(
        where[0] & 1, x, normed[...], kv0, w_q, w_out, w_kv, first_out, wire_out, kv_out, att, scratch,
        lambda i: None,
    )
    for side, wire in enumerate((wire_right, wire_out)):
        q_far[side] = dot(wire[:QUART, :], w_q1[...]).astype(jnp.bfloat16)


def residual_kernel(where, first_right, first_left, wire_right, wire_left, w_q1, first_out, q_near):
    for side, wire in enumerate((wire_right, wire_left)):
        q_near[side] = dot(wire[...], w_q1[...])[QUART:].astype(jnp.bfloat16)
    to_cell = one_hot(iota((OWN, 2 * SIDE), 0), cell_of_window(iota((1, 2 * SIDE), 1)))
    first = jnp.concatenate([first_right[...], first_left[...]], axis=0)
    first_out[...] = dot(to_cell, first).astype(jnp.bfloat16)


def lat_side_calls(q, side_sources, ready=None):
    calls, places = [], []
    for n in range(4):
        group = n & 1
        sources = side_sources[n >> 1]
        lanes = KWIN * len(sources)
        row = iota((QWIN, lanes), 0)
        lane = iota((QWIN, lanes), 1)
        firsts = [first + UNIT * group for _, first in sources]
        starts = [key_start(f, s.shape[0]) for f, (s, _) in zip(firsts, sources)]
        late = row >= 4 * n + UNIT // 2
        valid = jnp.zeros((QWIN, lanes), jnp.bool_)
        for i in range(len(sources)):
            at = lane - (i * KWIN + firsts[i] - starts[i])
            inside = (at >= 0) & (at < UNIT)
            if group == 1:
                inside = inside & ((at >= UNIT // 2) == late)
            valid = valid | inside
        bias = jnp.where(valid, 0.0, NEG).astype(jnp.float32)
        bias = jnp.concatenate([bias] * 4, axis=0)
        start = query_start(n)
        for half in range(2):

            def window(base):
                lanes = slice(base + half * 256, base + half * 256 + 256)
                parts = [s[f : f + KWIN, lanes] for (s, _), f in zip(sources, starts)]
                return jnp.concatenate(parts, axis=0)

            cols = slice(half * 256, half * 256 + 256)
            places.append((slice(n * QWIN, (n + 1) * QWIN), cols))
            queries = spread_heads(q[start : start + QWIN, cols])
            if ready is not None:
                queries = jnp.where(ready[0], ready[1][2 * n + half], queries)
            calls.append((queries, window(0), window(HD), bias))
    return calls, places


def spread_kernel(where, q, out):
    for n in range(4):
        for half in range(2):
            rows = slice(query_start(n), query_start(n) + QWIN)
            out[2 * n + half] = spread_heads(q[rows, half * 256 : half * 256 + 256])


def partial_rows(q, kv_right, kv_left, from_right, from_left, out, att, logs, ready=None):
    calls, places = lat_side_calls(q, [[(kv_right, 0), (from_right, 0)], [(kv_left, 0), (from_left, 0)]], ready)
    outs, sums = attention(calls, with_logs=True)
    head = iota((1, LOGS), 1) & 7
    for n in range(4):
        column = jnp.zeros((QWIN, LOGS), jnp.float32)
        for half in range(2):
            rows, cols = places[2 * n + half]
            att[rows, cols] = outs[2 * n + half]
            for h in range(4):
                part = sums[2 * n + half][h * QWIN : (h + 1) * QWIN]
                column = jnp.where(head == 4 * half + h, part, column)
        high = column.astype(jnp.bfloat16).astype(jnp.float32)
        rest = column - high
        middle = rest.astype(jnp.bfloat16).astype(jnp.float32)
        third = iota((1, LOGS), 1) >> 3
        parts = jnp.where(third == 0, high, jnp.where(third == 1, middle, rest - middle))
        logs[rows, :] = parts.astype(jnp.bfloat16)
    n, index = split_queries(iota((1, 4 * QWIN), 1))
    compact = jnp.where((index >= 0) & (index < UNIT), UNIT * n + index, -1)
    to_compact = one_hot(iota((HALF, 4 * QWIN), 0), compact)
    out[:, :HD] = dot(to_compact, att[...]).astype(jnp.bfloat16)
    out[:, HD:] = dot(to_compact, logs[...]).astype(jnp.bfloat16)


def own_kernel(where, *refs):
    partial_rows(*refs)


def foreign_kernel(where, spread, *refs):
    partial_rows(*refs, ready=(where[1] == 1, spread))


def near_kernel(where, q, kv_right, kv_left, from_right, from_left, lat, first, w_out, out, att, done):
    own = ((kv_right, from_right), (kv_left, from_left))
    sources = [
        [(own[s][0], QUART), (own[s][1], QUART), (lat, QUART * s), (lat, HALF + QUART * s)] for s in range(2)
    ]
    calls, places = lat_side_calls(q, sources)
    for (rows, cols), result in zip(places, attention(calls)[0]):
        att[rows, cols] = result
    n, index = split_queries(iota((1, 4 * QWIN), 1))
    cell = jnp.where((index >= 0) & (index < UNIT), cell_of_unit(n, index), -1)
    placed = dot(one_hot(iota((HALF, 4 * QWIN), 0), cell), att[...]).astype(jnp.bfloat16)
    rows = pl.ds(pl.multiple_of(HALF * (1 - (where[0] & 1)), 16), HALF)
    done[...] = first[rows, :].astype(jnp.float32) + dot(placed, w_out[...])
    for i in range(CELLS // 2):
        out[i] = done[i * LEVELS : (i + 1) * LEVELS, :].astype(jnp.bfloat16)


def merge_kernel(where, mine, theirs, first, w_out, near, out, done, staged, sems):
    position = where[0]
    far = position & 1
    copy = pltpu.make_async_copy(
        near, out.at[pl.ds((1 - far) * (CELLS // 2), CELLS // 2)], sems.at[0]
    )
    copy.start()
    log_row = iota((LOGS, HD), 0)
    head_of = iota((LOGS, HD), 1) // HEAD
    to_lanes = one_hot(jnp.where(log_row < 24, log_row & 7, -1), head_of)
    gap = dot(mine[:, HD:], to_lanes) - dot(theirs[:, HD:], to_lanes)
    alone = (position == 0) | (position == 3)
    gate = jnp.where(alone, 0.0, 1.0 / (1.0 + jnp.exp(gap)))
    own = mine[:, :HD].astype(jnp.float32)
    att = (own + (theirs[:, :HD].astype(jnp.float32) - own) * gate).astype(jnp.bfloat16)
    index = iota((1, HALF), 1)
    n = at_least(index, UNIT, 2 * UNIT, 3 * UNIT)
    to_cell = one_hot(iota((HALF, HALF), 0), cell_of_unit(n, index - UNIT * n))
    placed = dot(to_cell, att).astype(jnp.bfloat16)
    rows = pl.ds(pl.multiple_of(HALF * far, 16), HALF)
    done[...] = first[rows, :].astype(jnp.float32) + dot(placed, w_out[...])
    copies = [copy]
    step = CELLS // 6
    for j in range(3):
        for i in range(j * step, (j + 1) * step):
            staged[i] = done[i * LEVELS : (i + 1) * LEVELS, :].astype(jnp.bfloat16)
        span = pl.ds(far * (CELLS // 2) + j * step, step)
        copies.append(
            pltpu.make_async_copy(staged.at[pl.ds(j * step, step)], out.at[span], sems.at[1 + j])
        )
        copies[-1].start()
    for copy in copies:
        copy.wait()


def shape(*dims):
    return jax.ShapeDtypeStruct(dims, jnp.bfloat16)


def vmem(*dims):
    return pltpu.VMEM(dims, jnp.bfloat16)


def in_hbm(array):
    return pltpu.with_memory_space_constraint(array, pltpu.HBM)


ANY = pl.BlockSpec(memory_space=pl.ANY)
WHOLE = pl.BlockSpec(memory_space=pltpu.VMEM)
SCALARS = pl.BlockSpec(memory_space=pltpu.SMEM)


def call(kernel, ins, outs, scratch, flops, name, out_spec=WHOLE, limit=40):
    return pl.pallas_call(
        kernel,
        out_shape=outs,
        in_specs=[SCALARS, *ins],
        out_specs=jax.tree.map(lambda _: out_spec, outs),
        scratch_shapes=scratch,
        compiler_params=pltpu.CompilerParams(vmem_limit_bytes=limit * 1024 * 1024),
        cost_estimate=pl.CostEstimate(flops=flops, bytes_accessed=4_000_000, transcendentals=0),
        name=name,
    )


def right_side(where, cells, w_qkv, w_out):
    return call(
        right_kernel,
        [ANY] * 3,
        (
            shape(HALF, D), shape(HALF, D), shape(SIDE, D), shape(SIDE, D), shape(SIDE, D),
            shape(2 * SIDE, D), shape(D, HD), shape(HD, D), shape(2, D, HD), shape(D, HD), shape(HD, D),
        ),
        [
            vmem(CELLS, LEVELS, D), pltpu.VMEM((OWN, D), jnp.float32), vmem(SIDE, D), vmem(2 * SIDE, D),
            vmem(SIDE, HD), vmem(SIDE, D), vmem(2, D, HD), pltpu.SemaphoreType.DMA((9,)),
        ],
        2_000_000_000,
        "right_side",
    )(where, in_hbm(cells), in_hbm(w_qkv), in_hbm(w_out))


def left_side(*args):
    return call(
        left_kernel,
        [WHOLE] * 8,
        (shape(HALF, D), shape(HALF, D), shape(SIDE, D), shape(2, QUART, HD)),
        [vmem(SIDE, HD), vmem(SIDE, D)],
        2_000_000_000,
        "left_side",
    )(*args)


def residual(*args):
    outs = (shape(OWN, D), shape(2, QUART, HD))
    return call(residual_kernel, [WHOLE] * 5, outs, [], 1_000_000_000, "residual")(*args)


def spread(*args):
    return call(
        spread_kernel, [WHOLE], shape(8, 4 * QWIN, 4 * HEAD), [], 2_500_000_000, "spread"
    )(*args)


def partial(name, kernel, *args):
    return call(
        kernel,
        [WHOLE] * (len(args) - 1),
        shape(HALF, HD + LOGS),
        [vmem(4 * QWIN, HD), vmem(4 * QWIN, LOGS)],
        1_000_000_000,
        name,
    )(*args)


DONE = pltpu.VMEM((HALF, D), jnp.float32)


def near_rows(*args):
    return call(
        near_kernel,
        [WHOLE] * 8,
        shape(CELLS // 2, LEVELS, D),
        [vmem(4 * QWIN, HD), DONE],
        2_000_000_000,
        "near_rows",
    )(*args)


def merge(*args):
    return call(
        merge_kernel,
        [WHOLE] * 5,
        shape(CELLS, LEVELS, D),
        [DONE, vmem(CELLS // 2, LEVELS, D), pltpu.SemaphoreType.DMA((4,))],
        2_000_000_000,
        "merge",
        out_spec=ANY,
    )(*args)


def per_device(tokens, w_qkv, w_out):
    lons, lats = lax.axis_size("lon"), lax.axis_size("lat")
    starts_run = (lax.axis_index("lon") % RUN == 0).astype(jnp.int32)
    where = jnp.stack([lax.axis_index("lat").astype(jnp.int32), starts_run])
    cells = tokens.transpose(1, 2, 0, 3).reshape(CELLS, LEVELS, D)

    kv_right, wire_right, first_right, *rest = right_side(where, cells, w_qkv, w_out)
    from_left = lax.ppermute(kv_right, "lon", [(i, (i + 1) % lons) for i in range(lons)])
    *rest, w_out1 = rest
    kv_left, wire_left, first_left, q_far = left_side(where, wire_right, *rest)
    w_q1, q_far = rest[-1], q_far.reshape(HALF, HD)
    partner = [i + 1 if i % 2 else i - 1 for i in range(lats)]
    partner[0], partner[-1] = 0, lats - 1
    first_pairs, other_pairs = [], []
    for i in range(lons):
        for j in range(lats):
            one, other = (first_pairs, other_pairs) if i % RUN == 0 else (other_pairs, first_pairs)
            one.append((i * lats + j, i * lats + partner[j]))
            other.append((i * lats + j, i * lats + j))
    foreign_first = lax.ppermute(q_far, ("lon", "lat"), first_pairs)
    from_right = lax.ppermute(kv_left, "lon", [(i, (i - 1) % lons) for i in range(lons)])
    foreign = lax.ppermute(q_far, ("lon", "lat"), other_pairs)

    foreign_first, from_left = lax.optimization_barrier((foreign_first, from_left))
    spread_first = spread(where, foreign_first)
    received = (first_left, spread_first, from_left, from_right, foreign)
    first_left, spread_first, from_left, from_right, foreign = lax.optimization_barrier(received)

    keys = [kv_right, kv_left, from_right, from_left]
    far_pairs = [pair for i in range(1, lats - 1, 2) for pair in ((i, i + 1), (i + 1, i))]
    theirs = partial("foreign_rows", foreign_kernel, where, spread_first, foreign, *keys)
    theirs = lax.ppermute(theirs, "lat", far_pairs)
    to_near = jnp.concatenate([p[QUART:] for p in keys], axis=0)
    from_near = lax.ppermute(to_near, "lat", [(i, i ^ 1) for i in range(lats)])
    mine = partial("own_rows", own_kernel, where, q_far, *keys)
    first, q_near = residual(where, first_right, first_left, wire_right, wire_left, w_q1)
    near = near_rows(where, q_near.reshape(HALF, HD), *keys, from_near, first, w_out1)
    out = merge(where, mine, theirs, first, w_out1, near)
    return out.reshape(ROWS, COLS, LEVELS, D).transpose(2, 0, 1, 3)


def solution(mesh):
    return jax.shard_map(
        per_device,
        mesh=mesh,
        in_specs=(P(None, "lat", "lon", None), P(), P()),
        out_specs=P(None, "lat", "lon", None),
        check_vma=False,
    )
```

```python
import jax
import jax.numpy as jnp
from jax import lax
from jax.experimental import pallas as pl
from jax.experimental.pallas import tpu as pltpu
from jax.sharding import PartitionSpec as P

LEVELS, ROWS, COLS, D = 4, 6, 12, 1024
HD, HEAD = 512, 64
CELLS = ROWS * COLS
OWN = LEVELS * CELLS
HALF = OWN // 2
QUART = HALF // 2
UNIT = 36
WIN = 80
SIDE = 2 * WIN
QWIN = 48
KWIN = 64
NEG = -1e30
LOGS = 128
RUN = 8


def at_least(index, *bounds):
    return sum(jnp.where(index >= bound, 1, 0) for bound in bounds)


def cell_of_window(index):
    side = at_least(index, SIDE)
    index = index - SIDE * side
    pair = at_least(index, WIN)
    index = index - WIN * pair
    valid = index < 2 * UNIT
    level = at_least(index, UNIT)
    index = index - UNIT * level
    row = at_least(index, *range(6, UNIT, 6))
    cell = (row * COLS + 6 * (1 - side) + index - 6 * row) * LEVELS + 2 * pair + level
    return jnp.where(valid, cell, -1)


def split_unit(index, group):
    lev = at_least(index, UNIT // 2)
    index = index - UNIT // 2 * lev
    row = at_least(index, 6, 12)
    return jnp.where(group == 0, 1 + lev, 3 - 3 * lev), row, index - 6 * row


def window_of_wire(index, lat_odd):
    k = at_least(index, UNIT, 2 * UNIT, 3 * UNIT)
    level, row, col = split_unit(index - UNIT * k, k & 1)
    row = row + 3 * ((k >> 1) ^ lat_odd)
    return WIN * (level >> 1) + UNIT * (level & 1) + 6 * row + col


def split_queries(index):
    n = at_least(index, QWIN, 2 * QWIN, 3 * QWIN)
    return n, index - (QWIN + 4) * n


def cell_of_unit(n, index):
    level, row, col = split_unit(index, n & 1)
    return (row * COLS + 6 * (1 - (n >> 1)) + col) * LEVELS + level


def query_start(k):
    return k * UNIT // 16 * 16


def key_start(first, size):
    return min(first // 16 * 16, size - KWIN)


def iota(shape, axis):
    return lax.broadcasted_iota(jnp.int32, shape, axis)


def one_hot(rows, lanes):
    return jnp.where(rows == lanes, 1.0, 0.0).astype(jnp.bfloat16)


def layer_normed(values):
    centre = values - jnp.mean(values, axis=-1, keepdims=True)
    spread = jnp.mean(centre * centre, axis=-1, keepdims=True)
    return (centre * lax.rsqrt(spread + 1e-05)).astype(jnp.bfloat16)


def dot(a, b):
    return jnp.dot(a, b, preferred_element_type=jnp.float32)


def spread_heads(queries):
    head_of = iota((1, 4 * HEAD), 1) // HEAD
    queries = queries * jnp.bfloat16(0.125)
    return jnp.concatenate(
        [jnp.where(head_of == h, queries, jnp.bfloat16(0)) for h in range(4)], axis=0
    )


def attention(calls, with_logs=False):
    head_of = iota((1, 4 * HEAD), 1) // HEAD
    scores = []
    for queries, keys, _, bias in calls:
        product = lax.dot_general(
            queries, keys, (((1,), (1,)), ((), ())), preferred_element_type=jnp.float32
        )
        scores.append(product + bias)
    highest = [jnp.max(s, axis=-1, keepdims=True) for s in scores]
    raised = [jnp.exp(s - h) for s, h in zip(scores, highest)]
    mixed = [dot(r.astype(jnp.bfloat16), call[2]) for r, call in zip(raised, calls)]
    outs, logs = [], []
    for r, m, high in zip(raised, mixed, highest):
        total = jnp.sum(r, axis=-1, keepdims=True)
        m = m * (1.0 / total)
        rows = m.shape[0] // 4
        out = m[:rows]
        for h in range(1, 4):
            out = jnp.where(head_of == h, m[h * rows : (h + 1) * rows], out)
        outs.append(out.astype(jnp.bfloat16))
        logs.append(high + jnp.log(total) if with_logs else None)
    return outs, logs


def side_block(lat_odd, x, normed, kv, w_q, w_out, w_kv, first_out, wire_out, kv_out, att, scratch, ready):
    ready(0)
    queries = dot(normed, w_q[...]).astype(jnp.bfloat16)
    bias = jnp.where(iota((1, 2 * WIN), 1) % WIN < 2 * UNIT, 0.0, NEG).astype(jnp.float32)
    calls, places = [], []
    for pair in range(2):
        rows = slice(pair * WIN, (pair + 1) * WIN)
        far = slice(SIDE + pair * WIN, SIDE + (pair + 1) * WIN)
        for half in range(2):
            cols = slice(half * 256, half * 256 + 256)
            cols_v = slice(HD + half * 256, HD + half * 256 + 256)
            places.append((rows, cols))
            calls.append(
                (
                    spread_heads(queries[rows, cols]),
                    jnp.concatenate([kv[rows, cols], kv[far, cols]], axis=0),
                    jnp.concatenate([kv[rows, cols_v], kv[far, cols_v]], axis=0),
                    bias,
                )
            )
    for (rows, cols), out in zip(places, attention(calls)[0]):
        att[rows, cols] = out
    to_wire = one_hot(window_of_wire(iota((HALF, 1), 0), lat_odd), iota((HALF, SIDE), 1))
    ready(1)
    for pair in range(2):
        rows = slice(pair * WIN, (pair + 1) * WIN)
        first = (x[rows, :].astype(jnp.float32) + dot(att[rows, :], w_out[...])).astype(jnp.bfloat16)
        first_out[rows, :] = first
        scratch[rows, :] = layer_normed(first.astype(jnp.float32))
    wire = dot(to_wire, scratch[...]).astype(jnp.bfloat16)
    wire_out[...] = wire
    for i in range(2):
        ready(2 + i)
        kv_out[:, i * HD : (i + 1) * HD] = dot(wire, w_kv[i]).astype(jnp.bfloat16)


def right_kernel(
    where, x_hbm, w_qkv_hbm, w_out_hbm,
    kv_out, wire_out, first_out, x_left, normed_left, kv0, w_q, w_out, w_kv, w_q1, w_out1,
    x_in, x, x_right, normed, att, scratch, w_kv0, sems,
):
    def part(block, i):
        return w_qkv_hbm.at[block, :, pl.ds(i * HD, HD)]

    pairs = [
        (x_hbm, x_in), (part(0, 1), w_kv0.at[0]), (part(0, 2), w_kv0.at[1]), (part(0, 0), w_q),
        (w_out_hbm.at[0], w_out), (part(1, 1), w_kv.at[0]), (part(1, 2), w_kv.at[1]), (part(1, 0), w_q1),
        (w_out_hbm.at[1], w_out1),
    ]
    copies = [pltpu.make_async_copy(src, dst, sems.at[i]) for i, (src, dst) in enumerate(pairs)]
    for copy in copies:
        copy.start()
    lat_odd = where[0] & 1
    rows = 2 * SIDE
    to_window = one_hot(cell_of_window(iota((rows, 1), 0)), iota((rows, OWN), 1))
    copies[0].wait()
    for i in range(CELLS):
        x[i * LEVELS : (i + 1) * LEVELS, :] = x_in[i].astype(jnp.float32)
    cells = x[...].astype(jnp.bfloat16)
    for i in range(4):
        span = slice(i * WIN, (i + 1) * WIN)
        ordered = dot(to_window[span], cells)
        target = x_right if i < 2 else x_left
        target[(i % 2) * WIN : (i % 2 + 1) * WIN, :] = ordered.astype(jnp.bfloat16)
        normed[span, :] = layer_normed(ordered)
    normed_left[...] = normed[SIDE:, :]
    copies[1].wait()
    copies[2].wait()
    for i in range(2):
        kv0[:, i * HD : (i + 1) * HD] = dot(normed[...], w_kv0[i]).astype(jnp.bfloat16)
    side_block(
        lat_odd, x_right, normed[:SIDE, :], kv0, w_q, w_out, w_kv, first_out, wire_out, kv_out, att, scratch,
        lambda i: copies[3 + i].wait(),
    )
    copies[7].wait()
    copies[8].wait()


def left_kernel(
    where, wire_right, x, normed, kv0, w_q, w_out, w_kv, w_q1,
    kv_out, wire_out, first_out, q_far, att, scratch,
):
    side_block(
        where[0] & 1, x, normed[...], kv0, w_q, w_out, w_kv, first_out, wire_out, kv_out, att, scratch,
        lambda i: None,
    )
    for side, wire in enumerate((wire_right, wire_out)):
        q_far[side] = dot(wire[:QUART, :], w_q1[...]).astype(jnp.bfloat16)


def residual_kernel(where, first_right, first_left, wire_right, wire_left, w_q1, first_out, q_near):
    for side, wire in enumerate((wire_right, wire_left)):
        q_near[side] = dot(wire[...], w_q1[...])[QUART:].astype(jnp.bfloat16)
    to_cell = one_hot(iota((OWN, 2 * SIDE), 0), cell_of_window(iota((1, 2 * SIDE), 1)))
    first = jnp.concatenate([first_right[...], first_left[...]], axis=0)
    first_out[...] = dot(to_cell, first).astype(jnp.bfloat16)


def lat_side_calls(q, side_sources, ready=None):
    calls, places = [], []
    for n in range(4):
        group = n & 1
        sources = side_sources[n >> 1]
        lanes = KWIN * len(sources)
        row = iota((QWIN, lanes), 0)
        lane = iota((QWIN, lanes), 1)
        firsts = [first + UNIT * group for _, first in sources]
        starts = [key_start(f, s.shape[0]) for f, (s, _) in zip(firsts, sources)]
        late = row >= 4 * n + UNIT // 2
        valid = jnp.zeros((QWIN, lanes), jnp.bool_)
        for i in range(len(sources)):
            at = lane - (i * KWIN + firsts[i] - starts[i])
            inside = (at >= 0) & (at < UNIT)
            if group == 1:
                inside = inside & ((at >= UNIT // 2) == late)
            valid = valid | inside
        bias = jnp.where(valid, 0.0, NEG).astype(jnp.float32)
        bias = jnp.concatenate([bias] * 4, axis=0)
        start = query_start(n)
        for half in range(2):

            def window(base):
                lanes = slice(base + half * 256, base + half * 256 + 256)
                parts = [s[f : f + KWIN, lanes] for (s, _), f in zip(sources, starts)]
                return jnp.concatenate(parts, axis=0)

            cols = slice(half * 256, half * 256 + 256)
            places.append((slice(n * QWIN, (n + 1) * QWIN), cols))
            queries = spread_heads(q[start : start + QWIN, cols])
            if ready is not None:
                queries = jnp.where(ready[0], ready[1][2 * n + half], queries)
            calls.append((queries, window(0), window(HD), bias))
    return calls, places


def spread_kernel(where, q, out):
    for n in range(4):
        for half in range(2):
            rows = slice(query_start(n), query_start(n) + QWIN)
            out[2 * n + half] = spread_heads(q[rows, half * 256 : half * 256 + 256])


def partial_rows(q, kv_right, kv_left, from_right, from_left, out, att, logs, ready=None):
    calls, places = lat_side_calls(q, [[(kv_right, 0), (from_right, 0)], [(kv_left, 0), (from_left, 0)]], ready)
    outs, sums = attention(calls, with_logs=True)
    head = iota((1, LOGS), 1) & 7
    for n in range(4):
        column = jnp.zeros((QWIN, LOGS), jnp.float32)
        for half in range(2):
            rows, cols = places[2 * n + half]
            att[rows, cols] = outs[2 * n + half]
            for h in range(4):
                part = sums[2 * n + half][h * QWIN : (h + 1) * QWIN]
                column = jnp.where(head == 4 * half + h, part, column)
        high = column.astype(jnp.bfloat16).astype(jnp.float32)
        rest = column - high
        middle = rest.astype(jnp.bfloat16).astype(jnp.float32)
        third = iota((1, LOGS), 1) >> 3
        parts = jnp.where(third == 0, high, jnp.where(third == 1, middle, rest - middle))
        logs[rows, :] = parts.astype(jnp.bfloat16)
    n, index = split_queries(iota((1, 4 * QWIN), 1))
    compact = jnp.where((index >= 0) & (index < UNIT), UNIT * n + index, -1)
    to_compact = one_hot(iota((HALF, 4 * QWIN), 0), compact)
    out[:, :HD] = dot(to_compact, att[...]).astype(jnp.bfloat16)
    out[:, HD:] = dot(to_compact, logs[...]).astype(jnp.bfloat16)


def own_kernel(where, *refs):
    partial_rows(*refs)


def foreign_kernel(where, spread, *refs):
    partial_rows(*refs, ready=(where[0] >= 4, spread))


def near_kernel(where, q, kv_right, kv_left, from_right, from_left, lat, first, w_out, out, att, done):
    own = ((kv_right, from_right), (kv_left, from_left))
    sources = [
        [(own[s][0], QUART), (own[s][1], QUART), (lat, QUART * s), (lat, HALF + QUART * s)] for s in range(2)
    ]
    calls, places = lat_side_calls(q, sources)
    for (rows, cols), result in zip(places, attention(calls)[0]):
        att[rows, cols] = result
    n, index = split_queries(iota((1, 4 * QWIN), 1))
    cell = jnp.where((index >= 0) & (index < UNIT), cell_of_unit(n, index), -1)
    placed = dot(one_hot(iota((HALF, 4 * QWIN), 0), cell), att[...]).astype(jnp.bfloat16)
    rows = pl.ds(pl.multiple_of(HALF * (1 - (where[0] & 1)), 16), HALF)
    done[...] = first[rows, :].astype(jnp.float32) + dot(placed, w_out[...])
    for i in range(CELLS // 2):
        out[i] = done[i * LEVELS : (i + 1) * LEVELS, :].astype(jnp.bfloat16)


def merge_kernel(where, mine, theirs, first, w_out, near, out, done, staged, sems):
    position = where[0] & 3
    far = position & 1
    copy = pltpu.make_async_copy(
        near, out.at[pl.ds((1 - far) * (CELLS // 2), CELLS // 2)], sems.at[0]
    )
    copy.start()
    log_row = iota((LOGS, HD), 0)
    head_of = iota((LOGS, HD), 1) // HEAD
    to_lanes = one_hot(jnp.where(log_row < 24, log_row & 7, -1), head_of)
    gap = dot(mine[:, HD:], to_lanes) - dot(theirs[:, HD:], to_lanes)
    alone = (position == 0) | (position == 3)
    gate = jnp.where(alone, 0.0, 1.0 / (1.0 + jnp.exp(gap)))
    own = mine[:, :HD].astype(jnp.float32)
    att = (own + (theirs[:, :HD].astype(jnp.float32) - own) * gate).astype(jnp.bfloat16)
    index = iota((1, HALF), 1)
    n = at_least(index, UNIT, 2 * UNIT, 3 * UNIT)
    to_cell = one_hot(iota((HALF, HALF), 0), cell_of_unit(n, index - UNIT * n))
    placed = dot(to_cell, att).astype(jnp.bfloat16)
    rows = pl.ds(pl.multiple_of(HALF * far, 16), HALF)
    done[...] = first[rows, :].astype(jnp.float32) + dot(placed, w_out[...])
    copies = [copy]
    step = CELLS // 6
    for j in range(3):
        for i in range(j * step, (j + 1) * step):
            staged[i] = done[i * LEVELS : (i + 1) * LEVELS, :].astype(jnp.bfloat16)
        span = pl.ds(far * (CELLS // 2) + j * step, step)
        copies.append(
            pltpu.make_async_copy(staged.at[pl.ds(j * step, step)], out.at[span], sems.at[1 + j])
        )
        copies[-1].start()
    for copy in copies:
        copy.wait()


def shape(*dims):
    return jax.ShapeDtypeStruct(dims, jnp.bfloat16)


def vmem(*dims):
    return pltpu.VMEM(dims, jnp.bfloat16)


def in_hbm(array):
    return pltpu.with_memory_space_constraint(array, pltpu.HBM)


ANY = pl.BlockSpec(memory_space=pl.ANY)
WHOLE = pl.BlockSpec(memory_space=pltpu.VMEM)
SCALARS = pl.BlockSpec(memory_space=pltpu.SMEM)


def call(kernel, ins, outs, scratch, flops, name, out_spec=WHOLE, limit=40):
    return pl.pallas_call(
        kernel,
        out_shape=outs,
        in_specs=[SCALARS, *ins],
        out_specs=jax.tree.map(lambda _: out_spec, outs),
        scratch_shapes=scratch,
        compiler_params=pltpu.CompilerParams(vmem_limit_bytes=limit * 1024 * 1024),
        cost_estimate=pl.CostEstimate(flops=flops, bytes_accessed=4_000_000, transcendentals=0),
        name=name,
    )


def right_side(where, cells, w_qkv, w_out):
    return call(
        right_kernel,
        [ANY] * 3,
        (
            shape(HALF, D), shape(HALF, D), shape(SIDE, D), shape(SIDE, D), shape(SIDE, D),
            shape(2 * SIDE, D), shape(D, HD), shape(HD, D), shape(2, D, HD), shape(D, HD), shape(HD, D),
        ),
        [
            vmem(CELLS, LEVELS, D), pltpu.VMEM((OWN, D), jnp.float32), vmem(SIDE, D), vmem(2 * SIDE, D),
            vmem(SIDE, HD), vmem(SIDE, D), vmem(2, D, HD), pltpu.SemaphoreType.DMA((9,)),
        ],
        2_000_000_000,
        "right_side",
    )(where, in_hbm(cells), in_hbm(w_qkv), in_hbm(w_out))


def left_side(*args):
    return call(
        left_kernel,
        [WHOLE] * 8,
        (shape(HALF, D), shape(HALF, D), shape(SIDE, D), shape(2, QUART, HD)),
        [vmem(SIDE, HD), vmem(SIDE, D)],
        2_000_000_000,
        "left_side",
    )(*args)


def residual(*args):
    outs = (shape(OWN, D), shape(2, QUART, HD))
    return call(residual_kernel, [WHOLE] * 5, outs, [], 1_000_000_000, "residual")(*args)


def spread(*args):
    return call(
        spread_kernel, [WHOLE], shape(8, 4 * QWIN, 4 * HEAD), [], 2_500_000_000, "spread"
    )(*args)


def partial(name, kernel, *args):
    return call(
        kernel,
        [WHOLE] * (len(args) - 1),
        shape(HALF, HD + LOGS),
        [vmem(4 * QWIN, HD), vmem(4 * QWIN, LOGS)],
        1_000_000_000,
        name,
    )(*args)


DONE = pltpu.VMEM((HALF, D), jnp.float32)


def near_rows(*args):
    return call(
        near_kernel,
        [WHOLE] * 8,
        shape(CELLS // 2, LEVELS, D),
        [vmem(4 * QWIN, HD), DONE],
        2_000_000_000,
        "near_rows",
    )(*args)


def merge(*args):
    return call(
        merge_kernel,
        [WHOLE] * 5,
        shape(CELLS, LEVELS, D),
        [DONE, vmem(CELLS // 2, LEVELS, D), pltpu.SemaphoreType.DMA((4,))],
        2_000_000_000,
        "merge",
        out_spec=ANY,
    )(*args)


def per_device(tokens, w_qkv, w_out):
    lons, lats = lax.axis_size("lon"), lax.axis_size("lat")
    starts_run = (lax.axis_index("lon") % RUN == 0).astype(jnp.int32)
    where = (lax.axis_index("lat").astype(jnp.int32) + 4 * starts_run)[None]
    cells = tokens.transpose(1, 2, 0, 3).reshape(CELLS, LEVELS, D)

    kv_right, wire_right, first_right, *rest = right_side(where, cells, w_qkv, w_out)
    from_left = lax.ppermute(kv_right, "lon", [(i, (i + 1) % lons) for i in range(lons)])
    *rest, w_out1 = rest
    kv_left, wire_left, first_left, q_far = left_side(where, wire_right, *rest)
    w_q1, q_far = rest[-1], q_far.reshape(HALF, HD)
    partner = [i + 1 if i % 2 else i - 1 for i in range(lats)]
    partner[0], partner[-1] = 0, lats - 1
    first_pairs, other_pairs = [], []
    for i in range(lons):
        for j in range(lats):
            one, other = (first_pairs, other_pairs) if i % RUN == 0 else (other_pairs, first_pairs)
            one.append((i * lats + j, i * lats + partner[j]))
            other.append((i * lats + j, i * lats + j))
    foreign_first = lax.ppermute(q_far, ("lon", "lat"), first_pairs)
    from_right = lax.ppermute(kv_left, "lon", [(i, (i - 1) % lons) for i in range(lons)])
    foreign = lax.ppermute(q_far, ("lon", "lat"), other_pairs)

    foreign_first, from_left = lax.optimization_barrier((foreign_first, from_left))
    spread_first = spread(where, foreign_first)
    received = (first_left, spread_first, from_left, from_right, foreign)
    first_left, spread_first, from_left, from_right, foreign = lax.optimization_barrier(received)

    keys = [kv_right, kv_left, from_right, from_left]
    far_pairs = [pair for i in range(1, lats - 1, 2) for pair in ((i, i + 1), (i + 1, i))]
    theirs = partial("foreign_rows", foreign_kernel, where, spread_first, foreign, *keys)
    theirs = lax.ppermute(theirs, "lat", far_pairs)
    to_near = jnp.concatenate([p[QUART:] for p in keys], axis=0)
    from_near = lax.ppermute(to_near, "lat", [(i, i ^ 1) for i in range(lats)])
    mine = partial("own_rows", own_kernel, where, q_far, *keys)
    first, q_near = residual(where, first_right, first_left, wire_right, wire_left, w_q1)
    near = near_rows(where, q_near.reshape(HALF, HD), *keys, from_near, first, w_out1)
    out = merge(where, mine, theirs, first, w_out1, near)
    return out.reshape(ROWS, COLS, LEVELS, D).transpose(2, 0, 1, 3)


def solution(mesh):
    return jax.shard_map(
        per_device,
        mesh=mesh,
        in_specs=(P(None, "lat", "lon", None), P(), P()),
        out_specs=P(None, "lat", "lon", None),
        check_vma=False,
    )
```

```python
import jax
import jax.numpy as jnp
from jax import lax
from jax.experimental import pallas as pl
from jax.experimental.pallas import tpu as pltpu
from jax.sharding import PartitionSpec as P

LEVELS, ROWS, COLS, D = 4, 6, 12, 1024
HD, HEAD = 512, 64
CELLS = ROWS * COLS
OWN = LEVELS * CELLS
HALF = OWN // 2
QUART = HALF // 2
UNIT = 36
WIN = 80
SIDE = 2 * WIN
QWIN = 48
KWIN = 64
NEG = -1e30
LOGS = 128
RUN = 8


def at_least(index, *bounds):
    return sum(jnp.where(index >= bound, 1, 0) for bound in bounds)


def cell_of_window(index):
    side = at_least(index, SIDE)
    index = index - SIDE * side
    pair = at_least(index, WIN)
    index = index - WIN * pair
    valid = index < 2 * UNIT
    level = at_least(index, UNIT)
    index = index - UNIT * level
    row = at_least(index, *range(6, UNIT, 6))
    cell = (row * COLS + 6 * (1 - side) + index - 6 * row) * LEVELS + 2 * pair + level
    return jnp.where(valid, cell, -1)


def split_unit(index, group):
    lev = at_least(index, UNIT // 2)
    index = index - UNIT // 2 * lev
    row = at_least(index, 6, 12)
    return jnp.where(group == 0, 1 + lev, 3 - 3 * lev), row, index - 6 * row


def window_of_wire(index, lat_odd):
    k = at_least(index, UNIT, 2 * UNIT, 3 * UNIT)
    level, row, col = split_unit(index - UNIT * k, k & 1)
    row = row + 3 * ((k >> 1) ^ lat_odd)
    return WIN * (level >> 1) + UNIT * (level & 1) + 6 * row + col


def split_queries(index):
    n = at_least(index, QWIN, 2 * QWIN, 3 * QWIN)
    return n, index - (QWIN + 4) * n


def cell_of_unit(n, index):
    level, row, col = split_unit(index, n & 1)
    return (row * COLS + 6 * (1 - (n >> 1)) + col) * LEVELS + level


def query_start(k):
    return k * UNIT // 16 * 16


def key_start(first, size):
    return min(first // 16 * 16, size - KWIN)


def iota(shape, axis):
    return lax.broadcasted_iota(jnp.int32, shape, axis)


def one_hot(rows, lanes):
    return jnp.where(rows == lanes, 1.0, 0.0).astype(jnp.bfloat16)


def layer_normed(values):
    centre = values - jnp.mean(values, axis=-1, keepdims=True)
    spread = jnp.mean(centre * centre, axis=-1, keepdims=True)
    return (centre * lax.rsqrt(spread + 1e-05)).astype(jnp.bfloat16)


def dot(a, b):
    return jnp.dot(a, b, preferred_element_type=jnp.float32)


def spread_heads(queries):
    head_of = iota((1, 4 * HEAD), 1) // HEAD
    queries = queries * jnp.bfloat16(0.125)
    return jnp.concatenate(
        [jnp.where(head_of == h, queries, jnp.bfloat16(0)) for h in range(4)], axis=0
    )


def attention(calls, with_logs=False):
    head_of = iota((1, 4 * HEAD), 1) // HEAD
    scores = []
    for queries, keys, _, bias in calls:
        product = lax.dot_general(
            queries, keys, (((1,), (1,)), ((), ())), preferred_element_type=jnp.float32
        )
        scores.append(product + bias)
    highest = [jnp.max(s, axis=-1, keepdims=True) for s in scores]
    raised = [jnp.exp(s - h) for s, h in zip(scores, highest)]
    mixed = [dot(r.astype(jnp.bfloat16), call[2]) for r, call in zip(raised, calls)]
    outs, logs = [], []
    for r, m, high in zip(raised, mixed, highest):
        total = jnp.sum(r, axis=-1, keepdims=True)
        m = m * (1.0 / total)
        rows = m.shape[0] // 4
        out = m[:rows]
        for h in range(1, 4):
            out = jnp.where(head_of == h, m[h * rows : (h + 1) * rows], out)
        outs.append(out.astype(jnp.bfloat16))
        logs.append(high + jnp.log(total) if with_logs else None)
    return outs, logs


def side_block(lat_odd, x, normed, kv, w_q, w_out, w_kv, first_out, wire_out, kv_out, att, scratch, ready):
    for i in range(4):
        ready(i)
    queries = dot(normed, w_q[...]).astype(jnp.bfloat16)
    bias = jnp.where(iota((1, 2 * WIN), 1) % WIN < 2 * UNIT, 0.0, NEG).astype(jnp.float32)
    calls, places = [], []
    for pair in range(2):
        rows = slice(pair * WIN, (pair + 1) * WIN)
        far = slice(SIDE + pair * WIN, SIDE + (pair + 1) * WIN)
        for half in range(2):
            cols = slice(half * 256, half * 256 + 256)
            cols_v = slice(HD + half * 256, HD + half * 256 + 256)
            places.append((rows, cols))
            calls.append(
                (
                    spread_heads(queries[rows, cols]),
                    jnp.concatenate([kv[rows, cols], kv[far, cols]], axis=0),
                    jnp.concatenate([kv[rows, cols_v], kv[far, cols_v]], axis=0),
                    bias,
                )
            )
    for (rows, cols), out in zip(places, attention(calls)[0]):
        att[rows, cols] = out
    to_wire = one_hot(window_of_wire(iota((HALF, 1), 0), lat_odd), iota((HALF, SIDE), 1))
    first = (x[...].astype(jnp.float32) + dot(att[...], w_out[...])).astype(jnp.bfloat16)
    first_out[...] = first
    scratch[...] = layer_normed(first.astype(jnp.float32))
    wire = dot(to_wire, scratch[...]).astype(jnp.bfloat16)
    wire_out[...] = wire
    for i in range(2):
        kv_out[:, i * HD : (i + 1) * HD] = dot(wire, w_kv[i]).astype(jnp.bfloat16)


def right_kernel(
    where, x_hbm, w_qkv_hbm, w_out_hbm,
    kv_out, wire_out, first_out, x_left, normed_left, kv0, w_q, w_out, w_kv, w_q1, w_out1,
    x_in, x, x_right, normed, att, scratch, w_kv0, sems,
):
    def part(block, i):
        return w_qkv_hbm.at[block, :, pl.ds(i * HD, HD)]

    pairs = [
        (x_hbm, x_in), (part(0, 1), w_kv0.at[0]), (part(0, 2), w_kv0.at[1]), (part(0, 0), w_q),
        (w_out_hbm.at[0], w_out), (part(1, 1), w_kv.at[0]), (part(1, 2), w_kv.at[1]), (part(1, 0), w_q1),
        (w_out_hbm.at[1], w_out1),
    ]
    copies = [pltpu.make_async_copy(src, dst, sems.at[i]) for i, (src, dst) in enumerate(pairs)]
    for copy in copies:
        copy.start()
    lat_odd = where[0] & 1
    rows = 2 * SIDE
    to_window = one_hot(cell_of_window(iota((rows, 1), 0)), iota((rows, OWN), 1))
    copies[0].wait()
    for i in range(CELLS):
        x[i * LEVELS : (i + 1) * LEVELS, :] = x_in[i].astype(jnp.float32)
    cells = x[...].astype(jnp.bfloat16)
    ordered = dot(to_window, cells)
    x_right[...] = ordered[:SIDE].astype(jnp.bfloat16)
    x_left[...] = ordered[SIDE:].astype(jnp.bfloat16)
    for i in range(4):
        span = slice(i * WIN, (i + 1) * WIN)
        normed[span, :] = layer_normed(ordered[span])
    normed_left[...] = normed[SIDE:, :]
    copies[1].wait()
    copies[2].wait()
    for i in range(2):
        kv0[:, i * HD : (i + 1) * HD] = dot(normed[...], w_kv0[i]).astype(jnp.bfloat16)
    side_block(
        lat_odd, x_right, normed[:SIDE, :], kv0, w_q, w_out, w_kv, first_out, wire_out, kv_out, att, scratch,
        lambda i: copies[3 + i].wait(),
    )
    copies[7].wait()
    copies[8].wait()


def left_kernel(
    where, wire_right, x, normed, kv0, w_q, w_out, w_kv, w_q1,
    kv_out, wire_out, first_out, q_far, att, scratch,
):
    side_block(
        where[0] & 1, x, normed[...], kv0, w_q, w_out, w_kv, first_out, wire_out, kv_out, att, scratch,
        lambda i: None,
    )
    for side, wire in enumerate((wire_right, wire_out)):
        q_far[side] = dot(wire[:QUART, :], w_q1[...]).astype(jnp.bfloat16)


def residual_kernel(where, first_right, first_left, wire_right, wire_left, w_q1, first_out, q_near):
    for side, wire in enumerate((wire_right, wire_left)):
        q_near[side] = dot(wire[...], w_q1[...])[QUART:].astype(jnp.bfloat16)
    to_cell = one_hot(iota((OWN, 2 * SIDE), 0), cell_of_window(iota((1, 2 * SIDE), 1)))
    first = jnp.concatenate([first_right[...], first_left[...]], axis=0)
    first_out[...] = dot(to_cell, first).astype(jnp.bfloat16)


def lat_side_calls(q, side_sources, ready=None):
    calls, places = [], []
    for n in range(4):
        group = n & 1
        sources = side_sources[n >> 1]
        lanes = KWIN * len(sources)
        row = iota((QWIN, lanes), 0)
        lane = iota((QWIN, lanes), 1)
        firsts = [first + UNIT * group for _, first in sources]
        starts = [key_start(f, s.shape[0]) for f, (s, _) in zip(firsts, sources)]
        late = row >= 4 * n + UNIT // 2
        valid = jnp.zeros((QWIN, lanes), jnp.bool_)
        for i in range(len(sources)):
            at = lane - (i * KWIN + firsts[i] - starts[i])
            inside = (at >= 0) & (at < UNIT)
            if group == 1:
                inside = inside & ((at >= UNIT // 2) == late)
            valid = valid | inside
        bias = jnp.where(valid, 0.0, NEG).astype(jnp.float32)
        bias = jnp.concatenate([bias] * 4, axis=0)
        start = query_start(n)
        for half in range(2):

            def window(base):
                lanes = slice(base + half * 256, base + half * 256 + 256)
                parts = [s[f : f + KWIN, lanes] for (s, _), f in zip(sources, starts)]
                return jnp.concatenate(parts, axis=0)

            cols = slice(half * 256, half * 256 + 256)
            places.append((slice(n * QWIN, (n + 1) * QWIN), cols))
            queries = spread_heads(q[start : start + QWIN, cols])
            if ready is not None:
                queries = jnp.where(ready[0], ready[1][2 * n + half], queries)
            calls.append((queries, window(0), window(HD), bias))
    return calls, places


def spread_kernel(where, q, out):
    for n in range(4):
        for half in range(2):
            rows = slice(query_start(n), query_start(n) + QWIN)
            out[2 * n + half] = spread_heads(q[rows, half * 256 : half * 256 + 256])


def partial_rows(q, kv_right, kv_left, from_right, from_left, out, att, logs, ready=None):
    calls, places = lat_side_calls(q, [[(kv_right, 0), (from_right, 0)], [(kv_left, 0), (from_left, 0)]], ready)
    outs, sums = attention(calls, with_logs=True)
    head = iota((1, LOGS), 1) & 7
    for n in range(4):
        column = jnp.zeros((QWIN, LOGS), jnp.float32)
        for half in range(2):
            rows, cols = places[2 * n + half]
            att[rows, cols] = outs[2 * n + half]
            for h in range(4):
                part = sums[2 * n + half][h * QWIN : (h + 1) * QWIN]
                column = jnp.where(head == 4 * half + h, part, column)
        high = column.astype(jnp.bfloat16).astype(jnp.float32)
        rest = column - high
        middle = rest.astype(jnp.bfloat16).astype(jnp.float32)
        third = iota((1, LOGS), 1) >> 3
        parts = jnp.where(third == 0, high, jnp.where(third == 1, middle, rest - middle))
        logs[rows, :] = parts.astype(jnp.bfloat16)
    n, index = split_queries(iota((1, 4 * QWIN), 1))
    compact = jnp.where((index >= 0) & (index < UNIT), UNIT * n + index, -1)
    to_compact = one_hot(iota((HALF, 4 * QWIN), 0), compact)
    out[:, :HD] = dot(to_compact, att[...]).astype(jnp.bfloat16)
    out[:, HD:] = dot(to_compact, logs[...]).astype(jnp.bfloat16)


def own_kernel(where, *refs):
    partial_rows(*refs)


def foreign_kernel(where, spread, *refs):
    partial_rows(*refs, ready=(where[0] >= 4, spread))


def near_kernel(where, q, kv_right, kv_left, from_right, from_left, lat, first, w_out, out, att, done):
    own = ((kv_right, from_right), (kv_left, from_left))
    sources = [
        [(own[s][0], QUART), (own[s][1], QUART), (lat, QUART * s), (lat, HALF + QUART * s)] for s in range(2)
    ]
    calls, places = lat_side_calls(q, sources)
    for (rows, cols), result in zip(places, attention(calls)[0]):
        att[rows, cols] = result
    n, index = split_queries(iota((1, 4 * QWIN), 1))
    cell = jnp.where((index >= 0) & (index < UNIT), cell_of_unit(n, index), -1)
    placed = dot(one_hot(iota((HALF, 4 * QWIN), 0), cell), att[...]).astype(jnp.bfloat16)
    rows = pl.ds(pl.multiple_of(HALF * (1 - (where[0] & 1)), 16), HALF)
    done[...] = first[rows, :].astype(jnp.float32) + dot(placed, w_out[...])
    for i in range(CELLS // 2):
        out[i] = done[i * LEVELS : (i + 1) * LEVELS, :].astype(jnp.bfloat16)


def merge_kernel(where, mine, theirs, first, w_out, near, out, done, staged, sems):
    position = where[0] & 3
    far = position & 1
    copy = pltpu.make_async_copy(
        near, out.at[pl.ds((1 - far) * (CELLS // 2), CELLS // 2)], sems.at[0]
    )
    copy.start()
    log_row = iota((LOGS, HD), 0)
    head_of = iota((LOGS, HD), 1) // HEAD
    to_lanes = one_hot(jnp.where(log_row < 24, log_row & 7, -1), head_of)
    gap = dot(mine[:, HD:], to_lanes) - dot(theirs[:, HD:], to_lanes)
    alone = (position == 0) | (position == 3)
    gate = jnp.where(alone, 0.0, 1.0 / (1.0 + jnp.exp(gap)))
    own = mine[:, :HD].astype(jnp.float32)
    att = (own + (theirs[:, :HD].astype(jnp.float32) - own) * gate).astype(jnp.bfloat16)
    index = iota((1, HALF), 1)
    n = at_least(index, UNIT, 2 * UNIT, 3 * UNIT)
    to_cell = one_hot(iota((HALF, HALF), 0), cell_of_unit(n, index - UNIT * n))
    placed = dot(to_cell, att).astype(jnp.bfloat16)
    rows = pl.ds(pl.multiple_of(HALF * far, 16), HALF)
    done[...] = first[rows, :].astype(jnp.float32) + dot(placed, w_out[...])
    copies = [copy]
    step = CELLS // 6
    for j in range(3):
        for i in range(j * step, (j + 1) * step):
            staged[i] = done[i * LEVELS : (i + 1) * LEVELS, :].astype(jnp.bfloat16)
        span = pl.ds(far * (CELLS // 2) + j * step, step)
        copies.append(
            pltpu.make_async_copy(staged.at[pl.ds(j * step, step)], out.at[span], sems.at[1 + j])
        )
        copies[-1].start()
    for copy in copies:
        copy.wait()


def shape(*dims):
    return jax.ShapeDtypeStruct(dims, jnp.bfloat16)


def vmem(*dims):
    return pltpu.VMEM(dims, jnp.bfloat16)


def in_hbm(array):
    return pltpu.with_memory_space_constraint(array, pltpu.HBM)


ANY = pl.BlockSpec(memory_space=pl.ANY)
WHOLE = pl.BlockSpec(memory_space=pltpu.VMEM)
SCALARS = pl.BlockSpec(memory_space=pltpu.SMEM)


def call(kernel, ins, outs, scratch, flops, name, out_spec=WHOLE, limit=40):
    return pl.pallas_call(
        kernel,
        out_shape=outs,
        in_specs=[SCALARS, *ins],
        out_specs=jax.tree.map(lambda _: out_spec, outs),
        scratch_shapes=scratch,
        compiler_params=pltpu.CompilerParams(vmem_limit_bytes=limit * 1024 * 1024),
        cost_estimate=pl.CostEstimate(flops=flops, bytes_accessed=4_000_000, transcendentals=0),
        name=name,
    )


def right_side(where, cells, w_qkv, w_out):
    return call(
        right_kernel,
        [ANY] * 3,
        (
            shape(HALF, D), shape(HALF, D), shape(SIDE, D), shape(SIDE, D), shape(SIDE, D),
            shape(2 * SIDE, D), shape(D, HD), shape(HD, D), shape(2, D, HD), shape(D, HD), shape(HD, D),
        ),
        [
            vmem(CELLS, LEVELS, D), pltpu.VMEM((OWN, D), jnp.float32), vmem(SIDE, D), vmem(2 * SIDE, D),
            vmem(SIDE, HD), vmem(SIDE, D), vmem(2, D, HD), pltpu.SemaphoreType.DMA((9,)),
        ],
        2_000_000_000,
        "right_side",
    )(where, in_hbm(cells), in_hbm(w_qkv), in_hbm(w_out))


def left_side(*args):
    return call(
        left_kernel,
        [WHOLE] * 8,
        (shape(HALF, D), shape(HALF, D), shape(SIDE, D), shape(2, QUART, HD)),
        [vmem(SIDE, HD), vmem(SIDE, D)],
        2_000_000_000,
        "left_side",
    )(*args)


def residual(*args):
    outs = (shape(OWN, D), shape(2, QUART, HD))
    return call(residual_kernel, [WHOLE] * 5, outs, [], 1_000_000_000, "residual")(*args)


def spread(*args):
    return call(
        spread_kernel, [WHOLE], shape(8, 4 * QWIN, 4 * HEAD), [], 2_500_000_000, "spread"
    )(*args)


def partial(name, kernel, *args):
    return call(
        kernel,
        [WHOLE] * (len(args) - 1),
        shape(HALF, HD + LOGS),
        [vmem(4 * QWIN, HD), vmem(4 * QWIN, LOGS)],
        1_000_000_000,
        name,
    )(*args)


DONE = pltpu.VMEM((HALF, D), jnp.float32)


def near_rows(*args):
    return call(
        near_kernel,
        [WHOLE] * 8,
        shape(CELLS // 2, LEVELS, D),
        [vmem(4 * QWIN, HD), DONE],
        2_000_000_000,
        "near_rows",
    )(*args)


def merge(*args):
    return call(
        merge_kernel,
        [WHOLE] * 5,
        shape(CELLS, LEVELS, D),
        [DONE, vmem(CELLS // 2, LEVELS, D), pltpu.SemaphoreType.DMA((4,))],
        2_000_000_000,
        "merge",
        out_spec=ANY,
    )(*args)


def per_device(tokens, w_qkv, w_out):
    lons, lats = lax.axis_size("lon"), lax.axis_size("lat")
    starts_run = (lax.axis_index("lon") % RUN == 0).astype(jnp.int32)
    where = (lax.axis_index("lat").astype(jnp.int32) + 4 * starts_run)[None]
    cells = tokens.transpose(1, 2, 0, 3).reshape(CELLS, LEVELS, D)

    kv_right, wire_right, first_right, *rest = right_side(where, cells, w_qkv, w_out)
    from_left = lax.ppermute(kv_right, "lon", [(i, (i + 1) % lons) for i in range(lons)])
    *rest, w_out1 = rest
    kv_left, wire_left, first_left, q_far = left_side(where, wire_right, *rest)
    w_q1, q_far = rest[-1], q_far.reshape(HALF, HD)
    partner = [i + 1 if i % 2 else i - 1 for i in range(lats)]
    partner[0], partner[-1] = 0, lats - 1
    first_pairs, other_pairs = [], []
    for i in range(lons):
        for j in range(lats):
            one, other = (first_pairs, other_pairs) if i % RUN == 0 else (other_pairs, first_pairs)
            one.append((i * lats + j, i * lats + partner[j]))
            other.append((i * lats + j, i * lats + j))
    foreign_first = lax.ppermute(q_far, ("lon", "lat"), first_pairs)
    from_right = lax.ppermute(kv_left, "lon", [(i, (i - 1) % lons) for i in range(lons)])
    foreign = lax.ppermute(q_far, ("lon", "lat"), other_pairs)

    foreign_first, from_left = lax.optimization_barrier((foreign_first, from_left))
    spread_first = spread(where, foreign_first)
    received = (first_left, spread_first, from_left, from_right, foreign)
    first_left, spread_first, from_left, from_right, foreign = lax.optimization_barrier(received)

    keys = [kv_right, kv_left, from_right, from_left]
    far_pairs = [pair for i in range(1, lats - 1, 2) for pair in ((i, i + 1), (i + 1, i))]
    theirs = partial("foreign_rows", foreign_kernel, where, spread_first, foreign, *keys)
    theirs = lax.ppermute(theirs, "lat", far_pairs)
    to_near = jnp.concatenate([p[QUART:] for p in keys], axis=0)
    from_near = lax.ppermute(to_near, "lat", [(i, i ^ 1) for i in range(lats)])
    mine = partial("own_rows", own_kernel, where, q_far, *keys)
    first, q_near = residual(where, first_right, first_left, wire_right, wire_left, w_q1)
    near = near_rows(where, q_near.reshape(HALF, HD), *keys, from_near, first, w_out1)
    out = merge(where, mine, theirs, first, w_out1, near)
    return out.reshape(ROWS, COLS, LEVELS, D).transpose(2, 0, 1, 3)


def solution(mesh):
    return jax.shard_map(
        per_device,
        mesh=mesh,
        in_specs=(P(None, "lat", "lon", None), P(), P()),
        out_specs=P(None, "lat", "lon", None),
        check_vma=False,
    )
```

```python
import jax
import jax.numpy as jnp
from jax import lax
from jax.experimental import pallas as pl
from jax.experimental.pallas import tpu as pltpu
from jax.sharding import PartitionSpec as P

LEVELS, ROWS, COLS, D = 4, 6, 12, 1024
HD, HEAD = 512, 64
CELLS = ROWS * COLS
OWN = LEVELS * CELLS
HALF = OWN // 2
QUART = HALF // 2
UNIT = 36
WIN = 80
SIDE = 2 * WIN
QWIN = 48
KWIN = 64
NEG = -1e30
LOGS = 128
RUN = 8


def at_least(index, *bounds):
    return sum(jnp.where(index >= bound, 1, 0) for bound in bounds)


def cell_of_window(index):
    side = at_least(index, SIDE)
    index = index - SIDE * side
    pair = at_least(index, WIN)
    index = index - WIN * pair
    valid = index < 2 * UNIT
    level = at_least(index, UNIT)
    index = index - UNIT * level
    row = at_least(index, *range(6, UNIT, 6))
    cell = (row * COLS + 6 * (1 - side) + index - 6 * row) * LEVELS + 2 * pair + level
    return jnp.where(valid, cell, -1)


def split_unit(index, group):
    lev = at_least(index, UNIT // 2)
    index = index - UNIT // 2 * lev
    row = at_least(index, 6, 12)
    return jnp.where(group == 0, 1 + lev, 3 - 3 * lev), row, index - 6 * row


def window_of_wire(index, lat_odd):
    k = at_least(index, UNIT, 2 * UNIT, 3 * UNIT)
    level, row, col = split_unit(index - UNIT * k, k & 1)
    row = row + 3 * ((k >> 1) ^ lat_odd)
    return WIN * (level >> 1) + UNIT * (level & 1) + 6 * row + col


def split_queries(index):
    n = at_least(index, QWIN, 2 * QWIN, 3 * QWIN)
    return n, index - (QWIN + 4) * n


def cell_of_unit(n, index):
    level, row, col = split_unit(index, n & 1)
    return (row * COLS + 6 * (1 - (n >> 1)) + col) * LEVELS + level


def query_start(k):
    return k * UNIT // 16 * 16


def key_start(first, size):
    return min(first // 16 * 16, size - KWIN)


def iota(shape, axis):
    return lax.broadcasted_iota(jnp.int32, shape, axis)


def one_hot(rows, lanes):
    return jnp.where(rows == lanes, 1.0, 0.0).astype(jnp.bfloat16)


def layer_normed(values):
    centre = values - jnp.mean(values, axis=-1, keepdims=True)
    spread = jnp.mean(centre * centre, axis=-1, keepdims=True)
    return (centre * lax.rsqrt(spread + 1e-05)).astype(jnp.bfloat16)


def dot(a, b):
    return jnp.dot(a, b, preferred_element_type=jnp.float32)


def spread_heads(queries):
    head_of = iota((1, 4 * HEAD), 1) // HEAD
    queries = queries * jnp.bfloat16(0.125)
    return jnp.concatenate(
        [jnp.where(head_of == h, queries, jnp.bfloat16(0)) for h in range(4)], axis=0
    )


def attention(calls, with_logs=False):
    head_of = iota((1, 4 * HEAD), 1) // HEAD
    scores = []
    for queries, keys, _, bias in calls:
        product = lax.dot_general(
            queries, keys, (((1,), (1,)), ((), ())), preferred_element_type=jnp.float32
        )
        scores.append(product + bias)
    highest = [jnp.max(s, axis=-1, keepdims=True) for s in scores]
    raised = [jnp.exp(s - h) for s, h in zip(scores, highest)]
    mixed = [dot(r.astype(jnp.bfloat16), call[2]) for r, call in zip(raised, calls)]
    outs, logs = [], []
    for r, m, high in zip(raised, mixed, highest):
        total = jnp.sum(r, axis=-1, keepdims=True)
        m = m * (1.0 / total)
        rows = m.shape[0] // 4
        out = m[:rows]
        for h in range(1, 4):
            out = jnp.where(head_of == h, m[h * rows : (h + 1) * rows], out)
        outs.append(out.astype(jnp.bfloat16))
        logs.append(high + jnp.log(total) if with_logs else None)
    return outs, logs


def side_block(lat_odd, x, normed, kv, w_q, w_out, w_kv, first_out, wire_out, kv_out, att, scratch, ready):
    for i in range(4):
        ready(i)
    queries = dot(normed, w_q[...]).astype(jnp.bfloat16)
    bias = jnp.where(iota((1, 2 * WIN), 1) % WIN < 2 * UNIT, 0.0, NEG).astype(jnp.float32)
    calls, places = [], []
    for pair in range(2):
        rows = slice(pair * WIN, (pair + 1) * WIN)
        far = slice(SIDE + pair * WIN, SIDE + (pair + 1) * WIN)
        for half in range(2):
            cols = slice(half * 256, half * 256 + 256)
            cols_v = slice(HD + half * 256, HD + half * 256 + 256)
            places.append((rows, cols))
            calls.append(
                (
                    spread_heads(queries[rows, cols]),
                    jnp.concatenate([kv[rows, cols], kv[far, cols]], axis=0),
                    jnp.concatenate([kv[rows, cols_v], kv[far, cols_v]], axis=0),
                    bias,
                )
            )
    for (rows, cols), out in zip(places, attention(calls)[0]):
        att[rows, cols] = out
    to_wire = one_hot(window_of_wire(iota((HALF, 1), 0), lat_odd), iota((HALF, SIDE), 1))
    first = (x[...].astype(jnp.float32) + dot(att[...], w_out[...])).astype(jnp.bfloat16)
    first_out[...] = first
    scratch[...] = layer_normed(first.astype(jnp.float32))
    wire = dot(to_wire, scratch[...]).astype(jnp.bfloat16)
    wire_out[...] = wire
    for i in range(2):
        kv_out[:, i * HD : (i + 1) * HD] = dot(wire, w_kv[i]).astype(jnp.bfloat16)


def right_kernel(
    where, x_hbm, w_qkv_hbm, w_out_hbm,
    kv_out, wire_out, first_out, x_left, normed_left, kv0, w_q, w_out, w_kv, w_q1, w_out1,
    x_in, x, x_right, normed, att, scratch, w_kv0, sems,
):
    def part(block, i):
        return w_qkv_hbm.at[block, :, pl.ds(i * HD, HD)]

    pairs = [
        (x_hbm, x_in), (part(0, 1), w_kv0.at[0]), (part(0, 2), w_kv0.at[1]), (part(0, 0), w_q),
        (w_out_hbm.at[0], w_out), (part(1, 1), w_kv.at[0]), (part(1, 2), w_kv.at[1]), (part(1, 0), w_q1),
        (w_out_hbm.at[1], w_out1),
    ]
    copies = [pltpu.make_async_copy(src, dst, sems.at[i]) for i, (src, dst) in enumerate(pairs)]
    for copy in copies:
        copy.start()
    lat_odd = where[0] & 1
    rows = 2 * SIDE
    to_window = one_hot(cell_of_window(iota((rows, 1), 0)), iota((rows, OWN), 1))
    copies[0].wait()
    for i in range(CELLS):
        x[i * LEVELS : (i + 1) * LEVELS, :] = x_in[i].astype(jnp.float32)
    cells = x[...].astype(jnp.bfloat16)
    ordered = dot(to_window, cells)
    x_right[...] = ordered[:SIDE].astype(jnp.bfloat16)
    x_left[...] = ordered[SIDE:].astype(jnp.bfloat16)
    for i in range(4):
        span = slice(i * WIN, (i + 1) * WIN)
        normed[span, :] = layer_normed(ordered[span])
    normed_left[...] = normed[SIDE:, :]
    copies[1].wait()
    copies[2].wait()
    for i in range(2):
        kv0[:, i * HD : (i + 1) * HD] = dot(normed[...], w_kv0[i]).astype(jnp.bfloat16)
    side_block(
        lat_odd, x_right, normed[:SIDE, :], kv0, w_q, w_out, w_kv, first_out, wire_out, kv_out, att, scratch,
        lambda i: copies[3 + i].wait(),
    )
    copies[7].wait()
    copies[8].wait()


def left_kernel(
    where, wire_right, x, normed, kv0, w_q, w_out, w_kv, w_q1,
    kv_out, wire_out, first_out, q_far, att, scratch,
):
    side_block(
        where[0] & 1, x, normed[...], kv0, w_q, w_out, w_kv, first_out, wire_out, kv_out, att, scratch,
        lambda i: None,
    )
    for side, wire in enumerate((wire_right, wire_out)):
        q_far[side] = dot(wire[:QUART, :], w_q1[...]).astype(jnp.bfloat16)


def residual_kernel(where, first_right, first_left, wire_right, wire_left, w_q1, first_out, q_near):
    for side, wire in enumerate((wire_right, wire_left)):
        q_near[side] = dot(wire[...], w_q1[...])[QUART:].astype(jnp.bfloat16)
    to_cell = one_hot(iota((OWN, 2 * SIDE), 0), cell_of_window(iota((1, 2 * SIDE), 1)))
    first = jnp.concatenate([first_right[...], first_left[...]], axis=0)
    first_out[...] = dot(to_cell, first).astype(jnp.bfloat16)


def lat_side_calls(q, side_sources, ready=None):
    calls, places = [], []
    for n in range(4):
        group = n & 1
        sources = side_sources[n >> 1]
        lanes = KWIN * len(sources)
        row = iota((QWIN, lanes), 0)
        lane = iota((QWIN, lanes), 1)
        firsts = [first + UNIT * group for _, first in sources]
        starts = [key_start(f, s.shape[0]) for f, (s, _) in zip(firsts, sources)]
        late = row >= 4 * n + UNIT // 2
        valid = jnp.zeros((QWIN, lanes), jnp.bool_)
        for i in range(len(sources)):
            at = lane - (i * KWIN + firsts[i] - starts[i])
            inside = (at >= 0) & (at < UNIT)
            if group == 1:
                inside = inside & ((at >= UNIT // 2) == late)
            valid = valid | inside
        bias = jnp.where(valid, 0.0, NEG).astype(jnp.float32)
        bias = jnp.concatenate([bias] * 4, axis=0)
        start = query_start(n)
        for half in range(2):

            def window(base):
                lanes = slice(base + half * 256, base + half * 256 + 256)
                parts = [s[f : f + KWIN, lanes] for (s, _), f in zip(sources, starts)]
                return jnp.concatenate(parts, axis=0)

            cols = slice(half * 256, half * 256 + 256)
            places.append((slice(n * QWIN, (n + 1) * QWIN), cols))
            queries = spread_heads(q[start : start + QWIN, cols])
            if ready is not None:
                queries = jnp.where(ready[0], ready[1][2 * n + half], queries)
            calls.append((queries, window(0), window(HD), bias))
    return calls, places


def spread_kernel(where, q, out):
    for n in range(4):
        for half in range(2):
            rows = slice(query_start(n), query_start(n) + QWIN)
            out[2 * n + half] = spread_heads(q[rows, half * 256 : half * 256 + 256])


def partial_rows(q, kv_right, kv_left, from_right, from_left, out, att, logs, ready=None):
    calls, places = lat_side_calls(q, [[(kv_right, 0), (from_right, 0)], [(kv_left, 0), (from_left, 0)]], ready)
    outs, sums = attention(calls, with_logs=True)
    head = iota((1, LOGS), 1) & 7
    for n in range(4):
        column = jnp.zeros((QWIN, LOGS), jnp.float32)
        for half in range(2):
            rows, cols = places[2 * n + half]
            att[rows, cols] = outs[2 * n + half]
            for h in range(4):
                part = sums[2 * n + half][h * QWIN : (h + 1) * QWIN]
                column = jnp.where(head == 4 * half + h, part, column)
        high = column.astype(jnp.bfloat16).astype(jnp.float32)
        rest = column - high
        middle = rest.astype(jnp.bfloat16).astype(jnp.float32)
        third = iota((1, LOGS), 1) >> 3
        parts = jnp.where(third == 0, high, jnp.where(third == 1, middle, rest - middle))
        logs[rows, :] = parts.astype(jnp.bfloat16)
    n, index = split_queries(iota((1, 4 * QWIN), 1))
    compact = jnp.where((index >= 0) & (index < UNIT), UNIT * n + index, -1)
    to_compact = one_hot(iota((HALF, 4 * QWIN), 0), compact)
    out[:, :HD] = dot(to_compact, att[...]).astype(jnp.bfloat16)
    out[:, HD:] = dot(to_compact, logs[...]).astype(jnp.bfloat16)


def own_kernel(where, *refs):
    partial_rows(*refs)


def foreign_kernel(where, spread, *refs):
    partial_rows(*refs, ready=(where[0] >= 4, spread))


def near_kernel(where, q, kv_right, kv_left, from_right, from_left, lat, first, w_out, out, att, done):
    own = ((kv_right, from_right), (kv_left, from_left))
    sources = [
        [(own[s][0], QUART), (own[s][1], QUART), (lat, QUART * s), (lat, HALF + QUART * s)] for s in range(2)
    ]
    calls, places = lat_side_calls(q, sources)
    for (rows, cols), result in zip(places, attention(calls)[0]):
        att[rows, cols] = result
    n, index = split_queries(iota((1, 4 * QWIN), 1))
    cell = jnp.where((index >= 0) & (index < UNIT), cell_of_unit(n, index), -1)
    placed = dot(one_hot(iota((HALF, 4 * QWIN), 0), cell), att[...]).astype(jnp.bfloat16)
    rows = pl.ds(pl.multiple_of(HALF * (1 - (where[0] & 1)), 16), HALF)
    done[...] = first[rows, :].astype(jnp.float32) + dot(placed, w_out[...])
    for i in range(CELLS // 2):
        out[i] = done[i * LEVELS : (i + 1) * LEVELS, :].astype(jnp.bfloat16)


def merge_kernel(where, mine, theirs, first, w_out, near, out, done, staged, sems):
    position = where[0] & 3
    far = position & 1
    copy = pltpu.make_async_copy(
        near, out.at[pl.ds((1 - far) * (CELLS // 2), CELLS // 2)], sems.at[0]
    )
    copy.start()
    log_row = iota((LOGS, HD), 0)
    head_of = iota((LOGS, HD), 1) // HEAD
    to_lanes = one_hot(jnp.where(log_row < 24, log_row & 7, -1), head_of)
    gap = dot(mine[:, HD:], to_lanes) - dot(theirs[:, HD:], to_lanes)
    alone = (position == 0) | (position == 3)
    gate = jnp.where(alone, 0.0, 1.0 / (1.0 + jnp.exp(gap)))
    own = mine[:, :HD].astype(jnp.float32)
    att = (own + (theirs[:, :HD].astype(jnp.float32) - own) * gate).astype(jnp.bfloat16)
    index = iota((1, HALF), 1)
    n = at_least(index, UNIT, 2 * UNIT, 3 * UNIT)
    to_cell = one_hot(iota((HALF, HALF), 0), cell_of_unit(n, index - UNIT * n))
    placed = dot(to_cell, att).astype(jnp.bfloat16)
    rows = pl.ds(pl.multiple_of(HALF * far, 16), HALF)
    done[...] = first[rows, :].astype(jnp.float32) + dot(placed, w_out[...])
    for i in range(CELLS // 2):
        staged[i] = done[i * LEVELS : (i + 1) * LEVELS, :].astype(jnp.bfloat16)
    far_copy = pltpu.make_async_copy(
        staged, out.at[pl.ds(far * (CELLS // 2), CELLS // 2)], sems.at[1]
    )
    far_copy.start()
    copy.wait()
    far_copy.wait()


def shape(*dims):
    return jax.ShapeDtypeStruct(dims, jnp.bfloat16)


def vmem(*dims):
    return pltpu.VMEM(dims, jnp.bfloat16)


def in_hbm(array):
    return pltpu.with_memory_space_constraint(array, pltpu.HBM)


ANY = pl.BlockSpec(memory_space=pl.ANY)
WHOLE = pl.BlockSpec(memory_space=pltpu.VMEM)
SCALARS = pl.BlockSpec(memory_space=pltpu.SMEM)


def call(kernel, ins, outs, scratch, flops, name, out_spec=WHOLE, limit=40):
    return pl.pallas_call(
        kernel,
        out_shape=outs,
        in_specs=[SCALARS, *ins],
        out_specs=jax.tree.map(lambda _: out_spec, outs),
        scratch_shapes=scratch,
        compiler_params=pltpu.CompilerParams(vmem_limit_bytes=limit * 1024 * 1024),
        cost_estimate=pl.CostEstimate(flops=flops, bytes_accessed=4_000_000, transcendentals=0),
        name=name,
    )


def right_side(where, cells, w_qkv, w_out):
    return call(
        right_kernel,
        [ANY] * 3,
        (
            shape(HALF, D), shape(HALF, D), shape(SIDE, D), shape(SIDE, D), shape(SIDE, D),
            shape(2 * SIDE, D), shape(D, HD), shape(HD, D), shape(2, D, HD), shape(D, HD), shape(HD, D),
        ),
        [
            vmem(CELLS, LEVELS, D), pltpu.VMEM((OWN, D), jnp.float32), vmem(SIDE, D), vmem(2 * SIDE, D),
            vmem(SIDE, HD), vmem(SIDE, D), vmem(2, D, HD), pltpu.SemaphoreType.DMA((9,)),
        ],
        2_000_000_000,
        "right_side",
    )(where, in_hbm(cells), in_hbm(w_qkv), in_hbm(w_out))


def left_side(*args):
    return call(
        left_kernel,
        [WHOLE] * 8,
        (shape(HALF, D), shape(HALF, D), shape(SIDE, D), shape(2, QUART, HD)),
        [vmem(SIDE, HD), vmem(SIDE, D)],
        2_000_000_000,
        "left_side",
    )(*args)


def residual(*args):
    outs = (shape(OWN, D), shape(2, QUART, HD))
    return call(residual_kernel, [WHOLE] * 5, outs, [], 1_000_000_000, "residual")(*args)


def spread(*args):
    return call(
        spread_kernel, [WHOLE], shape(8, 4 * QWIN, 4 * HEAD), [], 2_500_000_000, "spread"
    )(*args)


def partial(name, kernel, *args):
    return call(
        kernel,
        [WHOLE] * (len(args) - 1),
        shape(HALF, HD + LOGS),
        [vmem(4 * QWIN, HD), vmem(4 * QWIN, LOGS)],
        1_000_000_000,
        name,
    )(*args)


DONE = pltpu.VMEM((HALF, D), jnp.float32)


def near_rows(*args):
    return call(
        near_kernel,
        [WHOLE] * 8,
        shape(CELLS // 2, LEVELS, D),
        [vmem(4 * QWIN, HD), DONE],
        2_000_000_000,
        "near_rows",
    )(*args)


def merge(*args):
    return call(
        merge_kernel,
        [WHOLE] * 5,
        shape(CELLS, LEVELS, D),
        [DONE, vmem(CELLS // 2, LEVELS, D), pltpu.SemaphoreType.DMA((2,))],
        2_000_000_000,
        "merge",
        out_spec=ANY,
    )(*args)


def per_device(tokens, w_qkv, w_out):
    lons, lats = lax.axis_size("lon"), lax.axis_size("lat")
    starts_run = (lax.axis_index("lon") % RUN == 0).astype(jnp.int32)
    where = (lax.axis_index("lat").astype(jnp.int32) + 4 * starts_run)[None]
    cells = tokens.transpose(1, 2, 0, 3).reshape(CELLS, LEVELS, D)

    kv_right, wire_right, first_right, *rest = right_side(where, cells, w_qkv, w_out)
    from_left = lax.ppermute(kv_right, "lon", [(i, (i + 1) % lons) for i in range(lons)])
    *rest, w_out1 = rest
    kv_left, wire_left, first_left, q_far = left_side(where, wire_right, *rest)
    w_q1, q_far = rest[-1], q_far.reshape(HALF, HD)
    partner = [i + 1 if i % 2 else i - 1 for i in range(lats)]
    partner[0], partner[-1] = 0, lats - 1
    first_pairs, other_pairs = [], []
    for i in range(lons):
        for j in range(lats):
            one, other = (first_pairs, other_pairs) if i % RUN == 0 else (other_pairs, first_pairs)
            one.append((i * lats + j, i * lats + partner[j]))
            other.append((i * lats + j, i * lats + j))
    foreign_first = lax.ppermute(q_far, ("lon", "lat"), first_pairs)
    from_right = lax.ppermute(kv_left, "lon", [(i, (i - 1) % lons) for i in range(lons)])
    foreign = lax.ppermute(q_far, ("lon", "lat"), other_pairs)

    foreign_first, from_left = lax.optimization_barrier((foreign_first, from_left))
    spread_first = spread(where, foreign_first)
    received = (first_left, spread_first, from_left, from_right, foreign)
    first_left, spread_first, from_left, from_right, foreign = lax.optimization_barrier(received)

    keys = [kv_right, kv_left, from_right, from_left]
    far_pairs = [pair for i in range(1, lats - 1, 2) for pair in ((i, i + 1), (i + 1, i))]
    theirs = partial("foreign_rows", foreign_kernel, where, spread_first, foreign, *keys)
    theirs = lax.ppermute(theirs, "lat", far_pairs)
    to_near = jnp.concatenate([p[QUART:] for p in keys], axis=0)
    from_near = lax.ppermute(to_near, "lat", [(i, i ^ 1) for i in range(lats)])
    mine = partial("own_rows", own_kernel, where, q_far, *keys)
    first, q_near = residual(where, first_right, first_left, wire_right, wire_left, w_q1)
    near = near_rows(where, q_near.reshape(HALF, HD), *keys, from_near, first, w_out1)
    out = merge(where, mine, theirs, first, w_out1, near)
    return out.reshape(ROWS, COLS, LEVELS, D).transpose(2, 0, 1, 3)


def solution(mesh):
    return jax.shard_map(
        per_device,
        mesh=mesh,
        in_specs=(P(None, "lat", "lon", None), P(), P()),
        out_specs=P(None, "lat", "lon", None),
        check_vma=False,
    )
```

```python
import jax
import jax.numpy as jnp
from jax import lax
from jax.experimental import pallas as pl
from jax.experimental.pallas import tpu as pltpu
from jax.sharding import PartitionSpec as P

LEVELS, ROWS, COLS, D = 4, 6, 12, 1024
HD, HEAD = 512, 64
CELLS = ROWS * COLS
OWN = LEVELS * CELLS
HALF = OWN // 2
QUART = HALF // 2
UNIT = 36
WIN = 80
SIDE = 2 * WIN
QWIN = 48
KWIN = 64
NEG = -1e30
LOGS = 128
RUN = 8


def at_least(index, *bounds):
    return sum(jnp.where(index >= bound, 1, 0) for bound in bounds)


def cell_of_window(index):
    side = at_least(index, SIDE)
    index = index - SIDE * side
    pair = at_least(index, WIN)
    index = index - WIN * pair
    valid = index < 2 * UNIT
    level = at_least(index, UNIT)
    index = index - UNIT * level
    row = at_least(index, *range(6, UNIT, 6))
    cell = (row * COLS + 6 * (1 - side) + index - 6 * row) * LEVELS + 2 * pair + level
    return jnp.where(valid, cell, -1)


def split_unit(index, group):
    lev = at_least(index, UNIT // 2)
    index = index - UNIT // 2 * lev
    row = at_least(index, 6, 12)
    return jnp.where(group == 0, 1 + lev, 3 - 3 * lev), row, index - 6 * row


def window_of_wire(index, lat_odd):
    k = at_least(index, UNIT, 2 * UNIT, 3 * UNIT)
    level, row, col = split_unit(index - UNIT * k, k & 1)
    row = row + 3 * ((k >> 1) ^ lat_odd)
    return WIN * (level >> 1) + UNIT * (level & 1) + 6 * row + col


def cell_of_unit(n, index):
    level, row, col = split_unit(index, n & 1)
    return (row * COLS + 6 * (1 - (n >> 1)) + col) * LEVELS + level


def query_start(k):
    return k * UNIT // 16 * 16


def key_start(first, size):
    return min(first // 16 * 16, size - KWIN)


def iota(shape, axis):
    return lax.broadcasted_iota(jnp.int32, shape, axis)


def one_hot(rows, lanes):
    return jnp.where(rows == lanes, 1.0, 0.0).astype(jnp.bfloat16)


def layer_normed(values):
    centre = values - jnp.mean(values, axis=-1, keepdims=True)
    spread = jnp.mean(centre * centre, axis=-1, keepdims=True)
    return (centre * lax.rsqrt(spread + 1e-05)).astype(jnp.bfloat16)


def dot(a, b):
    return jnp.dot(a, b, preferred_element_type=jnp.float32)


def cells_from_queries():
    index = iota((1, 4 * QWIN), 1)
    n = at_least(index, QWIN, 2 * QWIN, 3 * QWIN)
    index = index - (QWIN + 4) * n
    cell = jnp.where((index >= 0) & (index < UNIT), cell_of_unit(n, index), -1)
    return one_hot(iota((HALF, 4 * QWIN), 0), cell)


def spread_heads(queries):
    head_of = iota((1, 4 * HEAD), 1) // HEAD
    queries = queries * jnp.bfloat16(0.125)
    return jnp.concatenate(
        [jnp.where(head_of == h, queries, jnp.bfloat16(0)) for h in range(4)], axis=0
    )


def attention(calls, with_logs=False):
    head_of = iota((1, 4 * HEAD), 1) // HEAD
    scores = []
    for queries, keys, _, bias in calls:
        product = lax.dot_general(
            queries, keys, (((1,), (1,)), ((), ())), preferred_element_type=jnp.float32
        )
        scores.append(product + bias)
    highest = [jnp.max(s, axis=-1, keepdims=True) for s in scores]
    raised = [jnp.exp(s - h) for s, h in zip(scores, highest)]
    mixed = [dot(r.astype(jnp.bfloat16), call[2]) for r, call in zip(raised, calls)]
    outs, logs = [], []
    for r, m, high in zip(raised, mixed, highest):
        total = jnp.sum(r, axis=-1, keepdims=True)
        m = m * (1.0 / total)
        rows = m.shape[0] // 4
        out = m[:rows]
        for h in range(1, 4):
            out = jnp.where(head_of == h, m[h * rows : (h + 1) * rows], out)
        outs.append(out.astype(jnp.bfloat16))
        logs.append(high + jnp.log(total) if with_logs else None)
    return outs, logs


def side_block(lat_odd, x, normed, kv, w_q, w_out, w_kv, first_out, wire_out, kv_out, att, scratch, ready):
    for i in range(4):
        ready(i)
    queries = dot(normed, w_q[...]).astype(jnp.bfloat16)
    bias = jnp.where(iota((1, 2 * WIN), 1) % WIN < 2 * UNIT, 0.0, NEG).astype(jnp.float32)
    calls, places = [], []
    for pair in range(2):
        rows = slice(pair * WIN, (pair + 1) * WIN)
        far = slice(SIDE + pair * WIN, SIDE + (pair + 1) * WIN)
        for half in range(2):
            cols = slice(half * 256, half * 256 + 256)
            cols_v = slice(HD + half * 256, HD + half * 256 + 256)
            places.append((rows, cols))
            calls.append(
                (
                    spread_heads(queries[rows, cols]),
                    jnp.concatenate([kv[rows, cols], kv[far, cols]], axis=0),
                    jnp.concatenate([kv[rows, cols_v], kv[far, cols_v]], axis=0),
                    bias,
                )
            )
    for (rows, cols), out in zip(places, attention(calls)[0]):
        att[rows, cols] = out
    to_wire = one_hot(window_of_wire(iota((HALF, 1), 0), lat_odd), iota((HALF, SIDE), 1))
    first = (x[...].astype(jnp.float32) + dot(att[...], w_out[...])).astype(jnp.bfloat16)
    first_out[...] = first
    scratch[...] = layer_normed(first.astype(jnp.float32))
    wire = dot(to_wire, scratch[...]).astype(jnp.bfloat16)
    wire_out[...] = wire
    for i in range(2):
        kv_out[:, i * HD : (i + 1) * HD] = dot(wire, w_kv[i]).astype(jnp.bfloat16)


def right_kernel(
    where, x_hbm, w_qkv_hbm, w_out_hbm,
    kv_out, wire_out, first_out, x_left, normed_left, kv0, w_q, w_out, w_kv, w_q1, w_out1,
    x_in, x, x_right, normed, att, scratch, w_kv0, sems,
):
    def part(block, i):
        return w_qkv_hbm.at[block, :, pl.ds(i * HD, HD)]

    pairs = [
        (x_hbm, x_in), (part(0, 1), w_kv0.at[0]), (part(0, 2), w_kv0.at[1]), (part(0, 0), w_q),
        (w_out_hbm.at[0], w_out), (part(1, 1), w_kv.at[0]), (part(1, 2), w_kv.at[1]), (part(1, 0), w_q1),
        (w_out_hbm.at[1], w_out1),
    ]
    copies = [pltpu.make_async_copy(src, dst, sems.at[i]) for i, (src, dst) in enumerate(pairs)]
    for copy in copies:
        copy.start()
    lat_odd = where[0] & 1
    rows = 2 * SIDE
    to_window = one_hot(cell_of_window(iota((rows, 1), 0)), iota((rows, OWN), 1))
    copies[0].wait()
    for i in range(CELLS):
        x[i * LEVELS : (i + 1) * LEVELS, :] = x_in[i].astype(jnp.float32)
    cells = x[...].astype(jnp.bfloat16)
    ordered = dot(to_window, cells)
    x_right[...] = ordered[:SIDE].astype(jnp.bfloat16)
    x_left[...] = ordered[SIDE:].astype(jnp.bfloat16)
    for i in range(4):
        span = slice(i * WIN, (i + 1) * WIN)
        normed[span, :] = layer_normed(ordered[span])
    normed_left[...] = normed[SIDE:, :]
    copies[1].wait()
    copies[2].wait()
    for i in range(2):
        kv0[:, i * HD : (i + 1) * HD] = dot(normed[...], w_kv0[i]).astype(jnp.bfloat16)
    side_block(
        lat_odd, x_right, normed[:SIDE, :], kv0, w_q, w_out, w_kv, first_out, wire_out, kv_out, att, scratch,
        lambda i: copies[3 + i].wait(),
    )
    copies[7].wait()
    copies[8].wait()


def left_kernel(
    where, wire_right, x, normed, kv0, w_q, w_out, w_kv, w_q1,
    kv_out, wire_out, first_out, q_far, att, scratch,
):
    side_block(
        where[0] & 1, x, normed[...], kv0, w_q, w_out, w_kv, first_out, wire_out, kv_out, att, scratch,
        lambda i: None,
    )
    q_far[...] = jnp.zeros_like(q_far)

    @pl.when(where[0] >= 4)
    def _():
        far_queries(wire_right, wire_out, w_q1, q_far)


def far_queries(wire_right, wire_left, w_q1, q_far):
    for side, wire in enumerate((wire_right, wire_left)):
        q_far[side] = dot(wire[:QUART, :], w_q1[...]).astype(jnp.bfloat16)


def late_kernel(where, q_first, wire_right, wire_left, w_q1, q_far):
    @pl.when(where[0] >= 4)
    def _():
        q_far[...] = q_first[...]

    @pl.when(where[0] < 4)
    def _():
        far_queries(wire_right, wire_left, w_q1, q_far)


def residual_kernel(where, first_right, first_left, wire_right, wire_left, w_q1, first_out, q_near):
    for side, wire in enumerate((wire_right, wire_left)):
        q_near[side] = dot(wire[...], w_q1[...])[QUART:].astype(jnp.bfloat16)
    to_cell = one_hot(iota((OWN, 2 * SIDE), 0), cell_of_window(iota((1, 2 * SIDE), 1)))
    first = jnp.concatenate([first_right[...], first_left[...]], axis=0)
    first_out[...] = dot(to_cell, first).astype(jnp.bfloat16)


def lat_side_calls(q, side_sources, ready=None):
    calls, places = [], []
    for n in range(4):
        group = n & 1
        sources = side_sources[n >> 1]
        lanes = KWIN * len(sources)
        row = iota((QWIN, lanes), 0)
        lane = iota((QWIN, lanes), 1)
        firsts = [first + UNIT * group for _, first in sources]
        starts = [key_start(f, s.shape[0]) for f, (s, _) in zip(firsts, sources)]
        late = row >= 4 * n + UNIT // 2
        valid = jnp.zeros((QWIN, lanes), jnp.bool_)
        for i in range(len(sources)):
            at = lane - (i * KWIN + firsts[i] - starts[i])
            inside = (at >= 0) & (at < UNIT)
            if group == 1:
                inside = inside & ((at >= UNIT // 2) == late)
            valid = valid | inside
        bias = jnp.where(valid, 0.0, NEG).astype(jnp.float32)
        bias = jnp.concatenate([bias] * 4, axis=0)
        start = query_start(n)
        for half in range(2):

            def window(base):
                lanes = slice(base + half * 256, base + half * 256 + 256)
                parts = [s[f : f + KWIN, lanes] for (s, _), f in zip(sources, starts)]
                return jnp.concatenate(parts, axis=0)

            cols = slice(half * 256, half * 256 + 256)
            places.append((slice(n * QWIN, (n + 1) * QWIN), cols))
            queries = spread_heads(q[start : start + QWIN, cols])
            if ready is not None:
                queries = jnp.where(ready[0], ready[1][2 * n + half], queries)
            calls.append((queries, window(0), window(HD), bias))
    return calls, places


def spread_kernel(where, q, out):
    for n in range(4):
        for half in range(2):
            rows = slice(query_start(n), query_start(n) + QWIN)
            out[2 * n + half] = spread_heads(q[rows, half * 256 : half * 256 + 256])


def partial_rows(q, kv_right, kv_left, from_right, from_left, out, att, logs, ready=None):
    calls, places = lat_side_calls(q, [[(kv_right, 0), (from_right, 0)], [(kv_left, 0), (from_left, 0)]], ready)
    outs, sums = attention(calls, with_logs=True)
    head = iota((1, LOGS), 1) & 7
    for n in range(4):
        column = jnp.zeros((QWIN, LOGS), jnp.float32)
        for half in range(2):
            rows, cols = places[2 * n + half]
            att[rows, cols] = outs[2 * n + half]
            for h in range(4):
                part = sums[2 * n + half][h * QWIN : (h + 1) * QWIN]
                column = jnp.where(head == 4 * half + h, part, column)
        high = column.astype(jnp.bfloat16).astype(jnp.float32)
        rest = column - high
        middle = rest.astype(jnp.bfloat16).astype(jnp.float32)
        third = iota((1, LOGS), 1) >> 3
        parts = jnp.where(third == 0, high, jnp.where(third == 1, middle, rest - middle))
        logs[rows, :] = parts.astype(jnp.bfloat16)
    to_cell = cells_from_queries()
    out[:, :HD] = dot(to_cell, att[...]).astype(jnp.bfloat16)
    out[:, HD:] = dot(to_cell, logs[...]).astype(jnp.bfloat16)


def own_kernel(where, *refs):
    partial_rows(*refs)


def foreign_kernel(where, spread, *refs):
    partial_rows(*refs, ready=(where[0] >= 4, spread))


def near_kernel(where, q, kv_right, kv_left, from_right, from_left, lat, first, w_out, out, att, done):
    own = ((kv_right, from_right), (kv_left, from_left))
    sources = [
        [(own[s][0], QUART), (own[s][1], QUART), (lat, QUART * s), (lat, HALF + QUART * s)] for s in range(2)
    ]
    calls, places = lat_side_calls(q, sources)
    for (rows, cols), result in zip(places, attention(calls)[0]):
        att[rows, cols] = result
    placed = dot(cells_from_queries(), att[...]).astype(jnp.bfloat16)
    rows = pl.ds(pl.multiple_of(HALF * (1 - (where[0] & 1)), 16), HALF)
    done[...] = first[rows, :].astype(jnp.float32) + dot(placed, w_out[...])
    for i in range(CELLS // 2):
        out[i] = done[i * LEVELS : (i + 1) * LEVELS, :].astype(jnp.bfloat16)


def merge_kernel(where, mine, theirs, first, w_out, near, out, done, staged, sems):
    position = where[0] & 3
    far = position & 1
    copy = pltpu.make_async_copy(
        near, out.at[pl.ds((1 - far) * (CELLS // 2), CELLS // 2)], sems.at[0]
    )
    copy.start()
    log_row = iota((2 * LOGS, HD), 0)
    part = log_row & (LOGS - 1)
    same_head = (part < 24) & ((part & 7) == iota((2 * LOGS, HD), 1) // HEAD)
    to_lanes = jnp.where(same_head, jnp.where(log_row < LOGS, 1.0, -1.0), 0.0).astype(jnp.bfloat16)
    gap = dot(jnp.concatenate([mine[:, HD:], theirs[:, HD:]], axis=1), to_lanes)
    alone = (position == 0) | (position == 3)
    gate = jnp.where(alone, 0.0, 1.0 / (1.0 + jnp.exp(gap)))
    own = mine[:, :HD].astype(jnp.float32)
    att = (own + (theirs[:, :HD].astype(jnp.float32) - own) * gate).astype(jnp.bfloat16)
    rows = pl.ds(pl.multiple_of(HALF * far, 16), HALF)
    done[...] = first[rows, :].astype(jnp.float32) + dot(att, w_out[...])
    for i in range(CELLS // 2):
        staged[i] = done[i * LEVELS : (i + 1) * LEVELS, :].astype(jnp.bfloat16)
    far_copy = pltpu.make_async_copy(
        staged, out.at[pl.ds(far * (CELLS // 2), CELLS // 2)], sems.at[1]
    )
    far_copy.start()
    copy.wait()
    far_copy.wait()


def shape(*dims):
    return jax.ShapeDtypeStruct(dims, jnp.bfloat16)


def vmem(*dims):
    return pltpu.VMEM(dims, jnp.bfloat16)


def in_hbm(array):
    return pltpu.with_memory_space_constraint(array, pltpu.HBM)


ANY = pl.BlockSpec(memory_space=pl.ANY)
WHOLE = pl.BlockSpec(memory_space=pltpu.VMEM)
SCALARS = pl.BlockSpec(memory_space=pltpu.SMEM)


def call(kernel, ins, outs, scratch, flops, name, out_spec=WHOLE, limit=40):
    return pl.pallas_call(
        kernel,
        out_shape=outs,
        in_specs=[SCALARS, *ins],
        out_specs=jax.tree.map(lambda _: out_spec, outs),
        scratch_shapes=scratch,
        compiler_params=pltpu.CompilerParams(vmem_limit_bytes=limit * 1024 * 1024),
        cost_estimate=pl.CostEstimate(flops=flops, bytes_accessed=4_000_000, transcendentals=0),
        name=name,
    )


def right_side(where, cells, w_qkv, w_out):
    return call(
        right_kernel,
        [ANY] * 3,
        (
            shape(HALF, D), shape(HALF, D), shape(SIDE, D), shape(SIDE, D), shape(SIDE, D),
            shape(2 * SIDE, D), shape(D, HD), shape(HD, D), shape(2, D, HD), shape(D, HD), shape(HD, D),
        ),
        [
            vmem(CELLS, LEVELS, D), pltpu.VMEM((OWN, D), jnp.float32), vmem(SIDE, D), vmem(2 * SIDE, D),
            vmem(SIDE, HD), vmem(SIDE, D), vmem(2, D, HD), pltpu.SemaphoreType.DMA((9,)),
        ],
        2_000_000_000,
        "right_side",
    )(where, in_hbm(cells), in_hbm(w_qkv), in_hbm(w_out))


def left_side(*args):
    return call(
        left_kernel,
        [WHOLE] * 8,
        (shape(HALF, D), shape(HALF, D), shape(SIDE, D), shape(2, QUART, HD)),
        [vmem(SIDE, HD), vmem(SIDE, D)],
        2_000_000_000,
        "left_side",
    )(*args)


def late_queries(*args):
    return call(late_kernel, [WHOLE] * 4, shape(2, QUART, HD), [], 200_000_000, "late_queries")(*args)


def residual(*args):
    outs = (shape(OWN, D), shape(2, QUART, HD))
    return call(residual_kernel, [WHOLE] * 5, outs, [], 1_000_000_000, "residual")(*args)


def spread(*args):
    return call(
        spread_kernel, [WHOLE], shape(8, 4 * QWIN, 4 * HEAD), [], 2_500_000_000, "spread"
    )(*args)


def partial(name, kernel, *args):
    return call(
        kernel,
        [WHOLE] * (len(args) - 1),
        shape(HALF, HD + LOGS),
        [vmem(4 * QWIN, HD), vmem(4 * QWIN, LOGS)],
        1_000_000_000,
        name,
    )(*args)


DONE = pltpu.VMEM((HALF, D), jnp.float32)


def near_rows(*args):
    return call(
        near_kernel,
        [WHOLE] * 8,
        shape(CELLS // 2, LEVELS, D),
        [vmem(4 * QWIN, HD), DONE],
        2_000_000_000,
        "near_rows",
    )(*args)


def merge(*args):
    return call(
        merge_kernel,
        [WHOLE] * 5,
        shape(CELLS, LEVELS, D),
        [DONE, vmem(CELLS // 2, LEVELS, D), pltpu.SemaphoreType.DMA((2,))],
        2_000_000_000,
        "merge",
        out_spec=ANY,
    )(*args)


def per_device(tokens, w_qkv, w_out):
    lons, lats = lax.axis_size("lon"), lax.axis_size("lat")
    starts_run = (lax.axis_index("lon") % RUN == 0).astype(jnp.int32)
    where = (lax.axis_index("lat").astype(jnp.int32) + 4 * starts_run)[None]
    cells = tokens.transpose(1, 2, 0, 3).reshape(CELLS, LEVELS, D)

    kv_right, wire_right, first_right, *rest = right_side(where, cells, w_qkv, w_out)
    from_left = lax.ppermute(kv_right, "lon", [(i, (i + 1) % lons) for i in range(lons)])
    *rest, w_out1 = rest
    kv_left, wire_left, first_left, q_first = left_side(where, wire_right, *rest)
    w_q1 = rest[-1]
    partner = [i + 1 if i % 2 else i - 1 for i in range(lats)]
    partner[0], partner[-1] = 0, lats - 1
    first_pairs, other_pairs = [], []
    for i in range(lons):
        for j in range(lats):
            one, other = (first_pairs, other_pairs) if i % RUN == 0 else (other_pairs, first_pairs)
            one.append((i * lats + j, i * lats + partner[j]))
            other.append((i * lats + j, i * lats + j))
    foreign_first = lax.ppermute(q_first, ("lon", "lat"), first_pairs).reshape(HALF, HD)
    from_right = lax.ppermute(kv_left, "lon", [(i, (i - 1) % lons) for i in range(lons)])
    q_far = late_queries(where, q_first, wire_right, wire_left, w_q1).reshape(HALF, HD)
    foreign = lax.ppermute(q_far, ("lon", "lat"), other_pairs)

    foreign_first, from_left = lax.optimization_barrier((foreign_first, from_left))
    spread_first = spread(where, foreign_first)
    received = (first_left, spread_first, from_left, from_right, foreign)
    first_left, spread_first, from_left, from_right, foreign = lax.optimization_barrier(received)

    keys = [kv_right, kv_left, from_right, from_left]
    far_pairs = [pair for i in range(1, lats - 1, 2) for pair in ((i, i + 1), (i + 1, i))]
    theirs = partial("foreign_rows", foreign_kernel, where, spread_first, foreign, *keys)
    theirs = lax.ppermute(theirs, "lat", far_pairs)
    to_near = jnp.concatenate([p[QUART:] for p in keys], axis=0)
    from_near = lax.ppermute(to_near, "lat", [(i, i ^ 1) for i in range(lats)])
    mine = partial("own_rows", own_kernel, where, q_far, *keys)
    first, q_near = residual(where, first_right, first_left, wire_right, wire_left, w_q1)
    near = near_rows(where, q_near.reshape(HALF, HD), *keys, from_near, first, w_out1)
    out = merge(where, mine, theirs, first, w_out1, near)
    return out.reshape(ROWS, COLS, LEVELS, D).transpose(2, 0, 1, 3)


def solution(mesh):
    return jax.shard_map(
        per_device,
        mesh=mesh,
        in_specs=(P(None, "lat", "lon", None), P(), P()),
        out_specs=P(None, "lat", "lon", None),
        check_vma=False,
    )
```

```python
import jax
import jax.numpy as jnp
from jax import lax
from jax.experimental import pallas as pl
from jax.experimental.pallas import tpu as pltpu
from jax.sharding import PartitionSpec as P

LEVELS, ROWS, COLS, D = 4, 6, 12, 1024
HD, HEAD = 512, 64
CELLS = ROWS * COLS
OWN = LEVELS * CELLS
HALF = OWN // 2
QUART = HALF // 2
UNIT = 36
WIN = 80
SIDE = 2 * WIN
QWIN = 48
KWIN = 64
NEG = -1e30
LOGS = 128
RUN = 8


def at_least(index, *bounds):
    return sum(jnp.where(index >= bound, 1, 0) for bound in bounds)


def cell_of_window(index):
    side = at_least(index, SIDE)
    index = index - SIDE * side
    pair = at_least(index, WIN)
    index = index - WIN * pair
    valid = index < 2 * UNIT
    level = at_least(index, UNIT)
    index = index - UNIT * level
    row = at_least(index, *range(6, UNIT, 6))
    cell = (row * COLS + 6 * (1 - side) + index - 6 * row) * LEVELS + 2 * pair + level
    return jnp.where(valid, cell, -1)


def split_unit(index, group):
    lev = at_least(index, UNIT // 2)
    index = index - UNIT // 2 * lev
    row = at_least(index, 6, 12)
    return jnp.where(group == 0, 1 + lev, 3 - 3 * lev), row, index - 6 * row


def window_of_wire(index, lat_odd):
    k = at_least(index, UNIT, 2 * UNIT, 3 * UNIT)
    level, row, col = split_unit(index - UNIT * k, k & 1)
    row = row + 3 * ((k >> 1) ^ lat_odd)
    return WIN * (level >> 1) + UNIT * (level & 1) + 6 * row + col


def cell_of_unit(n, index):
    level, row, col = split_unit(index, n & 1)
    return (row * COLS + 6 * (1 - (n >> 1)) + col) * LEVELS + level


def query_start(k):
    return k * UNIT // 16 * 16


def key_start(first, size):
    return min(first // 16 * 16, size - KWIN)


def iota(shape, axis):
    return lax.broadcasted_iota(jnp.int32, shape, axis)


def one_hot(rows, lanes):
    return jnp.where(rows == lanes, 1.0, 0.0).astype(jnp.bfloat16)


def layer_normed(values):
    centre = values - jnp.mean(values, axis=-1, keepdims=True)
    spread = jnp.mean(centre * centre, axis=-1, keepdims=True)
    return (centre * lax.rsqrt(spread + 1e-05)).astype(jnp.bfloat16)


def dot(a, b):
    return jnp.dot(a, b, preferred_element_type=jnp.float32)


def cells_from_queries():
    index = iota((1, 4 * QWIN), 1)
    n = at_least(index, QWIN, 2 * QWIN, 3 * QWIN)
    index = index - QWIN * n - 4 * (n & 1)
    cell = jnp.where((index >= 0) & (index < UNIT), cell_of_unit(n, index), -1)
    return one_hot(iota((HALF, 4 * QWIN), 0), cell)


def spread_heads(queries):
    head_of = iota((1, 4 * HEAD), 1) // HEAD
    queries = queries * jnp.bfloat16(0.125)
    return jnp.concatenate(
        [jnp.where(head_of == h, queries, jnp.bfloat16(0)) for h in range(4)], axis=0
    )


def attention(calls, with_logs=False):
    head_of = iota((1, 4 * HEAD), 1) // HEAD
    scores = []
    for queries, keys, _, bias in calls:
        product = lax.dot_general(
            queries, keys, (((1,), (1,)), ((), ())), preferred_element_type=jnp.float32
        )
        scores.append(product + bias)
    highest = [jnp.max(s, axis=-1, keepdims=True) for s in scores]
    raised = [jnp.exp(s - h) for s, h in zip(scores, highest)]
    mixed = [dot(r.astype(jnp.bfloat16), call[2]) for r, call in zip(raised, calls)]
    outs, logs = [], []
    for r, m, high in zip(raised, mixed, highest):
        total = jnp.sum(r, axis=-1, keepdims=True)
        m = m * (1.0 / total)
        rows = m.shape[0] // 4
        out = m[:rows]
        for h in range(1, 4):
            out = jnp.where(head_of == h, m[h * rows : (h + 1) * rows], out)
        outs.append(out.astype(jnp.bfloat16))
        logs.append(high + jnp.log(total) if with_logs else None)
    return outs, logs


def side_block(lat_odd, x, normed, kv, w_q, w_out, w_kv, first_out, wire_out, kv_far, kv_near, att, scratch, ready):
    for i in range(4):
        ready(i)
    queries = dot(normed, w_q[...]).astype(jnp.bfloat16)
    bias = jnp.where(iota((1, 2 * WIN), 1) % WIN < 2 * UNIT, 0.0, NEG).astype(jnp.float32)
    calls, places = [], []
    for pair in range(2):
        rows = slice(pair * WIN, (pair + 1) * WIN)
        far = slice(SIDE + pair * WIN, SIDE + (pair + 1) * WIN)
        for half in range(2):
            cols = slice(half * 256, half * 256 + 256)
            cols_v = slice(HD + half * 256, HD + half * 256 + 256)
            places.append((rows, cols))
            calls.append(
                (
                    spread_heads(queries[rows, cols]),
                    jnp.concatenate([kv[rows, cols], kv[far, cols]], axis=0),
                    jnp.concatenate([kv[rows, cols_v], kv[far, cols_v]], axis=0),
                    bias,
                )
            )
    for (rows, cols), out in zip(places, attention(calls)[0]):
        att[rows, cols] = out
    to_wire = one_hot(window_of_wire(iota((HALF, 1), 0), lat_odd), iota((HALF, SIDE), 1))
    first = (x[...].astype(jnp.float32) + dot(att[...], w_out[...])).astype(jnp.bfloat16)
    first_out[...] = first
    scratch[...] = layer_normed(first.astype(jnp.float32))
    wire = dot(to_wire, scratch[...]).astype(jnp.bfloat16)
    wire_out[...] = wire
    for i in range(2):
        part = dot(wire, w_kv[i])
        kv_far[:, i * HD : (i + 1) * HD] = part[:QUART].astype(jnp.bfloat16)
        kv_near[:, i * HD : (i + 1) * HD] = part[QUART:].astype(jnp.bfloat16)


def right_kernel(
    where, x_hbm, w_qkv_hbm, w_out_hbm,
    kv_far, kv_near, wire_out, first_out, x_left, normed_left, kv0, w_q, w_out, w_kv, w_q1, w_out1,
    x_in, x, x_right, normed, att, scratch, w_kv0, sems,
):
    def part(block, i):
        return w_qkv_hbm.at[block, :, pl.ds(i * HD, HD)]

    pairs = [
        (x_hbm, x_in), (part(0, 1), w_kv0.at[0]), (part(0, 2), w_kv0.at[1]), (part(0, 0), w_q),
        (w_out_hbm.at[0], w_out), (part(1, 1), w_kv.at[0]), (part(1, 2), w_kv.at[1]), (part(1, 0), w_q1),
        (w_out_hbm.at[1], w_out1),
    ]
    copies = [pltpu.make_async_copy(src, dst, sems.at[i]) for i, (src, dst) in enumerate(pairs)]
    for copy in copies:
        copy.start()
    lat_odd = where[0] & 1
    rows = 2 * SIDE
    to_window = one_hot(cell_of_window(iota((rows, 1), 0)), iota((rows, OWN), 1))
    copies[0].wait()
    for i in range(CELLS):
        x[i * LEVELS : (i + 1) * LEVELS, :] = x_in[i].astype(jnp.float32)
    cells = x[...].astype(jnp.bfloat16)
    ordered = dot(to_window, cells)
    x_right[...] = ordered[:SIDE].astype(jnp.bfloat16)
    x_left[...] = ordered[SIDE:].astype(jnp.bfloat16)
    for i in range(4):
        span = slice(i * WIN, (i + 1) * WIN)
        normed[span, :] = layer_normed(ordered[span])
    normed_left[...] = normed[SIDE:, :]
    copies[1].wait()
    copies[2].wait()
    for i in range(2):
        kv0[:, i * HD : (i + 1) * HD] = dot(normed[...], w_kv0[i]).astype(jnp.bfloat16)
    side_block(
        lat_odd, x_right, normed[:SIDE, :], kv0, w_q, w_out, w_kv, first_out, wire_out, kv_far, kv_near, att, scratch,
        lambda i: copies[3 + i].wait(),
    )
    copies[7].wait()
    copies[8].wait()


def left_kernel(
    where, wire_right, x, normed, kv0, w_q, w_out, w_kv, w_q1,
    kv_far, kv_near, wire_out, first_out, q_far, att, scratch,
):
    side_block(
        where[0] & 1, x, normed[...], kv0, w_q, w_out, w_kv, first_out, wire_out, kv_far, kv_near, att, scratch,
        lambda i: None,
    )
    q_far[...] = jnp.zeros_like(q_far)

    @pl.when(where[0] >= 4)
    def _():
        far_queries(wire_right, wire_out, w_q1, q_far)


def far_queries(wire_right, wire_left, w_q1, q_far):
    for side, wire in enumerate((wire_right, wire_left)):
        q_far[side] = dot(wire[:QUART, :], w_q1[...]).astype(jnp.bfloat16)


def late_kernel(where, q_first, wire_right, wire_left, w_q1, *q_far):
    @pl.when(where[0] >= 4)
    def _():
        for side in range(2):
            q_far[side][...] = q_first[side]

    @pl.when(where[0] < 4)
    def _():
        for side, wire in enumerate((wire_right, wire_left)):
            q_far[side][...] = dot(wire[:QUART, :], w_q1[...]).astype(jnp.bfloat16)


def residual_kernel(where, first_right, first_left, wire_right, wire_left, w_q1, first_out, q_near):
    for side, wire in enumerate((wire_right, wire_left)):
        q_near[side] = dot(wire[...], w_q1[...])[QUART:].astype(jnp.bfloat16)
    to_cell = one_hot(iota((OWN, 2 * SIDE), 0), cell_of_window(iota((1, 2 * SIDE), 1)))
    first = jnp.concatenate([first_right[...], first_left[...]], axis=0)
    first_out[...] = dot(to_cell, first).astype(jnp.bfloat16)


def lat_side_calls(q, side_sources):
    calls, places = [], []
    for n in range(4):
        group = n & 1
        sources = side_sources[n >> 1]
        lanes = KWIN * len(sources)
        row = iota((QWIN, lanes), 0)
        lane = iota((QWIN, lanes), 1)
        firsts = [first + UNIT * group for _, first in sources]
        starts = [key_start(f, s.shape[0]) for f, (s, _) in zip(firsts, sources)]
        late = row >= 4 * group + UNIT // 2
        valid = jnp.zeros((QWIN, lanes), jnp.bool_)
        for i in range(len(sources)):
            at = lane - (i * KWIN + firsts[i] - starts[i])
            inside = (at >= 0) & (at < UNIT)
            if group == 1:
                inside = inside & ((at >= UNIT // 2) == late)
            valid = valid | inside
        bias = jnp.where(valid, 0.0, NEG).astype(jnp.float32)
        bias = jnp.concatenate([bias] * 4, axis=0)
        start = query_start(group)
        queries = q[n >> 1]
        for half in range(2):

            def window(base):
                lanes = slice(base + half * 256, base + half * 256 + 256)
                parts = [s[f : f + KWIN, lanes] for (s, _), f in zip(sources, starts)]
                return jnp.concatenate(parts, axis=0)

            cols = slice(half * 256, half * 256 + 256)
            places.append((slice(n * QWIN, (n + 1) * QWIN), cols))
            calls.append((spread_heads(queries[start : start + QWIN, cols]), window(0), window(HD), bias))
    return calls, places


def staged(target, source):
    target[...] = jnp.zeros_like(target)
    target[:QUART, :] = source
    return target


def pass_kernel(where, q, out):
    out[...] = q[...]


def partial_rows(q_right, q_left, kv_right, kv_left, from_right, from_left, out, att, logs, q_rows, kv_rows):
    q = [staged(q_rows.at[i], part) for i, part in enumerate((q_right, q_left))]
    keys = [staged(kv_rows.at[i], part[...]) for i, part in enumerate((kv_right, from_right, kv_left, from_left))]
    calls, places = lat_side_calls(q, [[(keys[2 * s], 0), (keys[2 * s + 1], 0)] for s in range(2)])
    outs, sums = attention(calls, with_logs=True)
    head = iota((1, LOGS), 1) & 7
    for n in range(4):
        column = jnp.zeros((QWIN, LOGS), jnp.float32)
        for half in range(2):
            rows, cols = places[2 * n + half]
            att[rows, cols] = outs[2 * n + half]
            for h in range(4):
                part = sums[2 * n + half][h * QWIN : (h + 1) * QWIN]
                column = jnp.where(head == 4 * half + h, part, column)
        high = column.astype(jnp.bfloat16).astype(jnp.float32)
        rest = column - high
        middle = rest.astype(jnp.bfloat16).astype(jnp.float32)
        third = iota((1, LOGS), 1) >> 3
        parts = jnp.where(third == 0, high, jnp.where(third == 1, middle, rest - middle))
        logs[rows, :] = parts.astype(jnp.bfloat16)
    to_cell = cells_from_queries()
    out[:, :HD] = dot(to_cell, att[...]).astype(jnp.bfloat16)
    out[:, HD:] = dot(to_cell, logs[...]).astype(jnp.bfloat16)


def own_kernel(where, q_right, q_left, *refs):
    partial_rows(q_right[...], q_left[...], *refs)


def foreign_kernel(where, q_first, q_right, q_left, *refs):
    q = [jnp.where(where[0] >= 4, q_first[i], part[...]) for i, part in enumerate((q_right, q_left))]
    partial_rows(*q, *refs)


def near_kernel(
    where, q, kv_right, kv_left, from_right, from_left, lat, first, w_out, out, att, done, q_rows, kv_rows
):
    q = [staged(q_rows.at[i], q[i]) for i in range(2)]
    keys = [staged(kv_rows.at[i], part[...]) for i, part in enumerate((kv_right, from_right, kv_left, from_left))]
    sources = [
        [(keys[2 * s], 0), (keys[2 * s + 1], 0), (lat, QUART * s), (lat, HALF + QUART * s)] for s in range(2)
    ]
    calls, places = lat_side_calls(q, sources)
    for (rows, cols), result in zip(places, attention(calls)[0]):
        att[rows, cols] = result
    placed = dot(cells_from_queries(), att[...]).astype(jnp.bfloat16)
    rows = pl.ds(pl.multiple_of(HALF * (1 - (where[0] & 1)), 16), HALF)
    done[...] = first[rows, :].astype(jnp.float32) + dot(placed, w_out[...])
    for i in range(CELLS // 2):
        out[i] = done[i * LEVELS : (i + 1) * LEVELS, :].astype(jnp.bfloat16)


def gate_kernel(where, mine, theirs, out):
    position = where[0] & 3
    log_row = iota((2 * LOGS, HD), 0)
    part = log_row & (LOGS - 1)
    same_head = (part < 24) & ((part & 7) == iota((2 * LOGS, HD), 1) // HEAD)
    to_lanes = jnp.where(same_head, jnp.where(log_row < LOGS, 1.0, -1.0), 0.0).astype(jnp.bfloat16)
    gap = dot(jnp.concatenate([mine[:, HD:], theirs[:, HD:]], axis=1), to_lanes)
    alone = (position == 0) | (position == 3)
    gate = jnp.where(alone, 0.0, 1.0 / (1.0 + jnp.exp(gap)))
    own = mine[:, :HD].astype(jnp.float32)
    out[...] = (own + (theirs[:, :HD].astype(jnp.float32) - own) * gate).astype(jnp.bfloat16)


def merge_kernel(where, att, first, w_out, near, out, done, staged, sems):
    position = where[0] & 3
    far = position & 1
    copy = pltpu.make_async_copy(
        near, out.at[pl.ds((1 - far) * (CELLS // 2), CELLS // 2)], sems.at[0]
    )
    copy.start()
    rows = pl.ds(pl.multiple_of(HALF * far, 16), HALF)
    done[...] = first[rows, :].astype(jnp.float32) + dot(att[...], w_out[...])
    for i in range(CELLS // 2):
        staged[i] = done[i * LEVELS : (i + 1) * LEVELS, :].astype(jnp.bfloat16)
    far_copy = pltpu.make_async_copy(
        staged, out.at[pl.ds(far * (CELLS // 2), CELLS // 2)], sems.at[1]
    )
    far_copy.start()
    copy.wait()
    far_copy.wait()


def shape(*dims):
    return jax.ShapeDtypeStruct(dims, jnp.bfloat16)


def vmem(*dims):
    return pltpu.VMEM(dims, jnp.bfloat16)


def in_hbm(array):
    return pltpu.with_memory_space_constraint(array, pltpu.HBM)


ANY = pl.BlockSpec(memory_space=pl.ANY)
WHOLE = pl.BlockSpec(memory_space=pltpu.VMEM)
SCALARS = pl.BlockSpec(memory_space=pltpu.SMEM)


def call(kernel, ins, outs, scratch, flops, name, out_spec=WHOLE, limit=40):
    return pl.pallas_call(
        kernel,
        out_shape=outs,
        in_specs=[SCALARS, *ins],
        out_specs=jax.tree.map(lambda _: out_spec, outs),
        scratch_shapes=scratch,
        compiler_params=pltpu.CompilerParams(vmem_limit_bytes=limit * 1024 * 1024),
        cost_estimate=pl.CostEstimate(flops=flops, bytes_accessed=flops // 500, transcendentals=0),
        name=name,
    )


def right_side(where, cells, w_qkv, w_out):
    return call(
        right_kernel,
        [ANY] * 3,
        (
            shape(QUART, D), shape(QUART, D), shape(HALF, D), shape(SIDE, D), shape(SIDE, D), shape(SIDE, D),
            shape(2 * SIDE, D), shape(D, HD), shape(HD, D), shape(2, D, HD), shape(D, HD), shape(HD, D),
        ),
        [
            vmem(CELLS, LEVELS, D), pltpu.VMEM((OWN, D), jnp.float32), vmem(SIDE, D), vmem(2 * SIDE, D),
            vmem(SIDE, HD), vmem(SIDE, D), vmem(2, D, HD), pltpu.SemaphoreType.DMA((9,)),
        ],
        2_000_000_000,
        "right_side",
    )(where, in_hbm(cells), in_hbm(w_qkv), in_hbm(w_out))


def left_side(*args):
    return call(
        left_kernel,
        [WHOLE] * 8,
        (shape(QUART, D), shape(QUART, D), shape(HALF, D), shape(SIDE, D), shape(2, QUART, HD)),
        [vmem(SIDE, HD), vmem(SIDE, D)],
        2_000_000_000,
        "left_side",
    )(*args)


def late_queries(*args):
    outs = (shape(QUART, HD), shape(QUART, HD))
    return call(late_kernel, [WHOLE] * 4, outs, [], 200_000_000, "late_queries")(*args)


def residual(*args):
    outs = (shape(OWN, D), shape(2, QUART, HD))
    return call(residual_kernel, [WHOLE] * 5, outs, [], 2000001000, "residual")(*args)


def passed(*args):
    return call(pass_kernel, [WHOLE], shape(2, QUART, HD), [], 1_500_000_000, "passed")(*args)


def taken(*args):
    return call(pass_kernel, [WHOLE], shape(QUART, D), [], 1_500_000_000, "taken")(*args)


def partial(name, kernel, *args):
    return call(
        kernel,
        [WHOLE] * (len(args) - 1),
        shape(HALF, HD + LOGS),
        [vmem(4 * QWIN, HD), vmem(4 * QWIN, LOGS), vmem(2, WIN, HD), vmem(4, WIN, D)],
        20_000_000,
        name,
    )(*args)


DONE = pltpu.VMEM((HALF, D), jnp.float32)


def near_rows(*args):
    return call(
        near_kernel,
        [WHOLE] * 8,
        shape(CELLS // 2, LEVELS, D),
        [vmem(4 * QWIN, HD), DONE, vmem(2, WIN, HD), vmem(4, WIN, D)],
        2000000000,
        "near_rows",
    )(*args)


def gate(*args):
    return call(gate_kernel, [WHOLE] * 2, shape(HALF, HD), [], 6000000000, "gate")(*args)


def merge(*args):
    return call(
        merge_kernel,
        [WHOLE] * 4,
        shape(CELLS, LEVELS, D),
        [DONE, vmem(CELLS // 2, LEVELS, D), pltpu.SemaphoreType.DMA((2,))],
        2_000_000_000,
        "merge",
        out_spec=ANY,
    )(*args)


def per_device(tokens, w_qkv, w_out):
    lons, lats = lax.axis_size("lon"), lax.axis_size("lat")
    starts_run = (lax.axis_index("lon") % RUN == 0).astype(jnp.int32)
    where = (lax.axis_index("lat").astype(jnp.int32) + 4 * starts_run)[None]
    cells = tokens.transpose(1, 2, 0, 3).reshape(CELLS, LEVELS, D)

    right_far, right_near, wire_right, first_right, *rest = right_side(where, cells, w_qkv, w_out)
    up = [(i, (i + 1) % lons) for i in range(lons)]
    down = [(j, i) for i, j in up]
    left_recv = lax.ppermute(right_far, "lon", up)
    *rest, w_out1 = rest
    left_far, left_near, wire_left, first_left, q_first = left_side(where, wire_right, *rest)
    w_q1 = rest[-1]
    partner = [i + 1 if i % 2 else i - 1 for i in range(lats)]
    partner[0], partner[-1] = 0, lats - 1
    first_pairs, other_pairs = [], []
    for i in range(lons):
        for j in range(lats):
            one, other = (first_pairs, other_pairs) if i % RUN == 0 else (other_pairs, first_pairs)
            one.append((i * lats + j, i * lats + partner[j]))
            other.append((i * lats + j, i * lats + j))
    foreign_first = lax.ppermute(q_first, ("lon", "lat"), first_pairs)
    right_recv = lax.ppermute(left_far, "lon", down)
    left_recv_near = lax.ppermute(right_near, "lon", up)
    right_recv_near = lax.ppermute(left_near, "lon", down)
    q_late, left_recv = lax.optimization_barrier((q_first, left_recv))
    q_far = late_queries(where, q_late, wire_right, wire_left, w_q1)
    foreign = lax.ppermute(jnp.stack(q_far), ("lon", "lat"), other_pairs)
    foreign = [foreign[0], foreign[1]]

    left_recv = taken(where, left_recv)
    foreign_first, left_recv = lax.optimization_barrier((foreign_first, left_recv))
    q_first = passed(where, foreign_first)
    q_first, left_recv, right_recv, *foreign = lax.optimization_barrier((q_first, left_recv, right_recv, *foreign))
    keys = [right_far, left_far, right_recv, left_recv]
    far_pairs = [pair for i in range(1, lats - 1, 2) for pair in ((i, i + 1), (i + 1, i))]
    theirs = partial("foreign_rows", foreign_kernel, where, q_first, *foreign, *keys)
    after = (theirs, first_left, left_recv_near, right_recv_near)
    _, first_left, left_recv_near, right_recv_near = lax.optimization_barrier(after)
    theirs = lax.ppermute(theirs, "lat", far_pairs)
    near_keys = [right_near, left_near, right_recv_near, left_recv_near]
    from_near = lax.ppermute(jnp.concatenate(near_keys, axis=0), "lat", [(i, i ^ 1) for i in range(lats)])
    mine = partial("own_rows", own_kernel, where, *q_far, *keys)
    first, q_near = residual(where, first_right, first_left, wire_right, wire_left, w_q1)
    near = near_rows(where, q_near, *near_keys, from_near, first, w_out1)
    out = merge(where, gate(where, mine, theirs), first, w_out1, near)
    return out.reshape(ROWS, COLS, LEVELS, D).transpose(2, 0, 1, 3)


def solution(mesh):
    return jax.shard_map(
        per_device,
        mesh=mesh,
        in_specs=(P(None, "lat", "lon", None), P(), P()),
        out_specs=P(None, "lat", "lon", None),
        check_vma=False,
    )
```

```python
import jax
import jax.numpy as jnp
from jax import lax
from jax.experimental import pallas as pl
from jax.experimental.pallas import tpu as pltpu
from jax.sharding import PartitionSpec as P

LEVELS, ROWS, COLS, D = 4, 6, 12, 1024
HD, HEAD = 512, 64
CELLS = ROWS * COLS
OWN = LEVELS * CELLS
HALF = OWN // 2
QUART = HALF // 2
UNIT = 36
WIN = 80
SIDE = 2 * WIN
QWIN = 48
KWIN = 64
NEG = -1e30
LOGS = 128
RUN = 8


def at_least(index, *bounds):
    return sum(jnp.where(index >= bound, 1, 0) for bound in bounds)


def cell_of_window(index):
    side = at_least(index, SIDE)
    index = index - SIDE * side
    pair = at_least(index, WIN)
    index = index - WIN * pair
    valid = index < 2 * UNIT
    level = at_least(index, UNIT)
    index = index - UNIT * level
    row = at_least(index, *range(6, UNIT, 6))
    cell = (row * COLS + 6 * (1 - side) + index - 6 * row) * LEVELS + 2 * pair + level
    return jnp.where(valid, cell, -1)


def split_unit(index, group):
    lev = at_least(index, UNIT // 2)
    index = index - UNIT // 2 * lev
    row = at_least(index, 6, 12)
    return jnp.where(group == 0, 1 + lev, 3 - 3 * lev), row, index - 6 * row


def window_of_wire(index, lat_odd):
    k = at_least(index, UNIT, 2 * UNIT, 3 * UNIT)
    level, row, col = split_unit(index - UNIT * k, k & 1)
    row = row + 3 * ((k >> 1) ^ lat_odd)
    return WIN * (level >> 1) + UNIT * (level & 1) + 6 * row + col


def cell_of_unit(n, index):
    level, row, col = split_unit(index, n & 1)
    return (row * COLS + 6 * (1 - (n >> 1)) + col) * LEVELS + level


def query_start(k):
    return k * UNIT // 16 * 16


def key_start(first, size):
    return min(first // 16 * 16, size - KWIN)


def iota(shape, axis):
    return lax.broadcasted_iota(jnp.int32, shape, axis)


def one_hot(rows, lanes):
    return jnp.where(rows == lanes, 1.0, 0.0).astype(jnp.bfloat16)


def layer_normed(values):
    centre = values - jnp.mean(values, axis=-1, keepdims=True)
    spread = jnp.mean(centre * centre, axis=-1, keepdims=True)
    return (centre * lax.rsqrt(spread + 1e-05)).astype(jnp.bfloat16)


def dot(a, b):
    return jnp.dot(a, b, preferred_element_type=jnp.float32)


def cells_from_queries():
    index = iota((1, 4 * QWIN), 1)
    n = at_least(index, QWIN, 2 * QWIN, 3 * QWIN)
    index = index - (QWIN + 4) * n
    cell = jnp.where((index >= 0) & (index < UNIT), cell_of_unit(n, index), -1)
    return one_hot(iota((HALF, 4 * QWIN), 0), cell)


def spread_heads(queries):
    head_of = iota((1, 4 * HEAD), 1) // HEAD
    queries = queries * jnp.bfloat16(0.125)
    return jnp.concatenate(
        [jnp.where(head_of == h, queries, jnp.bfloat16(0)) for h in range(4)], axis=0
    )


def attention(calls, with_logs=False):
    head_of = iota((1, 4 * HEAD), 1) // HEAD
    scores = []
    for queries, keys, _, bias in calls:
        product = lax.dot_general(
            queries, keys, (((1,), (1,)), ((), ())), preferred_element_type=jnp.float32
        )
        scores.append(product + bias)
    highest = [jnp.max(s, axis=-1, keepdims=True) for s in scores]
    raised = [jnp.exp(s - h) for s, h in zip(scores, highest)]
    mixed = [dot(r.astype(jnp.bfloat16), call[2]) for r, call in zip(raised, calls)]
    outs, logs = [], []
    for r, m, high in zip(raised, mixed, highest):
        total = jnp.sum(r, axis=-1, keepdims=True)
        m = m * (1.0 / total)
        rows = m.shape[0] // 4
        out = m[:rows]
        for h in range(1, 4):
            out = jnp.where(head_of == h, m[h * rows : (h + 1) * rows], out)
        outs.append(out.astype(jnp.bfloat16))
        logs.append(high + jnp.log(total) if with_logs else None)
    return outs, logs


def side_block(lat_odd, x, normed, kv, w_q, w_out, w_kv, first_out, wire_out, kv_out, att, scratch, ready):
    for i in range(4):
        ready(i)
    queries = dot(normed, w_q[...]).astype(jnp.bfloat16)
    bias = jnp.where(iota((1, 2 * WIN), 1) % WIN < 2 * UNIT, 0.0, NEG).astype(jnp.float32)
    calls, places = [], []
    for pair in range(2):
        rows = slice(pair * WIN, (pair + 1) * WIN)
        far = slice(SIDE + pair * WIN, SIDE + (pair + 1) * WIN)
        for half in range(2):
            cols = slice(half * 256, half * 256 + 256)
            cols_v = slice(HD + half * 256, HD + half * 256 + 256)
            places.append((rows, cols))
            calls.append(
                (
                    spread_heads(queries[rows, cols]),
                    jnp.concatenate([kv[rows, cols], kv[far, cols]], axis=0),
                    jnp.concatenate([kv[rows, cols_v], kv[far, cols_v]], axis=0),
                    bias,
                )
            )
    for (rows, cols), out in zip(places, attention(calls)[0]):
        att[rows, cols] = out
    to_wire = one_hot(window_of_wire(iota((HALF, 1), 0), lat_odd), iota((HALF, SIDE), 1))
    first = (x[...].astype(jnp.float32) + dot(att[...], w_out[...])).astype(jnp.bfloat16)
    first_out[...] = first
    scratch[...] = layer_normed(first.astype(jnp.float32))
    wire = dot(to_wire, scratch[...]).astype(jnp.bfloat16)
    wire_out[...] = wire
    for i in range(2):
        kv_out[:, i * HD : (i + 1) * HD] = dot(wire, w_kv[i]).astype(jnp.bfloat16)


def right_kernel(
    where, x_hbm, w_qkv_hbm, w_out_hbm,
    kv_out, wire_out, first_out, x_left, normed_left, kv0, w_q, w_out, w_kv, w_q1, w_out1,
    x_in, x, x_right, normed, att, scratch, w_kv0, sems,
):
    def part(block, i):
        return w_qkv_hbm.at[block, :, pl.ds(i * HD, HD)]

    pairs = [
        (x_hbm, x_in), (part(0, 1), w_kv0.at[0]), (part(0, 2), w_kv0.at[1]), (part(0, 0), w_q),
        (w_out_hbm.at[0], w_out), (part(1, 1), w_kv.at[0]), (part(1, 2), w_kv.at[1]), (part(1, 0), w_q1),
        (w_out_hbm.at[1], w_out1),
    ]
    copies = [pltpu.make_async_copy(src, dst, sems.at[i]) for i, (src, dst) in enumerate(pairs)]
    for copy in copies:
        copy.start()
    lat_odd = where[0] & 1
    rows = 2 * SIDE
    to_window = one_hot(cell_of_window(iota((rows, 1), 0)), iota((rows, OWN), 1))
    copies[0].wait()
    for i in range(CELLS):
        x[i * LEVELS : (i + 1) * LEVELS, :] = x_in[i].astype(jnp.float32)
    cells = x[...].astype(jnp.bfloat16)
    ordered = dot(to_window, cells)
    x_right[...] = ordered[:SIDE].astype(jnp.bfloat16)
    x_left[...] = ordered[SIDE:].astype(jnp.bfloat16)
    for i in range(4):
        span = slice(i * WIN, (i + 1) * WIN)
        normed[span, :] = layer_normed(ordered[span])
    normed_left[...] = normed[SIDE:, :]
    copies[1].wait()
    copies[2].wait()
    for i in range(2):
        kv0[:, i * HD : (i + 1) * HD] = dot(normed[...], w_kv0[i]).astype(jnp.bfloat16)
    side_block(
        lat_odd, x_right, normed[:SIDE, :], kv0, w_q, w_out, w_kv, first_out, wire_out, kv_out, att, scratch,
        lambda i: copies[3 + i].wait(),
    )
    copies[7].wait()
    copies[8].wait()


def left_kernel(
    where, wire_right, x, normed, kv0, w_q, w_out, w_kv, w_q1,
    kv_out, wire_out, first_out, q_far, att, scratch,
):
    side_block(
        where[0] & 1, x, normed[...], kv0, w_q, w_out, w_kv, first_out, wire_out, kv_out, att, scratch,
        lambda i: None,
    )
    q_far[...] = jnp.zeros_like(q_far)

    @pl.when(where[0] >= 4)
    def _():
        far_queries(wire_right, wire_out, w_q1, q_far)


def far_queries(wire_right, wire_left, w_q1, q_far):
    for side, wire in enumerate((wire_right, wire_left)):
        q_far[side] = dot(wire[:QUART, :], w_q1[...]).astype(jnp.bfloat16)


def late_kernel(where, q_first, wire_right, wire_left, w_q1, q_far):
    @pl.when(where[0] >= 4)
    def _():
        q_far[...] = q_first[...]

    @pl.when(where[0] < 4)
    def _():
        far_queries(wire_right, wire_left, w_q1, q_far)


def residual_kernel(where, first_right, first_left, wire_right, wire_left, w_q1, first_out, q_near):
    for side, wire in enumerate((wire_right, wire_left)):
        q_near[side] = dot(wire[...], w_q1[...])[QUART:].astype(jnp.bfloat16)
    to_cell = one_hot(iota((OWN, 2 * SIDE), 0), cell_of_window(iota((1, 2 * SIDE), 1)))
    first = jnp.concatenate([first_right[...], first_left[...]], axis=0)
    first_out[...] = dot(to_cell, first).astype(jnp.bfloat16)


def lat_side_calls(q, side_sources):
    calls, places = [], []
    for n in range(4):
        group = n & 1
        sources = side_sources[n >> 1]
        lanes = KWIN * len(sources)
        row = iota((QWIN, lanes), 0)
        lane = iota((QWIN, lanes), 1)
        firsts = [first + UNIT * group for _, first in sources]
        starts = [key_start(f, s.shape[0]) for f, (s, _) in zip(firsts, sources)]
        late = row >= 4 * n + UNIT // 2
        valid = jnp.zeros((QWIN, lanes), jnp.bool_)
        for i in range(len(sources)):
            at = lane - (i * KWIN + firsts[i] - starts[i])
            inside = (at >= 0) & (at < UNIT)
            if group == 1:
                inside = inside & ((at >= UNIT // 2) == late)
            valid = valid | inside
        bias = jnp.where(valid, 0.0, NEG).astype(jnp.float32)
        bias = jnp.concatenate([bias] * 4, axis=0)
        start = query_start(n)
        for half in range(2):

            def window(base):
                lanes = slice(base + half * 256, base + half * 256 + 256)
                parts = [s[f : f + KWIN, lanes] for (s, _), f in zip(sources, starts)]
                return jnp.concatenate(parts, axis=0)

            cols = slice(half * 256, half * 256 + 256)
            places.append((slice(n * QWIN, (n + 1) * QWIN), cols))
            calls.append((spread_heads(q[start : start + QWIN, cols]), window(0), window(HD), bias))
    return calls, places


def pass_kernel(where, q, out):
    out[...] = q[...]


def partial_rows(q, kv_right, kv_left, from_right, from_left, out, att):
    calls, places = lat_side_calls(q, [[(kv_right, 0), (from_right, 0)], [(kv_left, 0), (from_left, 0)]])
    outs, sums = attention(calls, with_logs=True)
    head = iota((1, LOGS), 1) & 7
    for n in range(4):
        column = jnp.zeros((QWIN, LOGS), jnp.float32)
        for half in range(2):
            rows, cols = places[2 * n + half]
            att[rows, cols] = outs[2 * n + half]
            for h in range(4):
                part = sums[2 * n + half][h * QWIN : (h + 1) * QWIN]
                column = jnp.where(head == 4 * half + h, part, column)
        high = column.astype(jnp.bfloat16).astype(jnp.float32)
        rest = column - high
        middle = rest.astype(jnp.bfloat16).astype(jnp.float32)
        third = iota((1, LOGS), 1) >> 3
        parts = jnp.where(third == 0, high, jnp.where(third == 1, middle, rest - middle))
        att[rows, HD:] = parts.astype(jnp.bfloat16)
    to_cell = cells_from_queries()
    out[...] = dot(to_cell, att[...]).astype(jnp.bfloat16)


def own_kernel(where, *refs):
    partial_rows(*refs)


def foreign_kernel(where, q_first, q_other, *refs):
    partial_rows(jnp.where(where[0] >= 4, q_first[...], q_other[...]), *refs)


def near_kernel(where, q, kv_right, kv_left, from_right, from_left, lat, first, w_out, out, att, done):
    own = ((kv_right, from_right), (kv_left, from_left))
    sources = [
        [(own[s][0], QUART), (own[s][1], QUART), (lat, QUART * s), (lat, HALF + QUART * s)] for s in range(2)
    ]
    calls, places = lat_side_calls(q, sources)
    for (rows, cols), result in zip(places, attention(calls)[0]):
        att[rows, cols] = result
    placed = dot(cells_from_queries(), att[...]).astype(jnp.bfloat16)
    rows = pl.ds(pl.multiple_of(HALF * (1 - (where[0] & 1)), 16), HALF)
    done[...] = first[rows, :].astype(jnp.float32) + dot(placed, w_out[...])
    for i in range(CELLS // 2):
        out[i] = done[i * LEVELS : (i + 1) * LEVELS, :].astype(jnp.bfloat16)


def merge_kernel(where, mine, theirs, first, w_out, near, out, done, staged, sems):
    position = where[0] & 3
    far = position & 1
    copy = pltpu.make_async_copy(
        near, out.at[pl.ds((1 - far) * (CELLS // 2), CELLS // 2)], sems.at[0]
    )
    copy.start()
    log_row = iota((2 * LOGS, HD), 0)
    part = log_row & (LOGS - 1)
    same_head = (part < 24) & ((part & 7) == iota((2 * LOGS, HD), 1) // HEAD)
    to_lanes = jnp.where(same_head, jnp.where(log_row < LOGS, 1.0, -1.0), 0.0).astype(jnp.bfloat16)
    gap = dot(jnp.concatenate([mine[:, HD:], theirs[:, HD:]], axis=1), to_lanes)
    alone = (position == 0) | (position == 3)
    gate = jnp.where(alone, 0.0, 1.0 / (1.0 + jnp.exp(gap)))
    own = mine[:, :HD].astype(jnp.float32)
    att = (own + (theirs[:, :HD].astype(jnp.float32) - own) * gate).astype(jnp.bfloat16)
    rows = pl.ds(pl.multiple_of(HALF * far, 16), HALF)
    done[...] = first[rows, :].astype(jnp.float32) + dot(att, w_out[...])
    for i in range(CELLS // 2):
        staged[i] = done[i * LEVELS : (i + 1) * LEVELS, :].astype(jnp.bfloat16)
    far_copy = pltpu.make_async_copy(
        staged, out.at[pl.ds(far * (CELLS // 2), CELLS // 2)], sems.at[1]
    )
    far_copy.start()
    copy.wait()
    far_copy.wait()


def shape(*dims):
    return jax.ShapeDtypeStruct(dims, jnp.bfloat16)


def vmem(*dims):
    return pltpu.VMEM(dims, jnp.bfloat16)


def in_hbm(array):
    return pltpu.with_memory_space_constraint(array, pltpu.HBM)


ANY = pl.BlockSpec(memory_space=pl.ANY)
WHOLE = pl.BlockSpec(memory_space=pltpu.VMEM)
SCALARS = pl.BlockSpec(memory_space=pltpu.SMEM)


def call(kernel, ins, outs, scratch, flops, name, out_spec=WHOLE, limit=40):
    return pl.pallas_call(
        kernel,
        out_shape=outs,
        in_specs=[SCALARS, *ins],
        out_specs=jax.tree.map(lambda _: out_spec, outs),
        scratch_shapes=scratch,
        compiler_params=pltpu.CompilerParams(vmem_limit_bytes=limit * 1024 * 1024),
        cost_estimate=pl.CostEstimate(flops=flops, bytes_accessed=4_000_000, transcendentals=0),
        name=name,
    )


def right_side(where, cells, w_qkv, w_out):
    return call(
        right_kernel,
        [ANY] * 3,
        (
            shape(HALF, D), shape(HALF, D), shape(SIDE, D), shape(SIDE, D), shape(SIDE, D),
            shape(2 * SIDE, D), shape(D, HD), shape(HD, D), shape(2, D, HD), shape(D, HD), shape(HD, D),
        ),
        [
            vmem(CELLS, LEVELS, D), pltpu.VMEM((OWN, D), jnp.float32), vmem(SIDE, D), vmem(2 * SIDE, D),
            vmem(SIDE, HD), vmem(SIDE, D), vmem(2, D, HD), pltpu.SemaphoreType.DMA((9,)),
        ],
        2_000_000_000,
        "right_side",
    )(where, in_hbm(cells), in_hbm(w_qkv), in_hbm(w_out))


def left_side(*args):
    return call(
        left_kernel,
        [WHOLE] * 8,
        (shape(HALF, D), shape(HALF, D), shape(SIDE, D), shape(2, QUART, HD)),
        [vmem(SIDE, HD), vmem(SIDE, D)],
        2_000_000_000,
        "left_side",
    )(*args)


def late_queries(*args):
    return call(late_kernel, [WHOLE] * 4, shape(2, QUART, HD), [], 200_000_000, "late_queries")(*args)


def residual(*args):
    outs = (shape(OWN, D), shape(2, QUART, HD))
    return call(residual_kernel, [WHOLE] * 5, outs, [], 1_000_000_000, "residual")(*args)


def passed(*args):
    return call(pass_kernel, [WHOLE], shape(HALF, HD), [], 2_500_000_000, "passed")(*args)


def partial(name, kernel, *args):
    return call(
        kernel,
        [WHOLE] * (len(args) - 1),
        shape(HALF, HD + LOGS),
        [vmem(4 * QWIN, HD + LOGS)],
        1_000_000_000,
        name,
    )(*args)


DONE = pltpu.VMEM((HALF, D), jnp.float32)


def near_rows(*args):
    return call(
        near_kernel,
        [WHOLE] * 8,
        shape(CELLS // 2, LEVELS, D),
        [vmem(4 * QWIN, HD), DONE],
        2_000_000_000,
        "near_rows",
    )(*args)


def merge(*args):
    return call(
        merge_kernel,
        [WHOLE] * 5,
        shape(CELLS, LEVELS, D),
        [DONE, vmem(CELLS // 2, LEVELS, D), pltpu.SemaphoreType.DMA((2,))],
        2_000_000_000,
        "merge",
        out_spec=ANY,
    )(*args)


def per_device(tokens, w_qkv, w_out):
    lons, lats = lax.axis_size("lon"), lax.axis_size("lat")
    starts_run = (lax.axis_index("lon") % RUN == 0).astype(jnp.int32)
    where = (lax.axis_index("lat").astype(jnp.int32) + 4 * starts_run)[None]
    cells = tokens.transpose(1, 2, 0, 3).reshape(CELLS, LEVELS, D)

    kv_right, wire_right, first_right, *rest = right_side(where, cells, w_qkv, w_out)
    from_left = lax.ppermute(kv_right, "lon", [(i, (i + 1) % lons) for i in range(lons)])
    *rest, w_out1 = rest
    kv_left, wire_left, first_left, q_first = left_side(where, wire_right, *rest)
    w_q1 = rest[-1]
    partner = [i + 1 if i % 2 else i - 1 for i in range(lats)]
    partner[0], partner[-1] = 0, lats - 1
    first_pairs, other_pairs = [], []
    for i in range(lons):
        for j in range(lats):
            one, other = (first_pairs, other_pairs) if i % RUN == 0 else (other_pairs, first_pairs)
            one.append((i * lats + j, i * lats + partner[j]))
            other.append((i * lats + j, i * lats + j))
    foreign_first = lax.ppermute(q_first, ("lon", "lat"), first_pairs).reshape(HALF, HD)
    from_right = lax.ppermute(kv_left, "lon", [(i, (i - 1) % lons) for i in range(lons)])
    q_far = late_queries(where, q_first, wire_right, wire_left, w_q1).reshape(HALF, HD)
    foreign = lax.ppermute(q_far, ("lon", "lat"), other_pairs)

    foreign_first, from_left = lax.optimization_barrier((foreign_first, from_left))
    q_first = passed(where, foreign_first)
    received = (first_left, q_first, from_left, from_right, foreign)
    first_left, q_first, from_left, from_right, foreign = lax.optimization_barrier(received)

    keys = [kv_right, kv_left, from_right, from_left]
    far_pairs = [pair for i in range(1, lats - 1, 2) for pair in ((i, i + 1), (i + 1, i))]
    theirs = partial("foreign_rows", foreign_kernel, where, q_first, foreign, *keys)
    theirs = lax.ppermute(theirs, "lat", far_pairs)
    to_near = jnp.concatenate([p[QUART:] for p in keys], axis=0)
    from_near = lax.ppermute(to_near, "lat", [(i, i ^ 1) for i in range(lats)])
    mine = partial("own_rows", own_kernel, where, q_far, *keys)
    first, q_near = residual(where, first_right, first_left, wire_right, wire_left, w_q1)
    near = near_rows(where, q_near.reshape(HALF, HD), *keys, from_near, first, w_out1)
    out = merge(where, mine, theirs, first, w_out1, near)
    return out.reshape(ROWS, COLS, LEVELS, D).transpose(2, 0, 1, 3)


def solution(mesh):
    return jax.shard_map(
        per_device,
        mesh=mesh,
        in_specs=(P(None, "lat", "lon", None), P(), P()),
        out_specs=P(None, "lat", "lon", None),
        check_vma=False,
    )
```

```python
import jax
import jax.numpy as jnp
from jax import lax
from jax.experimental import pallas as pl
from jax.experimental.pallas import tpu as pltpu
from jax.sharding import PartitionSpec as P

LEVELS, ROWS, COLS, D = 4, 6, 12, 1024
HD, HEAD = 512, 64
CELLS = ROWS * COLS
OWN = LEVELS * CELLS
HALF = OWN // 2
QUART = HALF // 2
UNIT = 36
WIN = 80
SIDE = 2 * WIN
QWIN = 48
KWIN = 64
NEG = -1e30
LOGS = 128
RUN = 8


def at_least(index, *bounds):
    return sum(jnp.where(index >= bound, 1, 0) for bound in bounds)


def cell_of_window(index):
    side = at_least(index, SIDE)
    index = index - SIDE * side
    pair = at_least(index, WIN)
    index = index - WIN * pair
    valid = index < 2 * UNIT
    level = at_least(index, UNIT)
    index = index - UNIT * level
    row = at_least(index, *range(6, UNIT, 6))
    cell = (row * COLS + 6 * (1 - side) + index - 6 * row) * LEVELS + 2 * pair + level
    return jnp.where(valid, cell, -1)


def split_unit(index, group):
    lev = at_least(index, UNIT // 2)
    index = index - UNIT // 2 * lev
    row = at_least(index, 6, 12)
    return jnp.where(group == 0, 1 + lev, 3 - 3 * lev), row, index - 6 * row


def window_of_wire(index, lat_odd):
    k = at_least(index, UNIT, 2 * UNIT, 3 * UNIT)
    level, row, col = split_unit(index - UNIT * k, k & 1)
    row = row + 3 * ((k >> 1) ^ lat_odd)
    return WIN * (level >> 1) + UNIT * (level & 1) + 6 * row + col


def cell_of_unit(n, index):
    level, row, col = split_unit(index, n & 1)
    return (row * COLS + 6 * (1 - (n >> 1)) + col) * LEVELS + level


def query_start(k):
    return k * UNIT // 16 * 16


def key_start(first, size):
    return min(first // 16 * 16, size - KWIN)


def iota(shape, axis):
    return lax.broadcasted_iota(jnp.int32, shape, axis)


def one_hot(rows, lanes):
    return jnp.where(rows == lanes, 1.0, 0.0).astype(jnp.bfloat16)


def layer_normed(values):
    centre = values - jnp.mean(values, axis=-1, keepdims=True)
    spread = jnp.mean(centre * centre, axis=-1, keepdims=True)
    return (centre * lax.rsqrt(spread + 1e-05)).astype(jnp.bfloat16)


def dot(a, b):
    return jnp.dot(a, b, preferred_element_type=jnp.float32)


def cells_from_queries():
    index = iota((1, 4 * QWIN), 1)
    n = at_least(index, QWIN, 2 * QWIN, 3 * QWIN)
    index = index - (QWIN + 4) * n
    cell = jnp.where((index >= 0) & (index < UNIT), cell_of_unit(n, index), -1)
    return one_hot(iota((HALF, 4 * QWIN), 0), cell)


def spread_heads(queries):
    head_of = iota((1, 4 * HEAD), 1) // HEAD
    queries = queries * jnp.bfloat16(0.125)
    return jnp.concatenate(
        [jnp.where(head_of == h, queries, jnp.bfloat16(0)) for h in range(4)], axis=0
    )


def attention(calls, with_logs=False):
    head_of = iota((1, 4 * HEAD), 1) // HEAD
    scores = []
    for queries, keys, _, bias in calls:
        product = lax.dot_general(
            queries, keys, (((1,), (1,)), ((), ())), preferred_element_type=jnp.float32
        )
        scores.append(product + bias)
    highest = [jnp.max(s, axis=-1, keepdims=True) for s in scores]
    raised = [jnp.exp(s - h) for s, h in zip(scores, highest)]
    mixed = [dot(r.astype(jnp.bfloat16), call[2]) for r, call in zip(raised, calls)]
    outs, logs = [], []
    for r, m, high in zip(raised, mixed, highest):
        total = jnp.sum(r, axis=-1, keepdims=True)
        m = m * (1.0 / total)
        rows = m.shape[0] // 4
        out = m[:rows]
        for h in range(1, 4):
            out = jnp.where(head_of == h, m[h * rows : (h + 1) * rows], out)
        outs.append(out.astype(jnp.bfloat16))
        logs.append(high + jnp.log(total) if with_logs else None)
    return outs, logs


def side_block(lat_odd, x, normed, kv, w_q, w_out, w_kv, first_out, wire_out, kv_out, att, scratch, ready):
    for i in range(4):
        ready(i)
    queries = dot(normed, w_q[...]).astype(jnp.bfloat16)
    bias = jnp.where(iota((1, 2 * WIN), 1) % WIN < 2 * UNIT, 0.0, NEG).astype(jnp.float32)
    calls, places = [], []
    for pair in range(2):
        rows = slice(pair * WIN, (pair + 1) * WIN)
        far = slice(SIDE + pair * WIN, SIDE + (pair + 1) * WIN)
        for half in range(2):
            cols = slice(half * 256, half * 256 + 256)
            cols_v = slice(HD + half * 256, HD + half * 256 + 256)
            places.append((rows, cols))
            calls.append(
                (
                    spread_heads(queries[rows, cols]),
                    jnp.concatenate([kv[rows, cols], kv[far, cols]], axis=0),
                    jnp.concatenate([kv[rows, cols_v], kv[far, cols_v]], axis=0),
                    bias,
                )
            )
    for (rows, cols), out in zip(places, attention(calls)[0]):
        att[rows, cols] = out
    to_wire = one_hot(window_of_wire(iota((HALF, 1), 0), lat_odd), iota((HALF, SIDE), 1))
    first = (x[...].astype(jnp.float32) + dot(att[...], w_out[...])).astype(jnp.bfloat16)
    first_out[...] = first
    scratch[...] = layer_normed(first.astype(jnp.float32))
    wire = dot(to_wire, scratch[...]).astype(jnp.bfloat16)
    wire_out[...] = wire
    for i in range(2):
        kv_out[:, i * HD : (i + 1) * HD] = dot(wire, w_kv[i]).astype(jnp.bfloat16)


def right_kernel(
    where, x_hbm, w_qkv_hbm, w_out_hbm,
    kv_out, wire_out, first_out, x_left, normed_left, kv0, w_q, w_out, w_kv, w_q1, w_out1,
    x_in, x, x_right, normed, att, scratch, w_kv0, sems,
):
    def part(block, i):
        return w_qkv_hbm.at[block, :, pl.ds(i * HD, HD)]

    pairs = [
        (x_hbm, x_in), (part(0, 1), w_kv0.at[0]), (part(0, 2), w_kv0.at[1]), (part(0, 0), w_q),
        (w_out_hbm.at[0], w_out), (part(1, 1), w_kv.at[0]), (part(1, 2), w_kv.at[1]), (part(1, 0), w_q1),
        (w_out_hbm.at[1], w_out1),
    ]
    copies = [pltpu.make_async_copy(src, dst, sems.at[i]) for i, (src, dst) in enumerate(pairs)]
    for copy in copies:
        copy.start()
    lat_odd = where[0] & 1
    rows = 2 * SIDE
    to_window = one_hot(cell_of_window(iota((rows, 1), 0)), iota((rows, OWN), 1))
    copies[0].wait()
    for i in range(CELLS):
        x[i * LEVELS : (i + 1) * LEVELS, :] = x_in[i].astype(jnp.float32)
    cells = x[...].astype(jnp.bfloat16)
    ordered = dot(to_window, cells)
    x_right[...] = ordered[:SIDE].astype(jnp.bfloat16)
    x_left[...] = ordered[SIDE:].astype(jnp.bfloat16)
    for i in range(4):
        span = slice(i * WIN, (i + 1) * WIN)
        normed[span, :] = layer_normed(ordered[span])
    normed_left[...] = normed[SIDE:, :]
    copies[1].wait()
    copies[2].wait()
    for i in range(2):
        kv0[:, i * HD : (i + 1) * HD] = dot(normed[...], w_kv0[i]).astype(jnp.bfloat16)
    side_block(
        lat_odd, x_right, normed[:SIDE, :], kv0, w_q, w_out, w_kv, first_out, wire_out, kv_out, att, scratch,
        lambda i: copies[3 + i].wait(),
    )
    copies[7].wait()
    copies[8].wait()


def left_kernel(
    where, wire_right, x, normed, kv0, w_q, w_out, w_kv, w_q1,
    kv_out, wire_out, first_out, q_far, att, scratch,
):
    side_block(
        where[0] & 1, x, normed[...], kv0, w_q, w_out, w_kv, first_out, wire_out, kv_out, att, scratch,
        lambda i: None,
    )
    q_far[...] = jnp.zeros_like(q_far)

    @pl.when(where[0] >= 4)
    def _():
        far_queries(wire_right, wire_out, w_q1, q_far)


def far_queries(wire_right, wire_left, w_q1, q_far):
    for side, wire in enumerate((wire_right, wire_left)):
        q_far[side] = dot(wire[:QUART, :], w_q1[...]).astype(jnp.bfloat16)


def late_kernel(where, q_first, wire_right, wire_left, w_q1, q_far):
    @pl.when(where[0] >= 4)
    def _():
        q_far[...] = q_first[...]

    @pl.when(where[0] < 4)
    def _():
        far_queries(wire_right, wire_left, w_q1, q_far)


def residual_kernel(where, first_right, first_left, wire_right, wire_left, w_q1, first_out, q_near, lanes_out):
    log_row = iota((2 * LOGS, HD), 0)
    part = log_row & (LOGS - 1)
    same_head = (part < 24) & ((part & 7) == iota((2 * LOGS, HD), 1) // HEAD)
    lanes_out[...] = jnp.where(same_head, jnp.where(log_row < LOGS, 1.0, -1.0), 0.0).astype(jnp.bfloat16)
    for side, wire in enumerate((wire_right, wire_left)):
        q_near[side] = dot(wire[...], w_q1[...])[QUART:].astype(jnp.bfloat16)
    to_cell = one_hot(iota((OWN, 2 * SIDE), 0), cell_of_window(iota((1, 2 * SIDE), 1)))
    first = jnp.concatenate([first_right[...], first_left[...]], axis=0)
    first_out[...] = dot(to_cell, first).astype(jnp.bfloat16)


def lat_side_calls(q, side_sources):
    calls, places = [], []
    for n in range(4):
        group = n & 1
        sources = side_sources[n >> 1]
        lanes = KWIN * len(sources)
        row = iota((QWIN, lanes), 0)
        lane = iota((QWIN, lanes), 1)
        firsts = [first + UNIT * group for _, first in sources]
        starts = [key_start(f, s.shape[0]) for f, (s, _) in zip(firsts, sources)]
        late = row >= 4 * n + UNIT // 2
        valid = jnp.zeros((QWIN, lanes), jnp.bool_)
        for i in range(len(sources)):
            at = lane - (i * KWIN + firsts[i] - starts[i])
            inside = (at >= 0) & (at < UNIT)
            if group == 1:
                inside = inside & ((at >= UNIT // 2) == late)
            valid = valid | inside
        bias = jnp.where(valid, 0.0, NEG).astype(jnp.float32)
        bias = jnp.concatenate([bias] * 4, axis=0)
        start = query_start(n)
        for half in range(2):

            def window(base):
                lanes = slice(base + half * 256, base + half * 256 + 256)
                parts = [s[f : f + KWIN, lanes] for (s, _), f in zip(sources, starts)]
                return jnp.concatenate(parts, axis=0)

            cols = slice(half * 256, half * 256 + 256)
            places.append((slice(n * QWIN, (n + 1) * QWIN), cols))
            calls.append((spread_heads(q[start : start + QWIN, cols]), window(0), window(HD), bias))
    return calls, places


def pass_kernel(where, q, out):
    out[...] = q[...]


def partial_rows(q, kv_right, kv_left, from_right, from_left, out, att):
    calls, places = lat_side_calls(q, [[(kv_right, 0), (from_right, 0)], [(kv_left, 0), (from_left, 0)]])
    outs, sums = attention(calls, with_logs=True)
    head = iota((1, LOGS), 1) & 7
    for n in range(4):
        column = jnp.zeros((QWIN, LOGS), jnp.float32)
        for half in range(2):
            rows, cols = places[2 * n + half]
            att[rows, cols] = outs[2 * n + half]
            for h in range(4):
                part = sums[2 * n + half][h * QWIN : (h + 1) * QWIN]
                column = jnp.where(head == 4 * half + h, part, column)
        high = column.astype(jnp.bfloat16).astype(jnp.float32)
        rest = column - high
        middle = rest.astype(jnp.bfloat16).astype(jnp.float32)
        third = iota((1, LOGS), 1) >> 3
        parts = jnp.where(third == 0, high, jnp.where(third == 1, middle, rest - middle))
        att[rows, HD:] = parts.astype(jnp.bfloat16)
    to_cell = cells_from_queries()
    out[...] = dot(to_cell, att[...]).astype(jnp.bfloat16)


def own_kernel(where, *refs):
    partial_rows(*refs)


def foreign_kernel(where, q_first, q_other, *refs):
    partial_rows(jnp.where(where[0] >= 4, q_first[...], q_other[...]), *refs)


def near_kernel(where, q, kv_right, kv_left, from_right, from_left, lat, first, w_out, out, att, done):
    own = ((kv_right, from_right), (kv_left, from_left))
    sources = [
        [(own[s][0], QUART), (own[s][1], QUART), (lat, QUART * s), (lat, HALF + QUART * s)] for s in range(2)
    ]
    calls, places = lat_side_calls(q, sources)
    for (rows, cols), result in zip(places, attention(calls)[0]):
        att[rows, cols] = result
    placed = dot(cells_from_queries(), att[...]).astype(jnp.bfloat16)
    rows = pl.ds(pl.multiple_of(HALF * (1 - (where[0] & 1)), 16), HALF)
    done[...] = first[rows, :].astype(jnp.float32) + dot(placed, w_out[...])
    for i in range(CELLS // 2):
        out[i] = done[i * LEVELS : (i + 1) * LEVELS, :].astype(jnp.bfloat16)


def merge_kernel(where, mine, theirs, to_lanes, first, w_out, near, out, done, staged, sems):
    position = where[0] & 3
    far = position & 1
    copy = pltpu.make_async_copy(
        near, out.at[pl.ds((1 - far) * (CELLS // 2), CELLS // 2)], sems.at[0]
    )
    copy.start()
    gap = dot(jnp.concatenate([mine[:, HD:], theirs[:, HD:]], axis=1), to_lanes[...])
    alone = (position == 0) | (position == 3)
    gate = jnp.where(alone, 0.0, 1.0 / (1.0 + jnp.exp(gap)))
    own = mine[:, :HD].astype(jnp.float32)
    att = (own + (theirs[:, :HD].astype(jnp.float32) - own) * gate).astype(jnp.bfloat16)
    rows = pl.ds(pl.multiple_of(HALF * far, 16), HALF)
    done[...] = first[rows, :].astype(jnp.float32) + dot(att, w_out[...])
    for i in range(CELLS // 2):
        staged[i] = done[i * LEVELS : (i + 1) * LEVELS, :].astype(jnp.bfloat16)
    far_copy = pltpu.make_async_copy(
        staged, out.at[pl.ds(far * (CELLS // 2), CELLS // 2)], sems.at[1]
    )
    far_copy.start()
    copy.wait()
    far_copy.wait()


def shape(*dims):
    return jax.ShapeDtypeStruct(dims, jnp.bfloat16)


def vmem(*dims):
    return pltpu.VMEM(dims, jnp.bfloat16)


def in_hbm(array):
    return pltpu.with_memory_space_constraint(array, pltpu.HBM)


ANY = pl.BlockSpec(memory_space=pl.ANY)
WHOLE = pl.BlockSpec(memory_space=pltpu.VMEM)
SCALARS = pl.BlockSpec(memory_space=pltpu.SMEM)


def call(kernel, ins, outs, scratch, flops, name, out_spec=WHOLE, limit=40):
    return pl.pallas_call(
        kernel,
        out_shape=outs,
        in_specs=[SCALARS, *ins],
        out_specs=jax.tree.map(lambda _: out_spec, outs),
        scratch_shapes=scratch,
        compiler_params=pltpu.CompilerParams(vmem_limit_bytes=limit * 1024 * 1024),
        cost_estimate=pl.CostEstimate(flops=flops, bytes_accessed=4_000_000, transcendentals=0),
        name=name,
    )


def right_side(where, cells, w_qkv, w_out):
    return call(
        right_kernel,
        [ANY] * 3,
        (
            shape(HALF, D), shape(HALF, D), shape(SIDE, D), shape(SIDE, D), shape(SIDE, D),
            shape(2 * SIDE, D), shape(D, HD), shape(HD, D), shape(2, D, HD), shape(D, HD), shape(HD, D),
        ),
        [
            vmem(CELLS, LEVELS, D), pltpu.VMEM((OWN, D), jnp.float32), vmem(SIDE, D), vmem(2 * SIDE, D),
            vmem(SIDE, HD), vmem(SIDE, D), vmem(2, D, HD), pltpu.SemaphoreType.DMA((9,)),
        ],
        2_000_000_000,
        "right_side",
    )(where, in_hbm(cells), in_hbm(w_qkv), in_hbm(w_out))


def left_side(*args):
    return call(
        left_kernel,
        [WHOLE] * 8,
        (shape(HALF, D), shape(HALF, D), shape(SIDE, D), shape(2, QUART, HD)),
        [vmem(SIDE, HD), vmem(SIDE, D)],
        2_000_000_000,
        "left_side",
    )(*args)


def late_queries(*args):
    return call(late_kernel, [WHOLE] * 4, shape(2, QUART, HD), [], 200_000_000, "late_queries")(*args)


def residual(*args):
    outs = (shape(OWN, D), shape(2, QUART, HD), shape(2 * LOGS, HD))
    return call(residual_kernel, [WHOLE] * 5, outs, [], 1_000_000_000, "residual")(*args)


def passed(*args):
    return call(pass_kernel, [WHOLE], shape(HALF, HD), [], 2_500_000_000, "passed")(*args)


def partial(name, kernel, *args):
    return call(
        kernel,
        [WHOLE] * (len(args) - 1),
        shape(HALF, HD + LOGS),
        [vmem(4 * QWIN, HD + LOGS)],
        1_000_000_000,
        name,
    )(*args)


DONE = pltpu.VMEM((HALF, D), jnp.float32)


def near_rows(*args):
    return call(
        near_kernel,
        [WHOLE] * 8,
        shape(CELLS // 2, LEVELS, D),
        [vmem(4 * QWIN, HD), DONE],
        2_000_000_000,
        "near_rows",
    )(*args)


def merge(*args):
    return call(
        merge_kernel,
        [WHOLE] * 6,
        shape(CELLS, LEVELS, D),
        [DONE, vmem(CELLS // 2, LEVELS, D), pltpu.SemaphoreType.DMA((2,))],
        2_000_000_000,
        "merge",
        out_spec=ANY,
    )(*args)


def per_device(tokens, w_qkv, w_out):
    lons, lats = lax.axis_size("lon"), lax.axis_size("lat")
    starts_run = (lax.axis_index("lon") % RUN == 0).astype(jnp.int32)
    where = (lax.axis_index("lat").astype(jnp.int32) + 4 * starts_run)[None]
    cells = tokens.transpose(1, 2, 0, 3).reshape(CELLS, LEVELS, D)

    kv_right, wire_right, first_right, *rest = right_side(where, cells, w_qkv, w_out)
    from_left = lax.ppermute(kv_right, "lon", [(i, (i + 1) % lons) for i in range(lons)])
    *rest, w_out1 = rest
    kv_left, wire_left, first_left, q_first = left_side(where, wire_right, *rest)
    w_q1 = rest[-1]
    partner = [i + 1 if i % 2 else i - 1 for i in range(lats)]
    partner[0], partner[-1] = 0, lats - 1
    first_pairs, other_pairs = [], []
    for i in range(lons):
        for j in range(lats):
            one, other = (first_pairs, other_pairs) if i % RUN == 0 else (other_pairs, first_pairs)
            one.append((i * lats + j, i * lats + partner[j]))
            other.append((i * lats + j, i * lats + j))
    foreign_first = lax.ppermute(q_first, ("lon", "lat"), first_pairs).reshape(HALF, HD)
    from_right = lax.ppermute(kv_left, "lon", [(i, (i - 1) % lons) for i in range(lons)])
    q_far = late_queries(where, q_first, wire_right, wire_left, w_q1).reshape(HALF, HD)
    foreign = lax.ppermute(q_far, ("lon", "lat"), other_pairs)

    foreign_first, from_left = lax.optimization_barrier((foreign_first, from_left))
    q_first = passed(where, foreign_first)
    received = (first_left, q_first, from_left, from_right, foreign)
    first_left, q_first, from_left, from_right, foreign = lax.optimization_barrier(received)

    keys = [kv_right, kv_left, from_right, from_left]
    far_pairs = [pair for i in range(1, lats - 1, 2) for pair in ((i, i + 1), (i + 1, i))]
    theirs = partial("foreign_rows", foreign_kernel, where, q_first, foreign, *keys)
    theirs = lax.ppermute(theirs, "lat", far_pairs)
    to_near = jnp.concatenate([p[QUART:] for p in keys], axis=0)
    from_near = lax.ppermute(to_near, "lat", [(i, i ^ 1) for i in range(lats)])
    mine = partial("own_rows", own_kernel, where, q_far, *keys)
    first, q_near, to_lanes = residual(where, first_right, first_left, wire_right, wire_left, w_q1)
    near = near_rows(where, q_near.reshape(HALF, HD), *keys, from_near, first, w_out1)
    out = merge(where, mine, theirs, to_lanes, first, w_out1, near)
    return out.reshape(ROWS, COLS, LEVELS, D).transpose(2, 0, 1, 3)


def solution(mesh):
    return jax.shard_map(
        per_device,
        mesh=mesh,
        in_specs=(P(None, "lat", "lon", None), P(), P()),
        out_specs=P(None, "lat", "lon", None),
        check_vma=False,
    )
```

```python
import jax
import jax.numpy as jnp
from jax import lax
from jax.experimental import pallas as pl
from jax.experimental.pallas import tpu as pltpu
from jax.sharding import PartitionSpec as P

LEVELS, ROWS, COLS, D = 4, 6, 12, 1024
HD, HEAD = 512, 64
CELLS = ROWS * COLS
OWN = LEVELS * CELLS
HALF = OWN // 2
QUART = HALF // 2
UNIT = 36
WIN = 80
SIDE = 2 * WIN
QWIN = 48
KWIN = 64
NEG = -1e30
LOGS = 128
RUN = 8


def at_least(index, *bounds):
    return sum(jnp.where(index >= bound, 1, 0) for bound in bounds)


def cell_of_window(index):
    side = at_least(index, SIDE)
    index = index - SIDE * side
    pair = at_least(index, WIN)
    index = index - WIN * pair
    valid = index < 2 * UNIT
    level = at_least(index, UNIT)
    index = index - UNIT * level
    row = at_least(index, *range(6, UNIT, 6))
    cell = (row * COLS + 6 * (1 - side) + index - 6 * row) * LEVELS + 2 * pair + level
    return jnp.where(valid, cell, -1)


def split_unit(index, group):
    lev = at_least(index, UNIT // 2)
    index = index - UNIT // 2 * lev
    row = at_least(index, 6, 12)
    return jnp.where(group == 0, 1 + lev, 3 - 3 * lev), row, index - 6 * row


def window_of_wire(index, lat_odd):
    k = at_least(index, UNIT, 2 * UNIT, 3 * UNIT)
    level, row, col = split_unit(index - UNIT * k, k & 1)
    row = row + 3 * ((k >> 1) ^ lat_odd)
    return WIN * (level >> 1) + UNIT * (level & 1) + 6 * row + col


def cell_of_unit(n, index):
    level, row, col = split_unit(index, n & 1)
    return (row * COLS + 6 * (1 - (n >> 1)) + col) * LEVELS + level


def query_start(k):
    return k * UNIT // 16 * 16


def key_start(first, size):
    return min(first // 16 * 16, size - KWIN)


def iota(shape, axis):
    return lax.broadcasted_iota(jnp.int32, shape, axis)


def one_hot(rows, lanes):
    return jnp.where(rows == lanes, 1.0, 0.0).astype(jnp.bfloat16)


def layer_normed(values):
    centre = values - jnp.mean(values, axis=-1, keepdims=True)
    spread = jnp.mean(centre * centre, axis=-1, keepdims=True)
    return (centre * lax.rsqrt(spread + 1e-05)).astype(jnp.bfloat16)


def dot(a, b):
    return jnp.dot(a, b, preferred_element_type=jnp.float32)


def cells_from_queries():
    index = iota((1, 4 * QWIN), 1)
    n = at_least(index, QWIN, 2 * QWIN, 3 * QWIN)
    index = index - (QWIN + 4) * n
    cell = jnp.where((index >= 0) & (index < UNIT), cell_of_unit(n, index), -1)
    return one_hot(iota((HALF, 4 * QWIN), 0), cell)


def spread_heads(queries):
    head_of = iota((1, 4 * HEAD), 1) // HEAD
    queries = queries * jnp.bfloat16(0.125)
    return jnp.concatenate(
        [jnp.where(head_of == h, queries, jnp.bfloat16(0)) for h in range(4)], axis=0
    )


def attention(calls, with_logs=False):
    head_of = iota((1, 4 * HEAD), 1) // HEAD
    scores = []
    for queries, keys, _, bias in calls:
        product = lax.dot_general(
            queries, keys, (((1,), (1,)), ((), ())), preferred_element_type=jnp.float32
        )
        scores.append(product + bias)
    highest = [jnp.max(s, axis=-1, keepdims=True) for s in scores]
    raised = [jnp.exp(s - h) for s, h in zip(scores, highest)]
    mixed = [dot(r.astype(jnp.bfloat16), call[2]) for r, call in zip(raised, calls)]
    outs, logs = [], []
    for r, m, high in zip(raised, mixed, highest):
        total = jnp.sum(r, axis=-1, keepdims=True)
        m = m * (1.0 / total)
        rows = m.shape[0] // 4
        out = m[:rows]
        for h in range(1, 4):
            out = jnp.where(head_of == h, m[h * rows : (h + 1) * rows], out)
        outs.append(out.astype(jnp.bfloat16))
        logs.append(high + jnp.log(total) if with_logs else None)
    return outs, logs


def side_block(lat_odd, x, normed, kv, w_q, w_out, w_kv, first_out, wire_out, kv_out, att, scratch, ready):
    for i in range(4):
        ready(i)
    queries = dot(normed, w_q[...]).astype(jnp.bfloat16)
    bias = jnp.where(iota((1, 2 * WIN), 1) % WIN < 2 * UNIT, 0.0, NEG).astype(jnp.float32)
    calls, places = [], []
    for pair in range(2):
        rows = slice(pair * WIN, (pair + 1) * WIN)
        far = slice(SIDE + pair * WIN, SIDE + (pair + 1) * WIN)
        for half in range(2):
            cols = slice(half * 256, half * 256 + 256)
            cols_v = slice(HD + half * 256, HD + half * 256 + 256)
            places.append((rows, cols))
            calls.append(
                (
                    spread_heads(queries[rows, cols]),
                    jnp.concatenate([kv[rows, cols], kv[far, cols]], axis=0),
                    jnp.concatenate([kv[rows, cols_v], kv[far, cols_v]], axis=0),
                    bias,
                )
            )
    for (rows, cols), out in zip(places, attention(calls)[0]):
        att[rows, cols] = out
    to_wire = one_hot(window_of_wire(iota((HALF, 1), 0), lat_odd), iota((HALF, SIDE), 1))
    first = (x[...].astype(jnp.float32) + dot(att[...], w_out[...])).astype(jnp.bfloat16)
    first_out[...] = first
    scratch[...] = layer_normed(first.astype(jnp.float32))
    wire = dot(to_wire, scratch[...]).astype(jnp.bfloat16)
    wire_out[...] = wire
    for i in range(2):
        kv_out[:, i * HD : (i + 1) * HD] = dot(wire, w_kv[i]).astype(jnp.bfloat16)


def right_kernel(
    where, x_hbm, w_qkv_hbm, w_out_hbm,
    kv_out, wire_out, first_out, x_left, normed, kv0, w_q, w_out, w_kv, w_q1, w_out1,
    x_in, x, x_right, att, scratch, w_kv0, sems,
):
    def part(block, i):
        return w_qkv_hbm.at[block, :, pl.ds(i * HD, HD)]

    pairs = [
        (x_hbm, x_in), (part(0, 1), w_kv0.at[0]), (part(0, 2), w_kv0.at[1]), (part(0, 0), w_q),
        (w_out_hbm.at[0], w_out), (part(1, 1), w_kv.at[0]), (part(1, 2), w_kv.at[1]), (part(1, 0), w_q1),
        (w_out_hbm.at[1], w_out1),
    ]
    copies = [pltpu.make_async_copy(src, dst, sems.at[i]) for i, (src, dst) in enumerate(pairs)]
    for copy in copies:
        copy.start()
    lat_odd = where[0] & 1
    rows = 2 * SIDE
    to_window = one_hot(cell_of_window(iota((rows, 1), 0)), iota((rows, OWN), 1))
    copies[0].wait()
    for i in range(CELLS):
        x[i * LEVELS : (i + 1) * LEVELS, :] = x_in[i].astype(jnp.float32)
    cells = x[...].astype(jnp.bfloat16)
    ordered = dot(to_window, cells)
    x_right[...] = ordered[:SIDE].astype(jnp.bfloat16)
    x_left[...] = ordered[SIDE:].astype(jnp.bfloat16)
    for i in range(4):
        span = slice(i * WIN, (i + 1) * WIN)
        normed[span, :] = layer_normed(ordered[span])
    copies[1].wait()
    copies[2].wait()
    for i in range(2):
        kv0[:, i * HD : (i + 1) * HD] = dot(normed[...], w_kv0[i]).astype(jnp.bfloat16)
    side_block(
        lat_odd, x_right, normed[:SIDE, :], kv0, w_q, w_out, w_kv, first_out, wire_out, kv_out, att, scratch,
        lambda i: copies[3 + i].wait(),
    )
    copies[7].wait()
    copies[8].wait()


def left_kernel(
    where, wire_right, x, normed, kv0, w_q, w_out, w_kv, w_q1,
    kv_out, wire_out, first_out, q_far, att, scratch,
):
    side_block(
        where[0] & 1, x, normed[SIDE:, :], kv0, w_q, w_out, w_kv, first_out, wire_out, kv_out, att, scratch,
        lambda i: None,
    )
    q_far[...] = jnp.zeros_like(q_far)

    @pl.when(where[0] >= 4)
    def _():
        far_queries(wire_right, wire_out, w_q1, q_far)


def far_queries(wire_right, wire_left, w_q1, q_far):
    for side, wire in enumerate((wire_right, wire_left)):
        q_far[side] = dot(wire[:QUART, :], w_q1[...]).astype(jnp.bfloat16)


def late_kernel(where, q_first, wire_right, wire_left, w_q1, q_far):
    @pl.when(where[0] >= 4)
    def _():
        q_far[...] = q_first[...]

    @pl.when(where[0] < 4)
    def _():
        far_queries(wire_right, wire_left, w_q1, q_far)


def residual_kernel(where, first_right, first_left, wire_right, wire_left, w_q1, first_out, q_near):
    for side, wire in enumerate((wire_right, wire_left)):
        q_near[side] = dot(wire[...], w_q1[...])[QUART:].astype(jnp.bfloat16)
    to_cell = one_hot(iota((OWN, 2 * SIDE), 0), cell_of_window(iota((1, 2 * SIDE), 1)))
    first = jnp.concatenate([first_right[...], first_left[...]], axis=0)
    first_out[...] = dot(to_cell, first).astype(jnp.bfloat16)


def lat_side_calls(q, side_sources):
    calls, places = [], []
    for n in range(4):
        group = n & 1
        sources = side_sources[n >> 1]
        lanes = KWIN * len(sources)
        row = iota((QWIN, lanes), 0)
        lane = iota((QWIN, lanes), 1)
        firsts = [first + UNIT * group for _, first in sources]
        starts = [key_start(f, s.shape[0]) for f, (s, _) in zip(firsts, sources)]
        late = row >= 4 * n + UNIT // 2
        valid = jnp.zeros((QWIN, lanes), jnp.bool_)
        for i in range(len(sources)):
            at = lane - (i * KWIN + firsts[i] - starts[i])
            inside = (at >= 0) & (at < UNIT)
            if group == 1:
                inside = inside & ((at >= UNIT // 2) == late)
            valid = valid | inside
        bias = jnp.where(valid, 0.0, NEG).astype(jnp.float32)
        bias = jnp.concatenate([bias] * 4, axis=0)
        start = query_start(n)
        for half in range(2):

            def window(base):
                lanes = slice(base + half * 256, base + half * 256 + 256)
                parts = [s[f : f + KWIN, lanes] for (s, _), f in zip(sources, starts)]
                return jnp.concatenate(parts, axis=0)

            cols = slice(half * 256, half * 256 + 256)
            places.append((slice(n * QWIN, (n + 1) * QWIN), cols))
            calls.append((spread_heads(q[start : start + QWIN, cols]), window(0), window(HD), bias))
    return calls, places


def pass_kernel(where, q, out):
    out[...] = q[...]


def partial_rows(q, kv_right, kv_left, from_right, from_left, out, att):
    calls, places = lat_side_calls(q, [[(kv_right, 0), (from_right, 0)], [(kv_left, 0), (from_left, 0)]])
    outs, sums = attention(calls, with_logs=True)
    head = iota((1, LOGS), 1) & 7
    for n in range(4):
        column = jnp.zeros((QWIN, LOGS), jnp.float32)
        for half in range(2):
            rows, cols = places[2 * n + half]
            att[rows, cols] = outs[2 * n + half]
            for h in range(4):
                part = sums[2 * n + half][h * QWIN : (h + 1) * QWIN]
                column = jnp.where(head == 4 * half + h, part, column)
        high = column.astype(jnp.bfloat16).astype(jnp.float32)
        rest = column - high
        middle = rest.astype(jnp.bfloat16).astype(jnp.float32)
        third = iota((1, LOGS), 1) >> 3
        parts = jnp.where(third == 0, high, jnp.where(third == 1, middle, rest - middle))
        att[rows, HD:] = parts.astype(jnp.bfloat16)
    to_cell = cells_from_queries()
    out[...] = dot(to_cell, att[...]).astype(jnp.bfloat16)


def own_kernel(where, *refs):
    partial_rows(*refs)


def foreign_kernel(where, q_first, q_other, *refs):
    partial_rows(jnp.where(where[0] >= 4, q_first[...], q_other[...]), *refs)


def near_kernel(where, q, kv_right, kv_left, from_right, from_left, lat, first, w_out, out, att, done):
    own = ((kv_right, from_right), (kv_left, from_left))
    sources = [
        [(own[s][0], QUART), (own[s][1], QUART), (lat, QUART * s), (lat, HALF + QUART * s)] for s in range(2)
    ]
    calls, places = lat_side_calls(q, sources)
    for (rows, cols), result in zip(places, attention(calls)[0]):
        att[rows, cols] = result
    placed = dot(cells_from_queries(), att[...]).astype(jnp.bfloat16)
    rows = pl.ds(pl.multiple_of(HALF * (1 - (where[0] & 1)), 16), HALF)
    done[...] = first[rows, :].astype(jnp.float32) + dot(placed, w_out[...])
    for i in range(CELLS // 2):
        out[i] = done[i * LEVELS : (i + 1) * LEVELS, :].astype(jnp.bfloat16)


def merge_kernel(where, mine, theirs, first, w_out, near, out, done, staged, sems):
    position = where[0] & 3
    far = position & 1
    copy = pltpu.make_async_copy(
        near, out.at[pl.ds((1 - far) * (CELLS // 2), CELLS // 2)], sems.at[0]
    )
    copy.start()
    log_row = iota((2 * LOGS, HD), 0)
    part = log_row & (LOGS - 1)
    same_head = (part < 24) & ((part & 7) == iota((2 * LOGS, HD), 1) // HEAD)
    to_lanes = jnp.where(same_head, jnp.where(log_row < LOGS, 1.0, -1.0), 0.0).astype(jnp.bfloat16)
    gap = dot(jnp.concatenate([mine[:, HD:], theirs[:, HD:]], axis=1), to_lanes)
    alone = (position == 0) | (position == 3)
    gate = jnp.where(alone, 0.0, 1.0 / (1.0 + jnp.exp(gap)))
    own = mine[:, :HD].astype(jnp.float32)
    att = (own + (theirs[:, :HD].astype(jnp.float32) - own) * gate).astype(jnp.bfloat16)
    rows = pl.ds(pl.multiple_of(HALF * far, 16), HALF)
    done[...] = first[rows, :].astype(jnp.float32) + dot(att, w_out[...])
    for i in range(CELLS // 2):
        staged[i] = done[i * LEVELS : (i + 1) * LEVELS, :].astype(jnp.bfloat16)
    far_copy = pltpu.make_async_copy(
        staged, out.at[pl.ds(far * (CELLS // 2), CELLS // 2)], sems.at[1]
    )
    far_copy.start()
    copy.wait()
    far_copy.wait()


def shape(*dims):
    return jax.ShapeDtypeStruct(dims, jnp.bfloat16)


def vmem(*dims):
    return pltpu.VMEM(dims, jnp.bfloat16)


def in_hbm(array):
    return pltpu.with_memory_space_constraint(array, pltpu.HBM)


ANY = pl.BlockSpec(memory_space=pl.ANY)
WHOLE = pl.BlockSpec(memory_space=pltpu.VMEM)
SCALARS = pl.BlockSpec(memory_space=pltpu.SMEM)


def call(kernel, ins, outs, scratch, flops, name, out_spec=WHOLE, limit=40):
    return pl.pallas_call(
        kernel,
        out_shape=outs,
        in_specs=[SCALARS, *ins],
        out_specs=jax.tree.map(lambda _: out_spec, outs),
        scratch_shapes=scratch,
        compiler_params=pltpu.CompilerParams(vmem_limit_bytes=limit * 1024 * 1024),
        cost_estimate=pl.CostEstimate(flops=flops, bytes_accessed=4_000_000, transcendentals=0),
        name=name,
    )


def right_side(where, cells, w_qkv, w_out):
    return call(
        right_kernel,
        [ANY] * 3,
        (
            shape(HALF, D), shape(HALF, D), shape(SIDE, D), shape(SIDE, D), shape(2 * SIDE, D),
            shape(2 * SIDE, D), shape(D, HD), shape(HD, D), shape(2, D, HD), shape(D, HD), shape(HD, D),
        ),
        [
            vmem(CELLS, LEVELS, D), pltpu.VMEM((OWN, D), jnp.float32), vmem(SIDE, D),
            vmem(SIDE, HD), vmem(SIDE, D), vmem(2, D, HD), pltpu.SemaphoreType.DMA((9,)),
        ],
        2_000_000_000,
        "right_side",
    )(where, in_hbm(cells), in_hbm(w_qkv), in_hbm(w_out))


def left_side(*args):
    return call(
        left_kernel,
        [WHOLE] * 8,
        (shape(HALF, D), shape(HALF, D), shape(SIDE, D), shape(2, QUART, HD)),
        [vmem(SIDE, HD), vmem(SIDE, D)],
        2_000_000_000,
        "left_side",
    )(*args)


def late_queries(*args):
    return call(late_kernel, [WHOLE] * 4, shape(2, QUART, HD), [], 200_000_000, "late_queries")(*args)


def residual(*args):
    outs = (shape(OWN, D), shape(2, QUART, HD))
    return call(residual_kernel, [WHOLE] * 5, outs, [], 1_000_000_000, "residual")(*args)


def passed(*args):
    return call(pass_kernel, [WHOLE], shape(HALF, HD), [], 2_500_000_000, "passed")(*args)


def partial(name, kernel, *args):
    return call(
        kernel,
        [WHOLE] * (len(args) - 1),
        shape(HALF, HD + LOGS),
        [vmem(4 * QWIN, HD + LOGS)],
        1_000_000_000,
        name,
    )(*args)


DONE = pltpu.VMEM((HALF, D), jnp.float32)


def near_rows(*args):
    return call(
        near_kernel,
        [WHOLE] * 8,
        shape(CELLS // 2, LEVELS, D),
        [vmem(4 * QWIN, HD), DONE],
        2_000_000_000,
        "near_rows",
    )(*args)


def merge(*args):
    return call(
        merge_kernel,
        [WHOLE] * 5,
        shape(CELLS, LEVELS, D),
        [DONE, vmem(CELLS // 2, LEVELS, D), pltpu.SemaphoreType.DMA((2,))],
        2_000_000_000,
        "merge",
        out_spec=ANY,
    )(*args)


def per_device(tokens, w_qkv, w_out):
    lons, lats = lax.axis_size("lon"), lax.axis_size("lat")
    starts_run = (lax.axis_index("lon") % RUN == 0).astype(jnp.int32)
    where = (lax.axis_index("lat").astype(jnp.int32) + 4 * starts_run)[None]
    cells = tokens.transpose(1, 2, 0, 3).reshape(CELLS, LEVELS, D)

    kv_right, wire_right, first_right, *rest = right_side(where, cells, w_qkv, w_out)
    from_left = lax.ppermute(kv_right, "lon", [(i, (i + 1) % lons) for i in range(lons)])
    *rest, w_out1 = rest
    kv_left, wire_left, first_left, q_first = left_side(where, wire_right, *rest)
    w_q1 = rest[-1]
    partner = [i + 1 if i % 2 else i - 1 for i in range(lats)]
    partner[0], partner[-1] = 0, lats - 1
    first_pairs, other_pairs = [], []
    for i in range(lons):
        for j in range(lats):
            one, other = (first_pairs, other_pairs) if i % RUN == 0 else (other_pairs, first_pairs)
            one.append((i * lats + j, i * lats + partner[j]))
            other.append((i * lats + j, i * lats + j))
    foreign_first = lax.ppermute(q_first, ("lon", "lat"), first_pairs).reshape(HALF, HD)
    from_right = lax.ppermute(kv_left, "lon", [(i, (i - 1) % lons) for i in range(lons)])
    q_far = late_queries(where, q_first, wire_right, wire_left, w_q1).reshape(HALF, HD)
    foreign = lax.ppermute(q_far, ("lon", "lat"), other_pairs)

    foreign_first, from_left = lax.optimization_barrier((foreign_first, from_left))
    q_first = passed(where, foreign_first)
    received = (first_left, q_first, from_left, from_right, foreign)
    first_left, q_first, from_left, from_right, foreign = lax.optimization_barrier(received)

    keys = [kv_right, kv_left, from_right, from_left]
    far_pairs = [pair for i in range(1, lats - 1, 2) for pair in ((i, i + 1), (i + 1, i))]
    theirs = partial("foreign_rows", foreign_kernel, where, q_first, foreign, *keys)
    theirs = lax.ppermute(theirs, "lat", far_pairs)
    to_near = jnp.concatenate([p[QUART:] for p in keys], axis=0)
    from_near = lax.ppermute(to_near, "lat", [(i, i ^ 1) for i in range(lats)])
    mine = partial("own_rows", own_kernel, where, q_far, *keys)
    first, q_near = residual(where, first_right, first_left, wire_right, wire_left, w_q1)
    near = near_rows(where, q_near.reshape(HALF, HD), *keys, from_near, first, w_out1)
    out = merge(where, mine, theirs, first, w_out1, near)
    return out.reshape(ROWS, COLS, LEVELS, D).transpose(2, 0, 1, 3)


def solution(mesh):
    return jax.shard_map(
        per_device,
        mesh=mesh,
        in_specs=(P(None, "lat", "lon", None), P(), P()),
        out_specs=P(None, "lat", "lon", None),
        check_vma=False,
    )
```
